512 devices in a mesh: seq: 32 (over z_lo, y, core), clip: 16 (over z_hi, x).
Axes of the slice: x: 4, y: 4, z: 16 (z_hi: 4, z_lo: 4; z = z_hi * 4 + z_lo), core: 2. Of those that a mesh axis runs over, the one named last changes fastest.
Arguments:
- state: bfloat16 [3072, 4096], P(('clip', 'seq')), parts along dimension 0, may hold values from -5 to 5
- probe: bfloat16 [3072, 4096], P(('clip', 'seq')), parts along dimension 0, may hold values from -4 to 4
- norm_gain: float32 [4096], replicated, may hold values from 0.5 to 1.5
- head_maps: bfloat16 [32, 4096, 384], P('seq'), may hold values from -0.09375 to 0.09375
- query_gain: float32 [32, 128], P('seq'), may hold values from 0.5 to 1.5
- key_gain: float32 [32, 128], P('seq'), may hold values from 0.5 to 4
- out_map: bfloat16 [4096, 4096], P(None, 'seq'), may hold values from -0.09375 to 0.09375
- out_gate: float32 [4096], replicated, may hold values from 2 to 3
Outputs:
- next_state: bfloat16 [3072, 4096], P(('clip', 'seq')), parts along dimension 0
- density_change: float32 [16], P('clip'), parts along dimension 0
The draws below stay inside these ranges and needn't reach their ends.
There are 16 independent parts, one for each index of `clip`. The reference program is written for one: setup_inputs(seed, part) draws one part's arguments, and reference() takes and returns one part's arrays. A program takes and returns all parts, laid end to end along the dimension named above; an argument that names none is the same for every part. Nothing has to cross between parts.
All inputs are finite; a program needn't handle non-finite values.
Results may differ from the reference program's by a relative error of at most 0.035.
Values may be sent and summed in bfloat16 or wider, within the bound.
No kernel may reach another device: no remote copies, remote signals or barrier semaphores. Data moves between devices by JAX's collectives and lax.ppermute only.
A program may use at most 64 MiB of HBM per device.

```python
import math
import jax
import jax.numpy as jnp
from jax import lax

HEADS = 32
HD = 128
D = 4096
TOKENS = 192


def draw_state(key, part):
    key = jax.random.fold_in(key, 11)
    key_base, key_cols, key_rows = jax.random.split(key, 3)
    columns = jnp.exp(jax.random.uniform(key_cols, (D,), jnp.float32, math.log(0.05), math.log(0.5)))
    base = jnp.clip(jax.random.normal(key_base, (TOKENS, D), jnp.float32), -4.0, 4.0)
    scales = jnp.exp(jax.random.uniform(key_rows, (TOKENS, 1), jnp.float32, math.log(0.5), math.log(2.0)))
    return (base * scales * columns[None, :]).astype(jnp.bfloat16)


def steps_of(stream_key, dims, cuts, least, high):
    def one(position, blocks):
        steps = jax.random.uniform(jax.random.fold_in(jax.random.fold_in(stream_key, 6), position), (blocks,), jnp.float32, least / len(cuts), high / len(cuts))
        return jnp.repeat(jnp.exp(steps), dims[position] // blocks).reshape((-1,) + (1,) * (len(dims) - position - 1))

    factor_of = one(*cuts[0])
    for cut in cuts[1:]:
        factor_of = factor_of * one(*cut)
    return factor_of


def gaussian(key, shape, spread, reach, cuts=(), kind=jnp.bfloat16):
    level = steps_of(key, shape, cuts, -0.22, 0.18) if cuts else 1.0
    result = jax.random.normal(key, shape, jnp.float32) * spread * level
    return jnp.minimum(jnp.maximum(result, -reach), reach).astype(kind)


def setup_inputs(seed: int = 0, part: int = 0) -> dict:
    streams_of = jax.random.split(jax.random.key(seed), 9)
    part_keys = jax.random.split(jax.random.fold_in(streams_of[8], part), 9)
    return {
        "state": draw_state(jax.random.fold_in(jax.random.fold_in(streams_of[8], part), 71), part),
        "probe": gaussian(part_keys[1], (TOKENS, D), 1.0, 4.0, ((0, 32),)),
        "norm_gain": jnp.clip(1.0 + 0.1 * jax.random.normal(streams_of[2], (D,), jnp.float32), 0.5, 1.5),
        "head_maps": gaussian(streams_of[3], (HEADS, D, 3 * HD), D ** -0.5, 0.09375, ((0, 32),)),
        "query_gain": jnp.clip(1.0 + 0.1 * jax.random.normal(streams_of[4], (HEADS, HD), jnp.float32), 0.5, 1.5),
        "key_gain": jnp.clip(jnp.exp(math.log(4.0) - 2.0794415 * jax.random.uniform(streams_of[5], (HEADS, HD), jnp.float32) ** steps_of(streams_of[5], (HEADS, HD), ((0, 32),), -0.2, 0.2)), 0.5, 4.0),
        "out_map": gaussian(streams_of[6], (D, D), D ** -0.5, 0.09375, ((1, 32),)),
        "out_gate": jnp.clip(jnp.exp(jax.random.uniform(streams_of[7], (D,), jnp.float32, math.log(2.0), math.log(3.0))), 2.0, 3.0),
    }


EPS = 1e-06
step_length = 0.5

def qk_norm(vals, tang, gain):
    recip = lax.rsqrt(lax.optimization_barrier(jnp.mean(vals * vals, axis=-1, keepdims=True)) + EPS)
    d_recip = -recip ** 3 * lax.optimization_barrier(jnp.mean(vals * tang, axis=-1, keepdims=True))
    return (vals * recip * gain, (tang * recip + vals * d_recip) * gain)

def mix(form, left, right):
    return jnp.einsum(form, left.astype(jnp.float32), right.astype(jnp.float32), precision=lax.Precision.HIGHEST)

def local_heads(proj, d_proj, query_gain, key_gain):
    total = proj.shape[0]
    heads = proj.shape[1]
    width = proj.shape[2] // 3
    query, d_query = qk_norm(proj[..., :width], d_proj[..., :width], query_gain[None])
    keys, d_keys = qk_norm(proj[..., width:2 * width], d_proj[..., width:2 * width], key_gain[None])
    q_b = query.astype(jnp.bfloat16)
    dq_b = d_query.astype(jnp.bfloat16)
    k_b = keys.astype(jnp.bfloat16)
    dk_b = d_keys.astype(jnp.bfloat16)
    v_b = proj[..., 2 * width:].astype(jnp.bfloat16)
    dv_b = d_proj[..., 2 * width:].astype(jnp.bfloat16)
    block = min(512, total)
    count = total // block
    scale = width ** (-0.5)

    def one_block(index):
        rows = index * block
        q_rows = lax.dynamic_slice_in_dim(q_b, rows, block, 0)
        dq_rows = lax.dynamic_slice_in_dim(dq_b, rows, block, 0)
        scores = mix('qhd,khd->hqk', q_rows, k_b) * scale
        expo = jnp.exp(scores)
        probs = expo / lax.optimization_barrier(jnp.sum(expo, axis=-1, keepdims=True))
        d_scores = (mix('qhd,khd->hqk', dq_rows, k_b) + mix('qhd,khd->hqk', q_rows, dk_b)) * scale
        d_probs = probs * (d_scores - lax.optimization_barrier(jnp.sum(probs * d_scores, axis=-1, keepdims=True)))
        probs_b = probs.astype(jnp.bfloat16)
        d_probs_b = d_probs.astype(jnp.bfloat16)
        attended = mix('hqk,khd->qhd', probs_b, v_b)
        d_attended = mix('hqk,khd->qhd', d_probs_b, v_b) + mix('hqk,khd->qhd', probs_b, dv_b)
        return (attended.astype(jnp.bfloat16), d_attended.astype(jnp.bfloat16))
    attended, d_attended = lax.map(one_block, jnp.arange(count))
    return (attended.reshape(total, heads * width), d_attended.reshape(total, heads * width))

def field(state, probe_f, norm_gain, head_maps, query_gain, key_gain, out_map, out_gate):
    xf = state.astype(jnp.float32)
    recip = lax.rsqrt(lax.optimization_barrier(jnp.mean(xf * xf, axis=-1, keepdims=True)) + EPS)
    d_recip = -recip ** 3 * lax.optimization_barrier(jnp.mean(xf * probe_f, axis=-1, keepdims=True))
    normed = (xf * recip * norm_gain).astype(jnp.bfloat16)
    d_normed = ((probe_f * recip + xf * d_recip) * norm_gain).astype(jnp.bfloat16)
    proj = mix('td,hde->the', normed, head_maps)
    d_proj = mix('td,hde->the', d_normed, head_maps)
    attended, d_attended = local_heads(proj, d_proj, query_gain, key_gain)
    out = jnp.dot(attended, out_map, preferred_element_type=jnp.float32)
    d_out = jnp.dot(d_attended, out_map, preferred_element_type=jnp.float32)
    velocity = (out_gate * out).astype(jnp.bfloat16)
    tangent = (out_gate * d_out).astype(jnp.bfloat16)
    velocity, tangent = lax.optimization_barrier((velocity, tangent))
    velocity = velocity.astype(jnp.float32)
    tangent = tangent.astype(jnp.float32)
    return (velocity, jnp.sum(probe_f * tangent))

def reference(state, probe, norm_gain, head_maps, query_gain, key_gain, out_map, out_gate):
    probe_f = probe.astype(jnp.float32)
    start_f = state.astype(jnp.float32)
    first, trace_first = field(state, probe_f, norm_gain, head_maps, query_gain, key_gain, out_map, out_gate)
    middle = (start_f + step_length * first).astype(jnp.bfloat16)
    second, trace_second = field(middle, probe_f, norm_gain, head_maps, query_gain, key_gain, out_map, out_gate)
    next_state = (start_f + 0.5 * step_length * (first + second)).astype(jnp.bfloat16)
    change = -0.5 * step_length * (trace_first + trace_second) / TOKENS
    return (next_state, jnp.reshape(change, (1,)).astype(jnp.float32))
```

```python
import jax
import jax.numpy as jnp
from jax import lax
from jax.experimental import pallas as pl
from jax.experimental.pallas import tpu as pltpu
from jax.sharding import Mesh, PartitionSpec as P

EPS = 1e-06
STEP = 0.5
SEQ = ("z", "y", "c")
BF = jnp.bfloat16
F32 = jnp.float32
NT = (((1,), (1,)), ((), ()))
TOK = 192
SCALE = 128 ** (-0.5)


def dot(a, b):
    return jnp.dot(a, b, preferred_element_type=F32)


def dot_nt(a, b):
    return lax.dot_general(a, b, NT, preferred_element_type=F32)


def row_mean(v):
    return jnp.mean(v, axis=-1, keepdims=True)


def call(kernel, out_shape, n_scalar, *args):
    in_specs = [pl.BlockSpec(memory_space=pltpu.SMEM)] * n_scalar
    for a in args[n_scalar:]:
        if isinstance(a, tuple):
            in_specs.append(pl.BlockSpec(memory_space=pl.ANY))
        else:
            in_specs.append(pl.BlockSpec(memory_space=pltpu.VMEM))
    flat = [a[0] if isinstance(a, tuple) else a for a in args]
    multi = isinstance(out_shape, (tuple, list))
    vmem = pl.BlockSpec(memory_space=pltpu.VMEM)
    return pl.pallas_call(
        kernel,
        out_shape=out_shape,
        in_specs=in_specs,
        out_specs=[vmem] * len(out_shape) if multi else vmem,
        compiler_params=pltpu.CompilerParams(vmem_limit_bytes=28 * 1024 * 1024),
    )(*flat)


def shape(dims, kind=BF):
    return jax.ShapeDtypeStruct(dims, kind)


def selectors(first_row_token, rows):
    packed = lax.broadcasted_iota(jnp.int32, (TOK, rows), 1)
    token = lax.broadcasted_iota(jnp.int32, (TOK, rows), 0)
    slot = packed & 7
    base = first_row_token(packed)
    one = jnp.ones((TOK, rows), F32)
    zero = jnp.zeros((TOK, rows), F32)
    main = jnp.where((token == base + slot) & (slot < 6), one, zero).astype(BF)
    rest = [
        jnp.where((token == base + m + 3 * (slot - 6)) & (slot >= 6), one, zero).astype(BF)
        for m in range(3)
    ]
    return main, rest


def pieces(main, rest, chunk_of):
    tail = None
    for m in range(3):
        chunk = chunk_of(m)
        part = dot(rest[m], chunk)
        tail = part if tail is None else tail + part
        yield m * 1024, dot(main, chunk)
    yield 3072, tail


def qkv_norm(proj, q_gain, k_gain):
    query, key, val = proj[:, :128], proj[:, 128:256], proj[:, 256:]
    rq = lax.rsqrt(row_mean(query * query) + EPS)
    rk = lax.rsqrt(row_mean(key * key) + EPS)
    qn = (query * rq * q_gain).astype(BF)
    kn = (key * rk * k_gain).astype(BF)
    return query, key, rq, rk, qn, kn, val.astype(BF)


def probabilities(qn, kn):
    expo = jnp.exp(dot_nt(qn, kn) * SCALE)
    return expo / jnp.sum(expo, axis=-1, keepdims=True)


def attend(proj, q_gain, k_gain):
    _, _, _, _, qn, kn, val = qkv_norm(proj, q_gain, k_gain)
    return dot(probabilities(qn, kn).astype(BF), val).astype(BF)


def attend_tangent(proj, d_proj, q_gain, k_gain):
    query, key, rq, rk, qn, kn, val = qkv_norm(proj, q_gain, k_gain)
    dq, dk, dv = d_proj[:, :128], d_proj[:, 128:256], d_proj[:, 256:].astype(BF)
    drq = -(rq * rq * rq) * row_mean(query * dq)
    drk = -(rk * rk * rk) * row_mean(key * dk)
    dqn = ((dq * rq + query * drq) * q_gain).astype(BF)
    dkn = ((dk * rk + key * drk) * k_gain).astype(BF)
    probs = probabilities(qn, kn)
    ds = (dot_nt(dqn, kn) + dot_nt(qn, dkn)) * SCALE
    d_probs = probs * (ds - jnp.sum(probs * ds, axis=-1, keepdims=True))
    return dot(d_probs.astype(BF), val) + dot(probs.astype(BF), dv)


def tangent_of(raw, sum_sq, sum_sp, probe_proj, q_gain, k_gain):
    recip = lax.rsqrt(sum_sq[:, :1] * (1.0 / 4096) + EPS)
    d_recip = -(recip * recip * recip) * (sum_sp * (1.0 / 4096))
    proj = raw * recip
    d_proj = probe_proj * recip + raw * d_recip
    return attend_tangent(proj, d_proj, q_gain, k_gain)


def first_kernel(
    meta, xa, xb, maps, gain, q_gain, k_gain, att_ref, xc_ref, col_ref, raw_ref, sq_ref
):
    core = meta[0]

    def token_base(packed):
        inner = packed & 127
        other = packed >> 7
        z = (inner >> 3) & 3
        y = inner >> 5
        c = jnp.where(other == 0, core, 1 - core)
        return (z * 8 + y * 2 + c) * 6

    main, rest = selectors(token_base, 256)
    raw = jnp.zeros((TOK, 384), F32)
    sum_sq = jnp.zeros((TOK, 1), F32)
    chunk_of = lambda m: jnp.concatenate(
        [xa[:, m * 1024 : (m + 1) * 1024], xb[:, m * 1024 : (m + 1) * 1024]], axis=0
    )
    for start, x in pieces(main, rest, chunk_of):
        sum_sq = sum_sq + jnp.sum(x * x, axis=-1, keepdims=True)
        scaled = (x * gain[:, start : start + 1024]).astype(BF)
        raw = raw + dot(scaled, maps[start : start + 1024, :])
        for b in range(8):
            xc_ref[start // 128 + b] = x[:, b * 128 : (b + 1) * 128].astype(BF)
    recip = lax.rsqrt(sum_sq * (1.0 / 4096) + EPS)
    att = attend(raw * recip, q_gain[...], k_gain[...])
    for i in range(4):
        att_ref[i] = att
    col_ref[...] = xc_ref[meta[1]]
    raw_ref[...] = raw
    sq_ref[...] = jnp.broadcast_to(sum_sq, (TOK, 128))


def out_product(core, own, oth, out_map):
    total = jnp.zeros((TOK, 128), F32)
    for side, c in ((own, core), (oth, 1 - core)):
        for y in range(4):
            for z in (0, 2):
                b = y * 4 + z
                left = jnp.concatenate([side[b], side[b + 1]], axis=1)
                right = jnp.concatenate(
                    [out_map[z * 8 + y * 2 + c], out_map[z * 8 + 8 + y * 2 + c]], axis=0
                )
                total = total + dot(left, right)
    return total


def middle_kernel(meta, own, oth, out_map, gate, col, vel_ref, mid_ref):
    vel = (gate[...] * out_product(meta[0], own, oth, out_map)).astype(BF)
    vel_ref[...] = vel
    mid = (col[...].astype(F32) + STEP * vel.astype(F32)).astype(BF)
    for i in range(4):
        mid_ref[i] = mid


def second_kernel(meta, own, oth, maps, gain, q_gain, k_gain, att_ref, raw_ref, sq_ref):
    core = meta[0]
    raw = jnp.zeros((TOK, 384), F32)
    sum_sq = jnp.zeros((TOK, 1), F32)
    for side, c in ((own, core), (oth, 1 - core)):
        squares = jnp.zeros((TOK, 128), F32)
        for y in range(4):
            for z in (0, 2):
                b = y * 4 + z
                h0 = z * 8 + y * 2 + c
                left = side[b].astype(F32)
                right = side[b + 1].astype(F32)
                squares = squares + left * left + right * right
                scaled = jnp.concatenate(
                    [(left * gain[h0]).astype(BF), (right * gain[h0 + 8]).astype(BF)], axis=1
                )
                rows = jnp.concatenate([maps[h0], maps[h0 + 8]], axis=0)
                raw = raw + dot(scaled, rows)
        sum_sq = sum_sq + jnp.sum(squares, axis=-1, keepdims=True)
    recip = lax.rsqrt(sum_sq * (1.0 / 4096) + EPS)
    att = attend(raw * recip, q_gain[...], k_gain[...])
    for i in range(4):
        att_ref[i] = att
    raw_ref[...] = raw
    sq_ref[...] = jnp.broadcast_to(sum_sq, (TOK, 128))


def probe_kernel(
    meta, packed, xc, raw1, sq1, maps, out_map, gain, gate, q_gain, k_gain, after,
    pc_ref, pp_ref, datt_ref, back_ref,
):
    main, rest = selectors(lambda row: (row >> 3) * 6, 256)
    proj = jnp.zeros((TOK, 384), F32)
    dots = jnp.zeros((TOK, 128), F32)
    for start, x in pieces(main, rest, lambda m: packed[:, m * 1024 : (m + 1) * 1024]):
        scaled = (x * gain[:, start : start + 1024]).astype(BF)
        proj = proj + dot(scaled, maps[start : start + 1024, :])
        for b in range(8):
            piece = x[:, b * 128 : (b + 1) * 128]
            dots = dots + piece * xc[start // 128 + b].astype(F32)
            pc_ref[start // 128 + b] = piece.astype(BF)
    pp_ref[...] = proj
    sum_sp = jnp.sum(dots, axis=-1, keepdims=True)
    datt_ref[...] = tangent_of(raw1[...], sq1[...], sum_sp, proj, q_gain[...], k_gain[...])
    weighted = (pc_ref[meta[1]].astype(F32) * gate[...]).astype(BF)
    for h in range(32):
        back_ref[h] = dot_nt(weighted, out_map[h]).astype(back_ref.dtype)


def tangent_kernel(meta, own, oth, pc, raw2, sq2, pp, datt1, q_gain, k_gain, datt_ref):
    core = meta[0]
    dots = jnp.zeros((TOK, 128), F32)
    for side, c in ((own, core), (oth, 1 - core)):
        for y in range(4):
            for z in range(4):
                probe = pc[z * 8 + y * 2 + c].astype(F32)
                dots = dots + side[y * 4 + z].astype(F32) * probe
    sum_sp = jnp.sum(dots, axis=-1, keepdims=True)
    datt_ref[...] = datt1[...] + tangent_of(
        raw2[...], sq2[...], sum_sp, pp[...], q_gain[...], k_gain[...]
    )


def last_kernel(meta, own, oth, out_map, gate, col, vel1, datt, back, out_ref):
    vel = (gate[...] * out_product(meta[0], own, oth, out_map)).astype(BF)
    both = vel1[...].astype(F32) + vel.astype(F32)
    new = (col[...].astype(F32) + 0.5 * STEP * both).astype(BF)
    row = lax.broadcasted_iota(jnp.int32, (256, TOK), 0)
    token = lax.broadcasted_iota(jnp.int32, (256, TOK), 1)
    hit = (token == (row >> 3) * 6 + (row & 7)) & ((row & 7) < 6)
    place = jnp.where(hit, jnp.ones((256, TOK), F32), jnp.zeros((256, TOK), F32)).astype(BF)
    spread = dot(place, new)
    partial = jnp.sum(datt[...] * back[...].astype(F32), axis=0, keepdims=True)
    trace = jnp.sum(partial, axis=1, keepdims=True)
    high = trace.astype(BF).astype(F32)
    mid = (trace - high).astype(BF).astype(F32)
    low = trace - high - mid
    lane = lax.broadcasted_iota(jnp.int32, (1, 128), 1)
    coded = jnp.where(lane == 0, high, jnp.where(lane == 1, mid, jnp.where(lane == 2, low, 0.0)))
    slot = lax.broadcasted_iota(jnp.int32, (256, 128), 0) & 7
    out_ref[...] = jnp.where(slot == 6, coded, spread).astype(BF)


def land_kernel(got, next_ref, change_ref):
    total = jnp.zeros((8, 128), F32)
    for j in range(32):
        block = got[j]
        next_ref[:, j * 128 : (j + 1) * 128] = block[:6]
        total = total + block.astype(F32)
    trace = jnp.sum(total[6:7, :], axis=1, keepdims=True)
    change_ref[...] = jnp.broadcast_to(-0.5 * STEP * trace / TOK, (1, 128))


def spread(copies, rows, lanes):
    a = lax.all_to_all(copies.reshape(4 * rows, lanes), "z", 0, 0, tiled=True)
    b = lax.all_to_all(jnp.tile(a, (4, 1)), "y", 0, 0, tiled=True)
    return a, b


def swap(block):
    return lax.ppermute(block, "c", [(0, 1), (1, 0)])


def pack(rows):
    return jnp.concatenate([rows[:, :3072], rows[:, 3072:].reshape(2, 3072)], axis=0)


def per_device(state, probe, norm_gain, head_maps, query_gain, key_gain, out_map, out_gate):
    core = lax.axis_index("c")
    place = lax.axis_index(SEQ)
    meta = jnp.stack([core, place]).astype(jnp.int32)
    gate = lax.dynamic_slice_in_dim(out_gate, place * 128, 128).reshape(1, 128)
    maps = head_maps.reshape(4096, 384)
    maps_blocks = head_maps.reshape(32, 128, 384)
    out_blocks = out_map.reshape(32, 128, 128)
    gain = norm_gain.reshape(1, 4096)
    gain_blocks = norm_gain.reshape(32, 1, 128)

    packed_probe = lax.all_gather(pack(probe), SEQ, axis=0, tiled=True)
    _, own = spread(jnp.broadcast_to(pack(state)[None], (4, 8, 3072)), 8, 3072)
    att1, xc, col, raw1, sq1 = call(
        first_kernel,
        [shape((4, TOK, 128)), shape((32, TOK, 128)), shape((TOK, 128)), shape((TOK, 384), F32), shape((TOK, 128), F32)],
        1, meta, own, swap(own), maps, gain, query_gain, key_gain,
    )

    def gathered(copies):
        a, b = spread(copies, TOK, 128)
        other = swap(b)
        return a, b.reshape(16, TOK, 128), other.reshape(16, TOK, 128)

    _, own1, oth1 = gathered(att1)
    vel1, mid = call(
        middle_kernel, [shape((TOK, 128)), shape((4, TOK, 128))],
        1, meta, own1, oth1, out_blocks, gate, col,
    )
    early, own_m, oth_m = gathered(mid)
    pc, pp, datt1, back = call(
        probe_kernel,
        [shape((32, TOK, 128)), shape((TOK, 384), F32), shape((TOK, 128), F32), shape((32, TOK, 128), F32)],
        1, meta, packed_probe, xc, raw1, sq1, maps, out_blocks, gain, gate, query_gain, key_gain, (early,),
    )
    adjoint = lax.psum_scatter(back, SEQ, scatter_dimension=0, tiled=False)
    att2, raw2, sq2 = call(
        second_kernel,
        [shape((4, TOK, 128)), shape((TOK, 384), F32), shape((TOK, 128), F32)],
        1, meta, own_m, oth_m, maps_blocks, gain_blocks, query_gain, key_gain,
    )
    datt = call(
        tangent_kernel, shape((TOK, 128), F32),
        1, meta, own_m, oth_m, pc, raw2, sq2, pp, datt1, query_gain, key_gain,
    )
    _, own2, oth2 = gathered(att2)
    columns = call(
        last_kernel, shape((256, 128)),
        1, meta, own2, oth2, out_blocks, gate, col, vel1, datt, adjoint,
    )
    got = lax.all_to_all(columns, SEQ, 0, 0, tiled=True).reshape(32, 8, 128)
    next_state, change = call(land_kernel, [shape((6, 4096)), shape((1, 128), F32)], 0, got)
    return next_state, change[0, :1]


def solution(mesh):
    split = Mesh(mesh.devices.reshape(4, 4, 2, 4, 4), ("z", "y", "c", "w", "x"))
    rows = P(("w", "x", "z", "y", "c"), None)
    return jax.shard_map(
        per_device,
        mesh=split,
        in_specs=(rows, rows, P(), P(SEQ, None, None), P(SEQ, None), P(SEQ, None), P(None, SEQ), P()),
        out_specs=(rows, P(("w", "x"))),
        check_vma=False,
    )
```

```python
import jax
import jax.numpy as jnp
from jax import lax
from jax.experimental import pallas as pl
from jax.experimental.pallas import tpu as pltpu
from jax.sharding import Mesh, PartitionSpec as P

EPS = 1e-06
STEP = 0.5
SEQ = ("z", "y", "c")
BF = jnp.bfloat16
F32 = jnp.float32
NT = (((1,), (1,)), ((), ()))
TOK = 192
SCALE = 128 ** (-0.5)


def dot(a, b):
    return jnp.dot(a, b, preferred_element_type=F32)


def dot_nt(a, b):
    return lax.dot_general(a, b, NT, preferred_element_type=F32)


def row_mean(v):
    return jnp.mean(v, axis=-1, keepdims=True)


HELD = [pltpu.VMEM((32, TOK, 128), BF)]


def call(kernel, out_shape, n_scalar, *args, scratch=()):
    in_specs = [pl.BlockSpec(memory_space=pltpu.SMEM)] * n_scalar
    for a in args[n_scalar:]:
        if isinstance(a, tuple):
            in_specs.append(pl.BlockSpec(memory_space=pl.ANY))
        else:
            in_specs.append(pl.BlockSpec(memory_space=pltpu.VMEM))
    flat = [a[0] if isinstance(a, tuple) else a for a in args]
    multi = isinstance(out_shape, (tuple, list))
    vmem = pl.BlockSpec(memory_space=pltpu.VMEM)
    return pl.pallas_call(
        kernel,
        out_shape=out_shape,
        in_specs=in_specs,
        out_specs=[vmem] * len(out_shape) if multi else vmem,
        scratch_shapes=scratch,
        compiler_params=pltpu.CompilerParams(vmem_limit_bytes=20 * 1024 * 1024),
    )(*flat)


def shape(dims, kind=BF):
    return jax.ShapeDtypeStruct(dims, kind)


def selectors(first_row_token, rows):
    packed = lax.broadcasted_iota(jnp.int32, (TOK, rows), 1)
    token = lax.broadcasted_iota(jnp.int32, (TOK, rows), 0)
    slot = packed & 7
    base = first_row_token(packed)
    one = jnp.ones((TOK, rows), F32)
    zero = jnp.zeros((TOK, rows), F32)
    main = jnp.where((token == base + slot) & (slot < 6), one, zero).astype(BF)
    rest = [
        jnp.where((token == base + m + 3 * (slot - 6)) & (slot >= 6), one, zero).astype(BF)
        for m in range(3)
    ]
    return main, rest


def pieces(main, rest, chunk_of):
    tail = None
    for m in range(3):
        chunk = chunk_of(m)
        part = dot(rest[m], chunk)
        tail = part if tail is None else tail + part
        yield m * 1024, dot(main, chunk)
    yield 3072, tail


def qkv_norm(proj, q_gain, k_gain):
    query, key, val = proj[:, :128], proj[:, 128:256], proj[:, 256:]
    rq = lax.rsqrt(row_mean(query * query) + EPS)
    rk = lax.rsqrt(row_mean(key * key) + EPS)
    qn = (query * rq * q_gain).astype(BF)
    kn = (key * rk * k_gain).astype(BF)
    return query, key, rq, rk, qn, kn, val.astype(BF)


def probabilities(qn, kn):
    expo = jnp.exp(dot_nt(qn, kn) * SCALE)
    return expo / jnp.sum(expo, axis=-1, keepdims=True)


def attend(proj, q_gain, k_gain):
    _, _, _, _, qn, kn, val = qkv_norm(proj, q_gain, k_gain)
    return dot(probabilities(qn, kn).astype(BF), val).astype(BF)


def attend_tangent(proj, d_proj, q_gain, k_gain):
    query, key, rq, rk, qn, kn, val = qkv_norm(proj, q_gain, k_gain)
    dq, dk, dv = d_proj[:, :128], d_proj[:, 128:256], d_proj[:, 256:].astype(BF)
    drq = -(rq * rq * rq) * row_mean(query * dq)
    drk = -(rk * rk * rk) * row_mean(key * dk)
    dqn = ((dq * rq + query * drq) * q_gain).astype(BF)
    dkn = ((dk * rk + key * drk) * k_gain).astype(BF)
    probs = probabilities(qn, kn)
    ds = (dot_nt(dqn, kn) + dot_nt(qn, dkn)) * SCALE
    d_probs = probs * (ds - jnp.sum(probs * ds, axis=-1, keepdims=True))
    probs = probs.astype(BF)
    return dot(probs, val).astype(BF), dot(d_probs.astype(BF), val) + dot(probs, dv)


def pack_kernel(state, probe, state_ref, probe_ref):
    for source, write in ((state, None), (probe, probe_ref)):
        main = source[:, :3072]
        sixth = jnp.concatenate([source[q : q + 1, 3072:] for q in range(3)], axis=1)
        seventh = jnp.concatenate([source[q : q + 1, 3072:] for q in range(3, 6)], axis=1)
        whole = jnp.concatenate([main, sixth, seventh], axis=0)
        if write is None:
            for i in range(4):
                state_ref[i] = whole
        else:
            write[:, :3072] = whole
            write[:, 3072:] = whole


def core_order(core):
    def first_token(packed):
        inner = packed & 127
        z = (inner >> 3) & 3
        y = inner >> 5
        c = jnp.where((packed >> 7) == 0, core, 1 - core)
        return (z * 8 + y * 2 + c) * 6

    return first_token


def unpack_state(core, xa, xb, held):
    main, rest = selectors(core_order(core), 256)
    squares = jnp.zeros((TOK, 128), F32)

    def chunk_of(m):
        cols = slice(m * 1024, (m + 1) * 1024)
        return jnp.concatenate([xa[:, cols], xb[:, cols]], axis=0)

    for start, x in pieces(main, rest, chunk_of):
        for b in range(8):
            piece = x[:, b * 128 : (b + 1) * 128]
            squares = squares + piece * piece
            held[start // 128 + b] = piece.astype(BF)
    return lax.rsqrt(row_sum(squares) * (1.0 / 4096) + EPS)


def row_sum(v):
    return jnp.sum(v, axis=-1, keepdims=True)


def first_kernel(meta, xa, xb, maps, gain, q_gain, k_gain, att_ref, col_ref, held):
    recip = unpack_state(meta[0], xa, xb, held)
    proj = jnp.zeros((TOK, 384), F32)
    for h in range(0, 32, 2):
        left = (held[h].astype(F32) * recip * gain[h]).astype(BF)
        right = (held[h + 1].astype(F32) * recip * gain[h + 1]).astype(BF)
        rows = jnp.concatenate([maps[h], maps[h + 1]], axis=0)
        proj = proj + dot(jnp.concatenate([left, right], axis=1), rows)
    att = attend(proj, q_gain[...], k_gain[...])
    for i in range(4):
        att_ref[i] = att
    col_ref[...] = held[meta[1]]


def blocks(core, own, oth):
    for side, c in ((own, core), (oth, 1 - core)):
        for y in range(4):
            for z in (0, 2):
                yield side, y * 4 + z, z * 8 + y * 2 + c


def out_product(core, own, oth, out_map):
    total = jnp.zeros((own.shape[1], 128), F32)
    for side, b, h in blocks(core, own, oth):
        left = jnp.concatenate([side[b], side[b + 1]], axis=1)
        right = jnp.concatenate([out_map[h], out_map[h + 8]], axis=0)
        total = total + dot(left, right)
    return total


def middle_kernel(meta, own, oth, out_map, gate, col, vel_ref, mid_ref):
    vel = (gate[...] * out_product(meta[0], own, oth, out_map)).astype(BF)
    vel_ref[...] = vel
    mid = (col[...].astype(F32) + STEP * vel.astype(F32)).astype(BF)
    for i in range(4):
        mid_ref[i] = mid


def both_rows(x, probe, recip, d_recip, gain):
    normed = (x * recip * gain).astype(BF)
    d_normed = ((probe * recip + x * d_recip) * gain).astype(BF)
    return jnp.concatenate([normed, d_normed], axis=0)


def tangent_kernel(
    meta, xa, xb, packed, maps, gain, q_gain, k_gain, after, probe_ref, datt_ref, held
):
    recip = unpack_state(meta[0], xa, xb, held)
    main, rest = selectors(lambda row: (row >> 3) * 6, 256)
    dots = jnp.zeros((TOK, 128), F32)
    for start, x in pieces(main, rest, lambda m: packed[:, m * 1024 : (m + 1) * 1024]):
        for b in range(8):
            piece = x[:, b * 128 : (b + 1) * 128]
            dots = dots + piece * held[start // 128 + b].astype(F32)
            probe_ref[start // 128 + b] = piece.astype(BF)
    d_recip = -(recip * recip * recip) * (row_sum(dots) * (1.0 / 4096))
    proj = jnp.zeros((2 * TOK, 384), F32)
    for h in range(0, 32, 2):
        pair = [
            both_rows(held[i].astype(F32), probe_ref[i].astype(F32), recip, d_recip, gain[i])
            for i in (h, h + 1)
        ]
        rows = jnp.concatenate([maps[h], maps[h + 1]], axis=0)
        proj = proj + dot(jnp.concatenate(pair, axis=1), rows)
    datt_ref[...] = attend_tangent(proj[:TOK], proj[TOK:], q_gain[...], k_gain[...])[1]


def second_kernel(meta, own, oth, probe, maps, gain, q_gain, k_gain, datt1, both_ref):
    core = meta[0]
    squares = jnp.zeros((TOK, 128), F32)
    dots = jnp.zeros((TOK, 128), F32)
    for side, b, h in blocks(core, own, oth):
        for i in range(2):
            x = side[b + i].astype(F32)
            squares = squares + x * x
            dots = dots + x * probe[h + 8 * i].astype(F32)
    recip = lax.rsqrt(row_sum(squares) * (1.0 / 4096) + EPS)
    d_recip = -(recip * recip * recip) * (row_sum(dots) * (1.0 / 4096))
    proj = jnp.zeros((2 * TOK, 384), F32)
    for side, b, h in blocks(core, own, oth):
        pair = [
            both_rows(
                side[b + i].astype(F32), probe[h + 8 * i].astype(F32), recip, d_recip, gain[h + 8 * i]
            )
            for i in range(2)
        ]
        rows = jnp.concatenate([maps[h], maps[h + 8]], axis=0)
        proj = proj + dot(jnp.concatenate(pair, axis=1), rows)
    att, d_att = attend_tangent(proj[:TOK], proj[TOK:], q_gain[...], k_gain[...])
    d_both = (d_att + datt1[...]).astype(BF)
    for i in range(4):
        both_ref[i, :TOK] = att
        both_ref[i, TOK:] = d_both


def last_kernel(meta, own, oth, out_map, gate, col, vel1, probe, out_ref):
    mapped = gate[...] * out_product(meta[0], own, oth, out_map)
    both = vel1[...].astype(F32) + mapped[:TOK].astype(BF).astype(F32)
    new = (col[...].astype(F32) + 0.5 * STEP * both).astype(BF)
    row = lax.broadcasted_iota(jnp.int32, (256, TOK), 0)
    token = lax.broadcasted_iota(jnp.int32, (256, TOK), 1)
    hit = (token == (row >> 3) * 6 + (row & 7)) & ((row & 7) < 6)
    place = jnp.where(hit, jnp.ones((256, TOK), F32), jnp.zeros((256, TOK), F32)).astype(BF)
    laid = dot(place, new)
    terms = mapped[TOK:] * probe[meta[1]].astype(F32)
    trace = row_sum(jnp.sum(terms, axis=0, keepdims=True))
    high = trace.astype(BF).astype(F32)
    mid = (trace - high).astype(BF).astype(F32)
    low = trace - high - mid
    lane = lax.broadcasted_iota(jnp.int32, (1, 128), 1)
    coded = jnp.where(lane == 0, high, jnp.where(lane == 1, mid, jnp.where(lane == 2, low, 0.0)))
    slot = lax.broadcasted_iota(jnp.int32, (256, 128), 0) & 7
    out_ref[...] = jnp.where(slot == 6, coded, laid).astype(BF)


def land_kernel(got, next_ref, change_ref):
    total = jnp.zeros((8, 128), F32)
    for j in range(32):
        block = got[j]
        next_ref[:, j * 128 : (j + 1) * 128] = block[:6]
        total = total + block.astype(F32)
    change_ref[...] = jnp.broadcast_to(-0.5 * STEP * row_sum(total[6:7, :]) / TOK, (1, 128))


def spread(copies):
    n, rows, lanes = copies.shape
    a = lax.all_to_all(copies.reshape(n * rows, lanes), "z", 0, 0, tiled=True)
    return a, lax.all_to_all(jnp.tile(a, (4, 1)), "y", 0, 0, tiled=True)


def swap(block):
    return lax.ppermute(block, "c", [(0, 1), (1, 0)])


def gathered(copies):
    rows = copies.shape[1]
    early, own = spread(copies)
    other = swap(own)
    return early, own.reshape(16, rows, 128), other.reshape(16, rows, 128)


def per_device(state, probe, norm_gain, head_maps, query_gain, key_gain, out_map, out_gate):
    place = lax.axis_index(SEQ)
    meta = jnp.stack([lax.axis_index("c"), place]).astype(jnp.int32)
    gate = lax.dynamic_slice_in_dim(out_gate, place * 128, 128).reshape(1, 128)
    maps = head_maps.reshape(32, 128, 384)
    outs = out_map.reshape(32, 128, 128)
    gain = norm_gain.reshape(32, 1, 128)

    packed_state, packed_probe = call(
        pack_kernel, [shape((4, 8, 3072)), shape((8, 6144))], 0, state, probe
    )
    probe_all = lax.all_gather(packed_probe, SEQ, axis=0, tiled=True)
    _, own = spread(packed_state)
    oth = swap(own)
    att1, col = call(
        first_kernel, [shape((4, TOK, 128)), shape((TOK, 128))],
        1, meta, own, oth, maps, gain, query_gain, key_gain, scratch=HELD,
    )
    _, own1, oth1 = gathered(att1)
    vel1, mid = call(
        middle_kernel, [shape((TOK, 128)), shape((4, TOK, 128))],
        1, meta, own1, oth1, outs, gate, col,
    )
    early, own_m, oth_m = gathered(mid)
    probe_blocks, datt1 = call(
        tangent_kernel, [shape((32, TOK, 128)), shape((TOK, 128), F32)],
        1, meta, own, oth, probe_all, maps, gain, query_gain, key_gain, (early,), scratch=HELD,
    )
    both = call(
        second_kernel, shape((4, 2 * TOK, 128)),
        1, meta, own_m, oth_m, probe_blocks, maps, gain, query_gain, key_gain, datt1,
    )
    _, own2, oth2 = gathered(both)
    columns = call(
        last_kernel, shape((256, 128)),
        1, meta, own2, oth2, outs, gate, col, vel1, probe_blocks,
    )
    got = lax.all_to_all(columns, SEQ, 0, 0, tiled=True).reshape(32, 8, 128)
    next_state, change = call(land_kernel, [shape((6, 4096)), shape((1, 128), F32)], 0, got)
    return next_state, change[0, :1]


def solution(mesh):
    split = Mesh(mesh.devices.reshape(4, 4, 2, 4, 4), ("z", "y", "c", "w", "x"))
    rows = P(("w", "x", "z", "y", "c"), None)
    return jax.shard_map(
        per_device,
        mesh=split,
        in_specs=(rows, rows, P(), P(SEQ, None, None), P(SEQ, None), P(SEQ, None), P(None, SEQ), P()),
        out_specs=(rows, P(("w", "x"))),
        check_vma=False,
    )
```

```python
import jax
import jax.numpy as jnp
from jax import lax
from jax.experimental import pallas as pl
from jax.experimental.pallas import tpu as pltpu
from jax.sharding import Mesh, PartitionSpec as P

EPS = 1e-06
STEP = 0.5
SEQ = ("z", "y", "c")
BF = jnp.bfloat16
F32 = jnp.float32
NT = (((1,), (1,)), ((), ()))
TOK = 192
SCALE = 128 ** (-0.5)


def dot(a, b):
    return jnp.dot(a, b, preferred_element_type=F32)


def dot_nt(a, b):
    return lax.dot_general(a, b, NT, preferred_element_type=F32)


def row_mean(v):
    return jnp.mean(v, axis=-1, keepdims=True)


HELD = [pltpu.VMEM((32, TOK, 128), BF)]


def call(kernel, out_shape, n_scalar, *args, scratch=()):
    in_specs = [pl.BlockSpec(memory_space=pltpu.SMEM)] * n_scalar
    for a in args[n_scalar:]:
        if isinstance(a, tuple):
            in_specs.append(pl.BlockSpec(memory_space=pl.ANY))
        else:
            in_specs.append(pl.BlockSpec(memory_space=pltpu.VMEM))
    flat = [a[0] if isinstance(a, tuple) else a for a in args]
    multi = isinstance(out_shape, (tuple, list))
    vmem = pl.BlockSpec(memory_space=pltpu.VMEM)
    return pl.pallas_call(
        kernel,
        out_shape=out_shape,
        in_specs=in_specs,
        out_specs=[vmem] * len(out_shape) if multi else vmem,
        scratch_shapes=scratch,
        compiler_params=pltpu.CompilerParams(vmem_limit_bytes=20 * 1024 * 1024),
    )(*flat)


def shape(dims, kind=BF):
    return jax.ShapeDtypeStruct(dims, kind)


def selectors(first_row_token, rows):
    packed = lax.broadcasted_iota(jnp.int32, (TOK, rows), 1)
    token = lax.broadcasted_iota(jnp.int32, (TOK, rows), 0)
    slot = packed & 7
    base = first_row_token(packed)
    one = jnp.ones((TOK, rows), F32)
    zero = jnp.zeros((TOK, rows), F32)
    main = jnp.where((token == base + slot) & (slot < 6), one, zero).astype(BF)
    rest = [
        jnp.where((token == base + m + 3 * (slot - 6)) & (slot >= 6), one, zero).astype(BF)
        for m in range(3)
    ]
    return main, rest


def pieces(main, rest, chunk_of):
    tail = None
    for m in range(3):
        chunk = chunk_of(m)
        part = dot(rest[m], chunk)
        tail = part if tail is None else tail + part
        yield m * 1024, dot(main, chunk)
    yield 3072, tail


def qkv_norm(proj, q_gain, k_gain):
    query, key, val = proj[:, :128], proj[:, 128:256], proj[:, 256:]
    rq = lax.rsqrt(row_mean(query * query) + EPS)
    rk = lax.rsqrt(row_mean(key * key) + EPS)
    qn = (query * rq * q_gain).astype(BF)
    kn = (key * rk * k_gain).astype(BF)
    return query, key, rq, rk, qn, kn, val.astype(BF)


def probabilities(qn, kn):
    expo = jnp.exp(dot_nt(qn, kn) * SCALE)
    return expo / jnp.sum(expo, axis=-1, keepdims=True)


def attend(proj, q_gain, k_gain):
    _, _, _, _, qn, kn, val = qkv_norm(proj, q_gain, k_gain)
    return dot(probabilities(qn, kn).astype(BF), val).astype(BF)


def attend_tangent(proj, d_proj, q_gain, k_gain):
    query, key, rq, rk, qn, kn, val = qkv_norm(proj, q_gain, k_gain)
    dq, dk, dv = d_proj[:, :128], d_proj[:, 128:256], d_proj[:, 256:].astype(BF)
    drq = -(rq * rq * rq) * row_mean(query * dq)
    drk = -(rk * rk * rk) * row_mean(key * dk)
    dqn = ((dq * rq + query * drq) * q_gain).astype(BF)
    dkn = ((dk * rk + key * drk) * k_gain).astype(BF)
    probs = probabilities(qn, kn)
    ds = (dot_nt(dqn, kn) + dot_nt(qn, dkn)) * SCALE
    d_probs = probs * (ds - jnp.sum(probs * ds, axis=-1, keepdims=True))
    probs = probs.astype(BF)
    return dot(probs, val).astype(BF), dot(d_probs.astype(BF), val) + dot(probs, dv)


def pack_kernel(state, probe, state_ref, probe_ref):
    for source, write in ((state, None), (probe, probe_ref)):
        main = source[:, :3072]
        sixth = jnp.concatenate([source[q : q + 1, 3072:] for q in range(3)], axis=1)
        seventh = jnp.concatenate([source[q : q + 1, 3072:] for q in range(3, 6)], axis=1)
        whole = jnp.concatenate([main, sixth, seventh], axis=0)
        if write is None:
            for i in range(4):
                state_ref[i] = whole
        else:
            write[:, :3072] = whole
            write[:, 3072:] = whole


def core_order(core):
    def first_token(packed):
        inner = packed & 127
        z = (inner >> 3) & 3
        y = inner >> 5
        c = jnp.where((packed >> 7) == 0, core, 1 - core)
        return (z * 8 + y * 2 + c) * 6

    return first_token


def unpack_state(core, xa, xb, held):
    main, rest = selectors(core_order(core), 256)
    squares = jnp.zeros((TOK, 128), F32)

    def chunk_of(m):
        cols = slice(m * 1024, (m + 1) * 1024)
        return jnp.concatenate([xa[:, cols], xb[:, cols]], axis=0)

    for start, x in pieces(main, rest, chunk_of):
        for b in range(8):
            piece = x[:, b * 128 : (b + 1) * 128]
            squares = squares + piece * piece
            held[start // 128 + b] = piece.astype(BF)
    return lax.rsqrt(row_sum(squares) * (1.0 / 4096) + EPS)


def row_sum(v):
    return jnp.sum(v, axis=-1, keepdims=True)


def first_kernel(meta, xa, xb, maps, gain, q_gain, k_gain, att_ref, col_ref, held):
    recip = unpack_state(meta[0], xa, xb, held)
    proj = jnp.zeros((TOK, 384), F32)
    for h in range(0, 32, 2):
        left = (held[h].astype(F32) * recip * gain[h]).astype(BF)
        right = (held[h + 1].astype(F32) * recip * gain[h + 1]).astype(BF)
        rows = jnp.concatenate([maps[h], maps[h + 1]], axis=0)
        proj = proj + dot(jnp.concatenate([left, right], axis=1), rows)
    att = attend(proj, q_gain[...], k_gain[...])
    for i in range(4):
        att_ref[i] = att
    col_ref[...] = held[meta[1]]


def blocks(core, own, oth):
    for side, c in ((own, core), (oth, 1 - core)):
        for y in range(4):
            for z in (0, 2):
                yield side, y * 4 + z, z * 8 + y * 2 + c


def out_product(core, own, oth, out_map):
    total = jnp.zeros((own.shape[1], 128), F32)
    for side, b, h in blocks(core, own, oth):
        left = jnp.concatenate([side[b], side[b + 1]], axis=1)
        right = jnp.concatenate([out_map[h], out_map[h + 8]], axis=0)
        total = total + dot(left, right)
    return total


def middle_kernel(meta, own, oth, out_map, gate, col, vel_ref, mid_ref):
    vel = (gate[...] * out_product(meta[0], own, oth, out_map)).astype(BF)
    vel_ref[...] = vel
    mid = (col[...].astype(F32) + STEP * vel.astype(F32)).astype(BF)
    for i in range(4):
        mid_ref[i] = mid


def both_rows(x, probe, recip, d_recip, gain):
    normed = (x * recip * gain).astype(BF)
    d_normed = ((probe * recip + x * d_recip) * gain).astype(BF)
    return jnp.concatenate([normed, d_normed], axis=0)


def tangent_kernel(
    meta, xa, xb, packed, maps, gain, q_gain, k_gain, after, probe_ref, datt_ref, held
):
    recip = unpack_state(meta[0], xa, xb, held)
    main, rest = selectors(lambda row: (row >> 3) * 6, 256)
    dots = jnp.zeros((TOK, 128), F32)
    for start, x in pieces(main, rest, lambda m: packed[:, m * 1024 : (m + 1) * 1024]):
        for b in range(8):
            piece = x[:, b * 128 : (b + 1) * 128]
            dots = dots + piece * held[start // 128 + b].astype(F32)
            probe_ref[start // 128 + b] = piece.astype(BF)
    d_recip = -(recip * recip * recip) * (row_sum(dots) * (1.0 / 4096))
    proj = jnp.zeros((2 * TOK, 384), F32)
    for h in range(0, 32, 2):
        pair = [
            both_rows(held[i].astype(F32), probe_ref[i].astype(F32), recip, d_recip, gain[i])
            for i in (h, h + 1)
        ]
        rows = jnp.concatenate([maps[h], maps[h + 1]], axis=0)
        proj = proj + dot(jnp.concatenate(pair, axis=1), rows)
    datt_ref[...] = attend_tangent(proj[:TOK], proj[TOK:], q_gain[...], k_gain[...])[1]


def second_kernel(meta, own, oth, probe, maps, gain, q_gain, k_gain, datt1, both_ref):
    core = meta[0]
    squares = jnp.zeros((TOK, 128), F32)
    dots = jnp.zeros((TOK, 128), F32)
    for side, b, h in blocks(core, own, oth):
        for i in range(2):
            x = side[b + i].astype(F32)
            squares = squares + x * x
            dots = dots + x * probe[h + 8 * i].astype(F32)
    recip = lax.rsqrt(row_sum(squares) * (1.0 / 4096) + EPS)
    d_recip = -(recip * recip * recip) * (row_sum(dots) * (1.0 / 4096))
    proj = jnp.zeros((2 * TOK, 384), F32)
    for side, b, h in blocks(core, own, oth):
        pair = [
            both_rows(
                side[b + i].astype(F32), probe[h + 8 * i].astype(F32), recip, d_recip, gain[h + 8 * i]
            )
            for i in range(2)
        ]
        rows = jnp.concatenate([maps[h], maps[h + 8]], axis=0)
        proj = proj + dot(jnp.concatenate(pair, axis=1), rows)
    att, d_att = attend_tangent(proj[:TOK], proj[TOK:], q_gain[...], k_gain[...])
    d_both = (d_att + datt1[...]).astype(BF)
    for i in range(4):
        both_ref[i, :TOK] = att
        both_ref[i, TOK:] = d_both


def last_kernel(meta, own, oth, out_maps, gates, vel1, probe, out_ref, rows, sem):
    core, place, plane = meta[0], meta[1], meta[2]
    copy = pltpu.make_async_copy(out_maps.at[:, pl.ds(plane * 8, 8)], rows, sem)
    copy.start()
    row = lax.broadcasted_iota(jnp.int32, (256, TOK), 0)
    token = lax.broadcasted_iota(jnp.int32, (256, TOK), 1)
    hit = (token == (row >> 3) * 6 + (row & 7)) & ((row & 7) < 6)
    lay = jnp.where(hit, jnp.ones((256, TOK), F32), jnp.zeros((256, TOK), F32)).astype(BF)
    left = []
    for y in range(4):
        mine = own[y]
        other = oth[y]
        first = jnp.where(core == 0, mine, other)
        second = jnp.where(core == 0, other, mine)
        left.append(jnp.concatenate([first, second], axis=1))
    in_plane = place - plane * 8
    copy.wait()
    trace = jnp.zeros((1, 128), F32)
    laid = []
    for z in range(4):
        mapped = jnp.zeros((2 * TOK, 128), F32)
        for y in range(4):
            right = jnp.concatenate([rows[z, y * 2], rows[z, y * 2 + 1]], axis=0)
            mapped = mapped + dot(left[y], right)
        column = z * 8 + in_plane
        mapped = mapped * gates[column]
        terms = mapped[TOK:] * probe[column].astype(F32)
        trace = trace + jnp.sum(terms, axis=0, keepdims=True)
        vel = vel1[...].astype(F32)
        part = mapped[:TOK] + jnp.where(plane == z, vel, jnp.zeros_like(vel))
        laid.append(dot(lay, part.astype(BF)))
    trace = row_sum(trace)
    high = trace.astype(BF).astype(F32)
    mid = (trace - high).astype(BF).astype(F32)
    low = trace - high - mid
    lane = lax.broadcasted_iota(jnp.int32, (1, 128), 1)
    coded = jnp.where(lane == 0, high, jnp.where(lane == 1, mid, jnp.where(lane == 2, low, 0.0)))
    slot = lax.broadcasted_iota(jnp.int32, (256, 128), 0) & 7
    for z in range(4):
        block = jnp.where(slot == 6, coded, laid[z]) if z == 0 else laid[z]
        out_ref[:, z * 128 : (z + 1) * 128] = block.astype(BF)


def land_kernel(got, state, next_ref, change_ref):
    total = jnp.zeros((8, 128), F32)
    for j in range(8):
        sums = got[j].astype(F32)
        total = total + sums[:, :128]
        for z in range(1, 4):
            block = got[z * 8 + j].astype(F32)
            total = total + block[:, :128]
            sums = sums + block
        for z in range(4):
            cols = slice((z * 8 + j) * 128, (z * 8 + j + 1) * 128)
            both = sums[:6, z * 128 : (z + 1) * 128]
            next_ref[:, cols] = (state[:, cols].astype(F32) + 0.5 * STEP * both).astype(BF)
    change_ref[...] = jnp.broadcast_to(-0.5 * STEP * row_sum(total[6:7, :]) / TOK, (1, 128))


def spread(copies):
    n, rows, lanes = copies.shape
    a = lax.all_to_all(copies.reshape(n * rows, lanes), "z", 0, 0, tiled=True)
    return a, lax.all_to_all(jnp.tile(a, (4, 1)), "y", 0, 0, tiled=True)


def swap(block):
    return lax.ppermute(block, "c", [(0, 1), (1, 0)])


def gathered(copies):
    rows = copies.shape[1]
    early, own = spread(copies)
    other = swap(own)
    return early, own.reshape(16, rows, 128), other.reshape(16, rows, 128)


def per_device(state, probe, norm_gain, head_maps, query_gain, key_gain, out_map, out_gate):
    place = lax.axis_index(SEQ)
    meta = jnp.stack([lax.axis_index("c"), place, lax.axis_index("z")]).astype(jnp.int32)
    gate = lax.dynamic_slice_in_dim(out_gate, place * 128, 128).reshape(1, 128)
    maps = head_maps.reshape(32, 128, 384)
    outs = out_map.reshape(32, 128, 128)
    gain = norm_gain.reshape(32, 1, 128)

    packed_state, packed_probe = call(
        pack_kernel, [shape((4, 8, 3072)), shape((8, 6144))], 0, state, probe
    )
    probe_all = lax.all_gather(packed_probe, SEQ, axis=0, tiled=True)
    _, own = spread(packed_state)
    oth = swap(own)
    att1, col = call(
        first_kernel, [shape((4, TOK, 128)), shape((TOK, 128))],
        1, meta, own, oth, maps, gain, query_gain, key_gain, scratch=HELD,
    )
    _, own1, oth1 = gathered(att1)
    vel1, mid = call(
        middle_kernel, [shape((TOK, 128)), shape((4, TOK, 128))],
        1, meta, own1, oth1, outs, gate, col,
    )
    late_map, mid = lax.optimization_barrier((out_map, mid))
    all_outs = lax.all_gather(late_map, "z", axis=0, tiled=False)
    _, own_m = spread(mid)
    probe_blocks, datt1 = call(
        tangent_kernel, [shape((32, TOK, 128)), shape((TOK, 128), F32)],
        1, meta, own, oth, probe_all, maps, gain, query_gain, key_gain, (mid,), scratch=HELD,
    )
    own_m, datt1 = lax.optimization_barrier((own_m, datt1))
    oth_m = swap(own_m).reshape(16, TOK, 128)
    own_m = own_m.reshape(16, TOK, 128)
    both = call(
        second_kernel, shape((4, 2 * TOK, 128)),
        1, meta, own_m, oth_m, probe_blocks, maps, gain, query_gain, key_gain, datt1,
    )
    own2 = lax.all_to_all(both.reshape(8 * TOK, 128), "y", 0, 0, tiled=True)
    oth2 = swap(own2)
    columns = call(
        last_kernel, shape((256, 512)),
        1, meta, own2.reshape(4, 2 * TOK, 128), oth2.reshape(4, 2 * TOK, 128),
        (all_outs.reshape(4, 32, 128, 128),), out_gate.reshape(32, 1, 128), vel1, probe_blocks,
        scratch=[pltpu.VMEM((4, 8, 128, 128), BF), pltpu.SemaphoreType.DMA],
    )
    got = lax.all_to_all(columns, SEQ, 0, 0, tiled=True).reshape(32, 8, 512)
    next_state, change = call(
        land_kernel, [shape((6, 4096)), shape((1, 128), F32)], 0, got, state
    )
    return next_state, change[0, :1]


def solution(mesh):
    split = Mesh(mesh.devices.reshape(4, 4, 2, 4, 4), ("z", "y", "c", "w", "x"))
    rows = P(("w", "x", "z", "y", "c"), None)
    return jax.shard_map(
        per_device,
        mesh=split,
        in_specs=(rows, rows, P(), P(SEQ, None, None), P(SEQ, None), P(SEQ, None), P(None, SEQ), P()),
        out_specs=(rows, P(("w", "x"))),
        check_vma=False,
    )
```

```python
import jax
import jax.numpy as jnp
from jax import lax
from jax.experimental import pallas as pl
from jax.experimental.pallas import tpu as pltpu
from jax.sharding import Mesh, PartitionSpec as P

EPS = 1e-06
STEP = 0.5
SEQ = ("z", "y", "c")
BF = jnp.bfloat16
F32 = jnp.float32
NT = (((1,), (1,)), ((), ()))
TOK = 192
SCALE = 128 ** (-0.5)


def dot(a, b):
    return jnp.dot(a, b, preferred_element_type=F32)


def dot_nt(a, b):
    return lax.dot_general(a, b, NT, preferred_element_type=F32)


def row_mean(v):
    return jnp.mean(v, axis=-1, keepdims=True)


HELD = [pltpu.VMEM((32, TOK, 128), BF)]


def call(kernel, out_shape, n_scalar, *args, scratch=()):
    in_specs = [pl.BlockSpec(memory_space=pltpu.SMEM)] * n_scalar
    for a in args[n_scalar:]:
        if isinstance(a, tuple):
            in_specs.append(pl.BlockSpec(memory_space=pl.ANY))
        else:
            in_specs.append(pl.BlockSpec(memory_space=pltpu.VMEM))
    flat = [a[0] if isinstance(a, tuple) else a for a in args]
    multi = isinstance(out_shape, (tuple, list))
    vmem = pl.BlockSpec(memory_space=pltpu.VMEM)
    return pl.pallas_call(
        kernel,
        out_shape=out_shape,
        in_specs=in_specs,
        out_specs=[vmem] * len(out_shape) if multi else vmem,
        scratch_shapes=scratch,
        compiler_params=pltpu.CompilerParams(vmem_limit_bytes=20 * 1024 * 1024),
    )(*flat)


def shape(dims, kind=BF):
    return jax.ShapeDtypeStruct(dims, kind)


def selectors(first_row_token, rows):
    packed = lax.broadcasted_iota(jnp.int32, (TOK, rows), 1)
    token = lax.broadcasted_iota(jnp.int32, (TOK, rows), 0)
    slot = packed & 7
    base = first_row_token(packed)
    one = jnp.ones((TOK, rows), F32)
    zero = jnp.zeros((TOK, rows), F32)
    main = jnp.where((token == base + slot) & (slot < 6), one, zero).astype(BF)
    rest = [
        jnp.where((token == base + m + 3 * (slot - 6)) & (slot >= 6), one, zero).astype(BF)
        for m in range(3)
    ]
    return main, rest


def pieces(main, rest, chunk_of):
    tail = None
    for m in range(3):
        chunk = chunk_of(m)
        part = dot(rest[m], chunk)
        tail = part if tail is None else tail + part
        yield m * 1024, dot(main, chunk)
    yield 3072, tail


def qkv_norm(proj, q_gain, k_gain):
    query, key, val = proj[:, :128], proj[:, 128:256], proj[:, 256:]
    rq = lax.rsqrt(row_mean(query * query) + EPS)
    rk = lax.rsqrt(row_mean(key * key) + EPS)
    qn = (query * rq * q_gain).astype(BF)
    kn = (key * rk * k_gain).astype(BF)
    return query, key, rq, rk, qn, kn, val.astype(BF)


def probabilities(qn, kn):
    expo = jnp.exp(dot_nt(qn, kn) * SCALE)
    return expo / jnp.sum(expo, axis=-1, keepdims=True)


def attend(proj, q_gain, k_gain):
    _, _, _, _, qn, kn, val = qkv_norm(proj, q_gain, k_gain)
    return dot(probabilities(qn, kn).astype(BF), val).astype(BF)


def attend_tangent(proj, d_proj, q_gain, k_gain):
    query, key, rq, rk, qn, kn, val = qkv_norm(proj, q_gain, k_gain)
    dq, dk, dv = d_proj[:, :128], d_proj[:, 128:256], d_proj[:, 256:].astype(BF)
    drq = -(rq * rq * rq) * row_mean(query * dq)
    drk = -(rk * rk * rk) * row_mean(key * dk)
    dqn = ((dq * rq + query * drq) * q_gain).astype(BF)
    dkn = ((dk * rk + key * drk) * k_gain).astype(BF)
    probs = probabilities(qn, kn)
    ds = (dot_nt(dqn, kn) + dot_nt(qn, dkn)) * SCALE
    d_probs = probs * (ds - jnp.sum(probs * ds, axis=-1, keepdims=True))
    probs = probs.astype(BF)
    return dot(probs, val).astype(BF), dot(d_probs.astype(BF), val) + dot(probs, dv)


def pack_kernel(state, probe, state_ref, probe_ref):
    for source, write in ((state, None), (probe, probe_ref)):
        main = source[:, :3072]
        sixth = jnp.concatenate([source[q : q + 1, 3072:] for q in range(3)], axis=1)
        seventh = jnp.concatenate([source[q : q + 1, 3072:] for q in range(3, 6)], axis=1)
        whole = jnp.concatenate([main, sixth, seventh], axis=0)
        if write is None:
            for i in range(4):
                state_ref[i] = whole
        else:
            write[:, :3072] = whole
            write[:, 3072:] = whole


def core_order(core):
    def first_token(packed):
        inner = packed & 127
        z = (inner >> 3) & 3
        y = inner >> 5
        c = jnp.where((packed >> 7) == 0, core, 1 - core)
        return (z * 8 + y * 2 + c) * 6

    return first_token


def unpack_state(core, xa, xb, held):
    main, rest = selectors(core_order(core), 256)
    squares = jnp.zeros((TOK, 128), F32)

    def chunk_of(m):
        cols = slice(m * 1024, (m + 1) * 1024)
        return jnp.concatenate([xa[:, cols], xb[:, cols]], axis=0)

    for start, x in pieces(main, rest, chunk_of):
        for b in range(8):
            piece = x[:, b * 128 : (b + 1) * 128]
            squares = squares + piece * piece
            held[start // 128 + b] = piece.astype(BF)
    return lax.rsqrt(row_sum(squares) * (1.0 / 4096) + EPS)


def row_sum(v):
    return jnp.sum(v, axis=-1, keepdims=True)


def first_kernel(meta, xa, xb, maps, gain, q_gain, k_gain, att_ref, col_ref, held):
    recip = unpack_state(meta[0], xa, xb, held)
    proj = jnp.zeros((TOK, 384), F32)
    for h in range(0, 32, 2):
        left = (held[h].astype(F32) * recip * gain[h]).astype(BF)
        right = (held[h + 1].astype(F32) * recip * gain[h + 1]).astype(BF)
        rows = jnp.concatenate([maps[h], maps[h + 1]], axis=0)
        proj = proj + dot(jnp.concatenate([left, right], axis=1), rows)
    att = attend(proj, q_gain[...], k_gain[...])
    for i in range(4):
        att_ref[i] = att
    col_ref[...] = held[meta[1]]


def blocks(core, own, oth):
    for side, c in ((own, core), (oth, 1 - core)):
        for y in range(4):
            for z in (0, 2):
                yield side, y * 4 + z, z * 8 + y * 2 + c


def out_product(core, own, oth, out_map):
    total = jnp.zeros((own.shape[1], 128), F32)
    for side, b, h in blocks(core, own, oth):
        left = jnp.concatenate([side[b], side[b + 1]], axis=1)
        right = jnp.concatenate([out_map[h], out_map[h + 8]], axis=0)
        total = total + dot(left, right)
    return total


def middle_kernel(meta, own, oth, out_map, gate, col, vel_ref, mid_ref):
    vel = (gate[...] * out_product(meta[0], own, oth, out_map)).astype(BF)
    vel_ref[...] = vel
    mid = (col[...].astype(F32) + STEP * vel.astype(F32)).astype(BF)
    for i in range(4):
        mid_ref[i] = mid


def both_rows(x, probe, recip, d_recip, gain):
    normed = (x * recip * gain).astype(BF)
    d_normed = ((probe * recip + x * d_recip) * gain).astype(BF)
    return jnp.concatenate([normed, d_normed], axis=0)


def tangent_kernel(
    meta, xa, xb, packed, maps, gain, q_gain, k_gain, after, probe_ref, datt_ref, held
):
    recip = unpack_state(meta[0], xa, xb, held)
    main, rest = selectors(lambda row: (row >> 3) * 6, 256)
    dots = jnp.zeros((TOK, 128), F32)
    for start, x in pieces(main, rest, lambda m: packed[:, m * 1024 : (m + 1) * 1024]):
        for b in range(8):
            piece = x[:, b * 128 : (b + 1) * 128]
            dots = dots + piece * held[start // 128 + b].astype(F32)
            probe_ref[start // 128 + b] = piece.astype(BF)
    d_recip = -(recip * recip * recip) * (row_sum(dots) * (1.0 / 4096))
    proj = jnp.zeros((2 * TOK, 384), F32)
    for h in range(0, 32, 2):
        pair = [
            both_rows(held[i].astype(F32), probe_ref[i].astype(F32), recip, d_recip, gain[i])
            for i in (h, h + 1)
        ]
        rows = jnp.concatenate([maps[h], maps[h + 1]], axis=0)
        proj = proj + dot(jnp.concatenate(pair, axis=1), rows)
    datt_ref[...] = attend_tangent(proj[:TOK], proj[TOK:], q_gain[...], k_gain[...])[1]


def second_kernel(meta, own, oth, probe, maps, gain, q_gain, k_gain, datt1, both_ref):
    core = meta[0]
    squares = jnp.zeros((TOK, 128), F32)
    dots = jnp.zeros((TOK, 128), F32)
    for side, b, h in blocks(core, own, oth):
        for i in range(2):
            x = side[b + i].astype(F32)
            squares = squares + x * x
            dots = dots + x * probe[h + 8 * i].astype(F32)
    recip = lax.rsqrt(row_sum(squares) * (1.0 / 4096) + EPS)
    d_recip = -(recip * recip * recip) * (row_sum(dots) * (1.0 / 4096))
    proj = jnp.zeros((2 * TOK, 384), F32)
    for side, b, h in blocks(core, own, oth):
        pair = [
            both_rows(
                side[b + i].astype(F32), probe[h + 8 * i].astype(F32), recip, d_recip, gain[h + 8 * i]
            )
            for i in range(2)
        ]
        rows = jnp.concatenate([maps[h], maps[h + 8]], axis=0)
        proj = proj + dot(jnp.concatenate(pair, axis=1), rows)
    att, d_att = attend_tangent(proj[:TOK], proj[TOK:], q_gain[...], k_gain[...])
    d_both = (d_att + datt1[...]).astype(BF)
    for i in range(4):
        both_ref[i, :TOK] = att
        both_ref[i, TOK:] = d_both


def last_kernel(meta, own, oth, rows, gates, vel1, probe, out_ref):
    core, plane, slab = meta[0], meta[2], meta[3]
    row = lax.broadcasted_iota(jnp.int32, (256, TOK), 0)
    token = lax.broadcasted_iota(jnp.int32, (256, TOK), 1)
    hit = (token == (row >> 3) * 6 + (row & 7)) & ((row & 7) < 6)
    lay = jnp.where(hit, jnp.ones((256, TOK), F32), jnp.zeros((256, TOK), F32)).astype(BF)
    left = []
    for z in range(4):
        mine, other = own[z], oth[z]
        first = jnp.where(core == 0, mine, other)
        second = jnp.where(core == 0, other, mine)
        left.append(jnp.concatenate([first, second], axis=1))
    trace = jnp.zeros((1, 128), F32)
    laid = []
    for y in range(4):
        mapped = jnp.zeros((2 * TOK, 128), F32)
        for z in range(4):
            right = jnp.concatenate([rows[y, z * 2], rows[y, z * 2 + 1]], axis=0)
            mapped = mapped + dot(left[z], right)
        column = slab * 8 + y * 2 + core
        mapped = mapped * gates[column]
        terms = mapped[TOK:] * probe[column].astype(F32)
        trace = trace + jnp.sum(terms, axis=0, keepdims=True)
        vel = vel1[...].astype(F32)
        part = mapped[:TOK] + jnp.where(plane == y, vel, jnp.zeros_like(vel))
        laid.append(dot(lay, part.astype(BF)))
    trace = row_sum(trace)
    high = trace.astype(BF).astype(F32)
    mid = (trace - high).astype(BF).astype(F32)
    low = trace - high - mid
    lane = lax.broadcasted_iota(jnp.int32, (1, 128), 1)
    coded = jnp.where(lane == 0, high, jnp.where(lane == 1, mid, jnp.where(lane == 2, low, 0.0)))
    slot = lax.broadcasted_iota(jnp.int32, (256, 128), 0) & 7
    for y in range(4):
        block = jnp.where(slot == 6, coded, laid[y]) if y == 0 else laid[y]
        out_ref[:, y * 128 : (y + 1) * 128] = block.astype(BF)


def land_kernel(got, state, next_ref, change_ref):
    total = jnp.zeros((8, 128), F32)
    for z in range(4):
        for c in range(2):
            sums = jnp.zeros((8, 512), F32)
            for y in range(4):
                block = got[z * 8 + y * 2 + c].astype(F32)
                total = total + block[:, :128]
                sums = sums + block
            for y in range(4):
                j = z * 8 + y * 2 + c
                cols = slice(j * 128, (j + 1) * 128)
                both = sums[:6, y * 128 : (y + 1) * 128]
                next_ref[:, cols] = (state[:, cols].astype(F32) + 0.5 * STEP * both).astype(BF)
    change_ref[...] = jnp.broadcast_to(-0.5 * STEP * row_sum(total[6:7, :]) / TOK, (1, 128))


def spread(copies):
    n, rows, lanes = copies.shape
    a = lax.all_to_all(copies.reshape(n * rows, lanes), "z", 0, 0, tiled=True)
    return a, lax.all_to_all(jnp.tile(a, (4, 1)), "y", 0, 0, tiled=True)


def swap(block):
    return lax.ppermute(block, "c", [(0, 1), (1, 0)])


def gathered(copies):
    rows = copies.shape[1]
    early, own = spread(copies)
    other = swap(own)
    return early, own.reshape(16, rows, 128), other.reshape(16, rows, 128)


def per_device(state, probe, norm_gain, head_maps, query_gain, key_gain, out_map, out_gate):
    place = lax.axis_index(SEQ)
    meta = [lax.axis_index("c"), place, lax.axis_index("y"), lax.axis_index("z")]
    meta = jnp.stack(meta).astype(jnp.int32)
    gate = lax.dynamic_slice_in_dim(out_gate, place * 128, 128).reshape(1, 128)
    maps = head_maps.reshape(32, 128, 384)
    outs = out_map.reshape(32, 128, 128)
    gain = norm_gain.reshape(32, 1, 128)

    packed_state, packed_probe = call(
        pack_kernel, [shape((4, 8, 3072)), shape((8, 6144))], 0, state, probe
    )
    probe_all = lax.all_gather(packed_probe, SEQ, axis=0, tiled=True)
    _, own = spread(packed_state)
    oth = swap(own)
    att1, col = call(
        first_kernel, [shape((4, TOK, 128)), shape((TOK, 128))],
        1, meta, own, oth, maps, gain, query_gain, key_gain, scratch=HELD,
    )
    _, own1, oth1 = gathered(att1)
    vel1, mid = call(
        middle_kernel, [shape((TOK, 128)), shape((4, TOK, 128))],
        1, meta, own1, oth1, outs, gate, col,
    )
    _, own_m = spread(mid)
    late_map, own_m = lax.optimization_barrier((out_map, own_m))
    by_plane = late_map.reshape(4, 4, 256, 128).transpose(1, 0, 2, 3).reshape(4096, 128)
    plane_outs = lax.all_to_all(by_plane, "y", 0, 0, tiled=True)
    probe_blocks, datt1 = call(
        tangent_kernel, [shape((32, TOK, 128)), shape((TOK, 128), F32)],
        1, meta, own, oth, probe_all, maps, gain, query_gain, key_gain, (mid,), scratch=HELD,
    )
    oth_m = swap(own_m).reshape(16, TOK, 128)
    own_m = own_m.reshape(16, TOK, 128)
    both = call(
        second_kernel, shape((4, 2 * TOK, 128)),
        1, meta, own_m, oth_m, probe_blocks, maps, gain, query_gain, key_gain, datt1,
    )
    both, plane_outs = lax.optimization_barrier((both, plane_outs))
    own2 = lax.all_to_all(both.reshape(8 * TOK, 128), "z", 0, 0, tiled=True)
    oth2 = swap(own2)
    columns = call(
        last_kernel, shape((256, 512)),
        1, meta, own2.reshape(4, 2 * TOK, 128), oth2.reshape(4, 2 * TOK, 128),
        plane_outs.reshape(4, 8, 128, 128), out_gate.reshape(32, 1, 128), vel1, probe_blocks,
    )
    got = lax.all_to_all(columns, SEQ, 0, 0, tiled=True).reshape(32, 8, 512)
    next_state, change = call(
        land_kernel, [shape((6, 4096)), shape((1, 128), F32)], 0, got, state
    )
    return next_state, change[0, :1]


def solution(mesh):
    split = Mesh(mesh.devices.reshape(4, 4, 2, 4, 4), ("z", "y", "c", "w", "x"))
    rows = P(("w", "x", "z", "y", "c"), None)
    return jax.shard_map(
        per_device,
        mesh=split,
        in_specs=(rows, rows, P(), P(SEQ, None, None), P(SEQ, None), P(SEQ, None), P(None, SEQ), P()),
        out_specs=(rows, P(("w", "x"))),
        check_vma=False,
    )
```

```python
import jax
import jax.numpy as jnp
from jax import lax
from jax.experimental import pallas as pl
from jax.experimental.pallas import tpu as pltpu
from jax.sharding import Mesh, PartitionSpec as P

EPS = 1e-06
STEP = 0.5
SEQ = ("z", "y", "c")
BF = jnp.bfloat16
F32 = jnp.float32
NT = (((1,), (1,)), ((), ()))
TOK = 192
SCALE = 128 ** (-0.5)


def dot(a, b):
    return jnp.dot(a, b, preferred_element_type=F32)


def dot_nt(a, b):
    return lax.dot_general(a, b, NT, preferred_element_type=F32)


def row_mean(v):
    return jnp.mean(v, axis=-1, keepdims=True)


HELD = pltpu.VMEM((32, TOK, 128), BF)
MAPS = pltpu.VMEM((32, 128, 384), BF)


FULL = 60
LAST = 51
MIDDLE = 51
SECOND = 51


def sems(n):
    return pltpu.SemaphoreType.DMA((n,))


def fetch(sem, *pairs):
    copies = [pltpu.make_async_copy(a, b, sem.at[i]) for i, (a, b) in enumerate(pairs)]
    for copy in copies:
        copy.start()
    return copies


def call(kernel, out_shape, n_scalar, *args, scratch=(), vmem_mib=20):
    in_specs = [pl.BlockSpec(memory_space=pltpu.SMEM)] * n_scalar
    for a in args[n_scalar:]:
        if isinstance(a, tuple):
            in_specs.append(pl.BlockSpec(memory_space=pltpu.HBM))
        else:
            in_specs.append(pl.BlockSpec(memory_space=pltpu.VMEM))
    flat = [a[0] if isinstance(a, tuple) else a for a in args]
    multi = isinstance(out_shape, (tuple, list))
    vmem = pl.BlockSpec(memory_space=pltpu.VMEM)
    return pl.pallas_call(
        kernel,
        out_shape=out_shape,
        in_specs=in_specs,
        out_specs=[vmem] * len(out_shape) if multi else vmem,
        scratch_shapes=scratch,
        compiler_params=pltpu.CompilerParams(vmem_limit_bytes=vmem_mib * 1024 * 1024),
    )(*flat)


def shape(dims, kind=BF):
    return jax.ShapeDtypeStruct(dims, kind)


def selectors(first_row_token, rows):
    packed = lax.broadcasted_iota(jnp.int32, (TOK, rows), 1)
    token = lax.broadcasted_iota(jnp.int32, (TOK, rows), 0)
    slot = packed & 7
    base = first_row_token(packed)
    one = jnp.ones((TOK, rows), F32)
    zero = jnp.zeros((TOK, rows), F32)
    main = jnp.where((token == base + slot) & (slot < 6), one, zero).astype(BF)
    rest = [
        jnp.where((token == base + m + 3 * (slot - 6)) & (slot >= 6), one, zero).astype(BF)
        for m in range(3)
    ]
    return main, rest


def pieces(main, rest, chunk_of):
    tail = None
    for m in range(3):
        chunk = chunk_of(m)
        part = dot(rest[m], chunk)
        tail = part if tail is None else tail + part
        yield m * 1024, dot(main, chunk)
    yield 3072, tail


def qkv_norm(proj, q_gain, k_gain):
    query, key, val = proj[:, :128], proj[:, 128:256], proj[:, 256:]
    rq = lax.rsqrt(row_mean(query * query) + EPS)
    rk = lax.rsqrt(row_mean(key * key) + EPS)
    qn = (query * rq * q_gain).astype(BF)
    kn = (key * rk * k_gain).astype(BF)
    return query, key, rq, rk, qn, kn, val.astype(BF)


def probabilities(qn, kn):
    expo = jnp.exp(dot_nt(qn, kn) * SCALE)
    return expo / jnp.sum(expo, axis=-1, keepdims=True)


def attend(proj, q_gain, k_gain):
    _, _, _, _, qn, kn, val = qkv_norm(proj, q_gain, k_gain)
    return dot(probabilities(qn, kn).astype(BF), val).astype(BF)


def attend_tangent(proj, d_proj, q_gain, k_gain):
    query, key, rq, rk, qn, kn, val = qkv_norm(proj, q_gain, k_gain)
    dq, dk, dv = d_proj[:, :128], d_proj[:, 128:256], d_proj[:, 256:].astype(BF)
    drq = -(rq * rq * rq) * row_mean(query * dq)
    drk = -(rk * rk * rk) * row_mean(key * dk)
    dqn = ((dq * rq + query * drq) * q_gain).astype(BF)
    dkn = ((dk * rk + key * drk) * k_gain).astype(BF)
    probs = probabilities(qn, kn)
    ds = (dot_nt(dqn, kn) + dot_nt(qn, dkn)) * SCALE
    d_probs = probs * (ds - jnp.sum(probs * ds, axis=-1, keepdims=True))
    probs = probs.astype(BF)
    return dot(probs, val).astype(BF), dot(d_probs.astype(BF), val) + dot(probs, dv)


def pack_kernel(state_hbm, probe_hbm, state_ref, probe_ref, state, probe, sem):
    copies = fetch(sem, (state_hbm, state), (probe_hbm, probe))
    for i, (source, write) in enumerate(((state, None), (probe, probe_ref))):
        copies[i].wait()
        main = source[:, :3072]
        sixth = jnp.concatenate([source[q : q + 1, 3072:] for q in range(3)], axis=1)
        seventh = jnp.concatenate([source[q : q + 1, 3072:] for q in range(3, 6)], axis=1)
        whole = jnp.concatenate([main, sixth, seventh], axis=0)
        if write is None:
            for n in range(4):
                state_ref[n] = whole
        else:
            write[:, :3072] = whole
            write[:, 3072:] = whole


def core_order(core):
    def first_token(packed):
        inner = packed & 127
        z = (inner >> 3) & 3
        y = inner >> 5
        c = jnp.where((packed >> 7) == 0, core, 1 - core)
        return (z * 8 + y * 2 + c) * 6

    return first_token


def unpack_state(core, xa, xb, held):
    main, rest = selectors(core_order(core), 256)
    squares = jnp.zeros((TOK, 128), F32)

    def chunk_of(m):
        cols = slice(m * 1024, (m + 1) * 1024)
        return jnp.concatenate([xa[:, cols], xb[:, cols]], axis=0)

    for start, x in pieces(main, rest, chunk_of):
        for b in range(8):
            piece = x[:, b * 128 : (b + 1) * 128]
            squares = squares + piece * piece
            held[start // 128 + b] = piece.astype(BF)
    return lax.rsqrt(row_sum(squares) * (1.0 / 4096) + EPS)


def row_sum(v):
    return jnp.sum(v, axis=-1, keepdims=True)


def first_kernel(
    meta, xa, xb, maps_hbm, gain, q_gain, k_gain, att_ref, col_ref, held, maps, sem
):
    copies = fetch(sem, (maps_hbm, maps))
    recip = unpack_state(meta[0], xa, xb, held)
    copies[0].wait()
    proj = jnp.zeros((TOK, 384), F32)
    for h in range(0, 32, 2):
        left = (held[h].astype(F32) * recip * gain[h]).astype(BF)
        right = (held[h + 1].astype(F32) * recip * gain[h + 1]).astype(BF)
        rows = jnp.concatenate([maps[h], maps[h + 1]], axis=0)
        proj = proj + dot(jnp.concatenate([left, right], axis=1), rows)
    att = attend(proj, q_gain[...], k_gain[...])
    for i in range(4):
        att_ref[i] = att
    col_ref[...] = held[meta[1]]


def blocks(core, own, oth):
    for side, c in ((own, core), (oth, 1 - core)):
        for y in range(4):
            for z in (0, 2):
                yield side, y * 4 + z, z * 8 + y * 2 + c


def out_product(core, own, oth, out_map):
    total = jnp.zeros((own.shape[1], 128), F32)
    for side, b, h in blocks(core, own, oth):
        left = jnp.concatenate([side[b], side[b + 1]], axis=1)
        right = jnp.concatenate([out_map[h], out_map[h + 8]], axis=0)
        total = total + dot(left, right)
    return total


def middle_kernel(meta, own, oth, out_hbm, gates, col, vel_ref, mid_ref, out_map, sem):
    copies = fetch(sem, (out_hbm, out_map))
    gate = gates[meta[1]]
    copies[0].wait()
    vel = (gate * out_product(meta[0], own, oth, out_map)).astype(BF)
    vel_ref[...] = vel
    mid = (col[...].astype(F32) + STEP * vel.astype(F32)).astype(BF)
    for i in range(4):
        mid_ref[i] = mid


def both_rows(x, probe, recip, d_recip, gain):
    normed = (x * recip * gain).astype(BF)
    d_normed = ((probe * recip + x * d_recip) * gain).astype(BF)
    return jnp.concatenate([normed, d_normed], axis=0)


def tangent_kernel(
    meta, xa_hbm, xb_hbm, packed_hbm, maps_hbm, gain, q_gain, k_gain, after, probe_ref, datt_ref,
    held, xa, xb, packed, maps, sem,
):
    copies = fetch(
        sem, (xa_hbm, xa), (xb_hbm, xb), (packed_hbm.at[:, :3072], packed), (maps_hbm, maps)
    )
    copies[0].wait()
    copies[1].wait()
    recip = unpack_state(meta[0], xa, xb, held)
    main, rest = selectors(lambda row: (row >> 3) * 6, 256)
    copies[2].wait()
    dots = jnp.zeros((TOK, 128), F32)
    for start, x in pieces(main, rest, lambda m: packed[:, m * 1024 : (m + 1) * 1024]):
        for b in range(8):
            piece = x[:, b * 128 : (b + 1) * 128]
            dots = dots + piece * held[start // 128 + b].astype(F32)
            probe_ref[start // 128 + b] = piece.astype(BF)
    d_recip = -(recip * recip * recip) * (row_sum(dots) * (1.0 / 4096))
    copies[3].wait()
    proj = jnp.zeros((2 * TOK, 384), F32)
    for h in range(0, 32, 2):
        pair = [
            both_rows(held[i].astype(F32), probe_ref[i].astype(F32), recip, d_recip, gain[i])
            for i in (h, h + 1)
        ]
        rows = jnp.concatenate([maps[h], maps[h + 1]], axis=0)
        proj = proj + dot(jnp.concatenate(pair, axis=1), rows)
    datt_ref[...] = attend_tangent(proj[:TOK], proj[TOK:], q_gain[...], k_gain[...])[1]


def second_kernel(
    meta, own, oth, probe, maps_hbm, gain, q_gain, k_gain, datt1, both_ref, maps, sem
):
    core = meta[0]
    copies = fetch(sem, (maps_hbm, maps))
    squares = jnp.zeros((TOK, 128), F32)
    dots = jnp.zeros((TOK, 128), F32)
    for side, b, h in blocks(core, own, oth):
        for i in range(2):
            x = side[b + i].astype(F32)
            squares = squares + x * x
            dots = dots + x * probe[h + 8 * i].astype(F32)
    recip = lax.rsqrt(row_sum(squares) * (1.0 / 4096) + EPS)
    d_recip = -(recip * recip * recip) * (row_sum(dots) * (1.0 / 4096))
    copies[0].wait()
    proj = jnp.zeros((2 * TOK, 384), F32)
    for side, b, h in blocks(core, own, oth):
        pair = [
            both_rows(
                side[b + i].astype(F32), probe[h + 8 * i].astype(F32), recip, d_recip, gain[h + 8 * i]
            )
            for i in range(2)
        ]
        rows = jnp.concatenate([maps[h], maps[h + 8]], axis=0)
        proj = proj + dot(jnp.concatenate(pair, axis=1), rows)
    att, d_att = attend_tangent(proj[:TOK], proj[TOK:], q_gain[...], k_gain[...])
    d_both = (d_att + datt1[...]).astype(BF)
    for i in range(4):
        both_ref[i, :TOK] = att
        both_ref[i, TOK:] = d_both


def last_kernel(meta, own, oth, rows_hbm, gates, vel_hbm, probe_hbm, out_ref, rows, vel1, probe, sem):
    core, plane, slab = meta[0], meta[2], meta[3]
    columns = [(probe_hbm.at[slab * 8 + y * 2 + core], probe.at[y]) for y in range(4)]
    copies = fetch(sem, (rows_hbm, rows), (vel_hbm, vel1), *columns)
    row = lax.broadcasted_iota(jnp.int32, (256, TOK), 0)
    token = lax.broadcasted_iota(jnp.int32, (256, TOK), 1)
    hit = (token == (row >> 3) * 6 + (row & 7)) & ((row & 7) < 6)
    lay = jnp.where(hit, jnp.ones((256, TOK), F32), jnp.zeros((256, TOK), F32)).astype(BF)
    left = []
    for z in range(4):
        mine, other = own[z], oth[z]
        first = jnp.where(core == 0, mine, other)
        second = jnp.where(core == 0, other, mine)
        left.append(jnp.concatenate([first, second], axis=1))
    for copy in copies:
        copy.wait()
    trace = jnp.zeros((1, 128), F32)
    laid = []
    for y in range(4):
        mapped = jnp.zeros((2 * TOK, 128), F32)
        for z in range(4):
            right = jnp.concatenate([rows[y, z * 2], rows[y, z * 2 + 1]], axis=0)
            mapped = mapped + dot(left[z], right)
        column = slab * 8 + y * 2 + core
        mapped = mapped * gates[column]
        terms = mapped[TOK:] * probe[y].astype(F32)
        trace = trace + jnp.sum(terms, axis=0, keepdims=True)
        vel = vel1[...].astype(F32)
        part = mapped[:TOK] + jnp.where(plane == y, vel, jnp.zeros_like(vel))
        laid.append(dot(lay, part.astype(BF)))
    trace = row_sum(trace)
    high = trace.astype(BF).astype(F32)
    mid = (trace - high).astype(BF).astype(F32)
    low = trace - high - mid
    lane = lax.broadcasted_iota(jnp.int32, (1, 128), 1)
    coded = jnp.where(lane == 0, high, jnp.where(lane == 1, mid, jnp.where(lane == 2, low, 0.0)))
    slot = lax.broadcasted_iota(jnp.int32, (256, 128), 0) & 7
    for y in range(4):
        block = jnp.where(slot == 6, coded, laid[y]) if y == 0 else laid[y]
        out_ref[:, y * 128 : (y + 1) * 128] = block.astype(BF)


def land_kernel(got, state, next_ref, change_ref):
    total = jnp.zeros((8, 128), F32)
    for z in range(4):
        for c in range(2):
            sums = jnp.zeros((8, 512), F32)
            for y in range(4):
                block = got[z * 8 + y * 2 + c].astype(F32)
                total = total + block[:, :128]
                sums = sums + block
            for y in range(4):
                j = z * 8 + y * 2 + c
                cols = slice(j * 128, (j + 1) * 128)
                both = sums[:6, y * 128 : (y + 1) * 128]
                next_ref[:, cols] = (state[:, cols].astype(F32) + 0.5 * STEP * both).astype(BF)
    change_ref[...] = jnp.broadcast_to(-0.5 * STEP * row_sum(total[6:7, :]) / TOK, (1, 128))


def spread(copies):
    n, rows, lanes = copies.shape
    a = lax.all_to_all(copies.reshape(n * rows, lanes), "z", 0, 0, tiled=True)
    return a, lax.all_to_all(jnp.tile(a, (4, 1)), "y", 0, 0, tiled=True)


def swap(block):
    return lax.ppermute(block, "c", [(0, 1), (1, 0)])


def gathered(copies):
    rows = copies.shape[1]
    early, own = spread(copies)
    other = swap(own)
    return early, own.reshape(16, rows, 128), other.reshape(16, rows, 128)


def per_device(state, probe, norm_gain, head_maps, query_gain, key_gain, out_map, out_gate):
    place = lax.axis_index(SEQ)
    meta = [lax.axis_index("c"), place, lax.axis_index("y"), lax.axis_index("z")]
    meta = jnp.stack(meta).astype(jnp.int32)
    gates = out_gate.reshape(32, 1, 128)
    maps = head_maps.reshape(32, 128, 384)
    outs = out_map.reshape(32, 128, 128)
    gain = norm_gain.reshape(32, 1, 128)

    packed_state, packed_probe = call(
        pack_kernel, [shape((4, 8, 3072)), shape((8, 6144))], 0, (state,), (probe,),
        scratch=[pltpu.VMEM((6, 4096), BF), pltpu.VMEM((6, 4096), BF), sems(2)], vmem_mib=FULL,
    )
    probe_all = lax.all_gather(packed_probe, SEQ, axis=0, tiled=True)
    _, own = spread(packed_state)
    oth = swap(own)
    att1, col = call(
        first_kernel, [shape((4, TOK, 128)), shape((TOK, 128))],
        1, meta, own, oth, (maps,), gain, query_gain, key_gain, scratch=[HELD, MAPS, sems(1)],
    )
    _, own1, oth1 = gathered(att1)
    vel1, mid = call(
        middle_kernel, [shape((TOK, 128)), shape((4, TOK, 128))],
        1, meta, own1, oth1, (outs,), gates, col,
        scratch=[pltpu.VMEM((32, 128, 128), BF), sems(1)], vmem_mib=MIDDLE,
    )
    _, own_m = spread(mid)
    late_map, own_m = lax.optimization_barrier((out_map, own_m))
    by_plane = late_map.reshape(4, 4, 256, 128).transpose(1, 0, 2, 3).reshape(4096, 128)
    plane_outs = lax.all_to_all(by_plane, "y", 0, 0, tiled=True)
    probe_blocks, datt1 = call(
        tangent_kernel, [shape((32, TOK, 128)), shape((TOK, 128), F32)],
        1, meta, (own,), (oth,), (probe_all,), (maps,), gain, query_gain, key_gain, (mid,),
        scratch=[
            HELD, pltpu.VMEM((128, 3072), BF), pltpu.VMEM((128, 3072), BF),
            pltpu.VMEM((256, 3072), BF), MAPS, sems(4),
        ],
        vmem_mib=FULL,
    )
    oth_m = swap(own_m).reshape(16, TOK, 128)
    own_m = own_m.reshape(16, TOK, 128)
    both = call(
        second_kernel, shape((4, 2 * TOK, 128)),
        1, meta, own_m, oth_m, probe_blocks, (maps,), gain, query_gain, key_gain, datt1,
        scratch=[MAPS, sems(1)], vmem_mib=SECOND,
    )
    both, plane_outs = lax.optimization_barrier((both, plane_outs))
    own2 = lax.all_to_all(both.reshape(8 * TOK, 128), "z", 0, 0, tiled=True)
    oth2 = swap(own2)
    columns = call(
        last_kernel, shape((256, 512)),
        1, meta, own2.reshape(4, 2 * TOK, 128), oth2.reshape(4, 2 * TOK, 128),
        (plane_outs.reshape(4, 8, 128, 128),), gates, (vel1,), (probe_blocks,),
        scratch=[
            pltpu.VMEM((4, 8, 128, 128), BF), pltpu.VMEM((TOK, 128), BF),
            pltpu.VMEM((4, TOK, 128), BF), sems(6),
        ],
        vmem_mib=LAST,
    )
    got = lax.all_to_all(columns, SEQ, 0, 0, tiled=True).reshape(32, 8, 512)
    next_state, change = call(
        land_kernel, [shape((6, 4096)), shape((1, 128), F32)], 0, got, state
    )
    return next_state, change[0, :1]


def solution(mesh):
    split = Mesh(mesh.devices.reshape(4, 4, 2, 4, 4), ("z", "y", "c", "w", "x"))
    rows = P(("w", "x", "z", "y", "c"), None)
    return jax.shard_map(
        per_device,
        mesh=split,
        in_specs=(rows, rows, P(), P(SEQ, None, None), P(SEQ, None), P(SEQ, None), P(None, SEQ), P()),
        out_specs=(rows, P(("w", "x"))),
        check_vma=False,
    )
```

```python
import jax
import jax.numpy as jnp
from jax import lax
from jax.experimental import pallas as pl
from jax.experimental.pallas import tpu as pltpu
from jax.sharding import Mesh, PartitionSpec as P

EPS = 1e-06
STEP = 0.5
SEQ = ("z", "y", "c")
BF = jnp.bfloat16
F32 = jnp.float32
NT = (((1,), (1,)), ((), ()))
TOK = 192
SCALE = 128 ** (-0.5)


def dot(a, b):
    return jnp.dot(a, b, preferred_element_type=F32)


def dot_nt(a, b):
    return lax.dot_general(a, b, NT, preferred_element_type=F32)


def row_mean(v):
    return jnp.mean(v, axis=-1, keepdims=True)


HELD = pltpu.VMEM((32, TOK, 128), BF)
MAPS = pltpu.VMEM((32, 128, 384), BF)
ROWS = pltpu.VMEM((4, 8, 128, 128), BF)


FULL = 60
LAST = 51
MIDDLE = 51
SECOND = 51


def sems(n):
    return pltpu.SemaphoreType.DMA((n,))


def fetch(sem, *pairs):
    copies = [pltpu.make_async_copy(a, b, sem.at[i]) for i, (a, b) in enumerate(pairs)]
    for copy in copies:
        copy.start()
    return copies


def call(kernel, out_shape, n_scalar, *args, scratch=(), vmem_mib=20):
    in_specs = [pl.BlockSpec(memory_space=pltpu.SMEM)] * n_scalar
    for a in args[n_scalar:]:
        if isinstance(a, tuple):
            in_specs.append(pl.BlockSpec(memory_space=pltpu.HBM))
        else:
            in_specs.append(pl.BlockSpec(memory_space=pltpu.VMEM))
    flat = [a[0] if isinstance(a, tuple) else a for a in args]
    multi = isinstance(out_shape, (tuple, list))
    vmem = pl.BlockSpec(memory_space=pltpu.VMEM)
    return pl.pallas_call(
        kernel,
        out_shape=out_shape,
        in_specs=in_specs,
        out_specs=[vmem] * len(out_shape) if multi else vmem,
        scratch_shapes=scratch,
        compiler_params=pltpu.CompilerParams(vmem_limit_bytes=vmem_mib * 1024 * 1024),
    )(*flat)


def shape(dims, kind=BF):
    return jax.ShapeDtypeStruct(dims, kind)


def selectors(first_row_token, rows):
    packed = lax.broadcasted_iota(jnp.int32, (TOK, rows), 1)
    token = lax.broadcasted_iota(jnp.int32, (TOK, rows), 0)
    slot = packed & 7
    base = first_row_token(packed)
    one = jnp.ones((TOK, rows), F32)
    zero = jnp.zeros((TOK, rows), F32)
    main = jnp.where((token == base + slot) & (slot < 6), one, zero).astype(BF)
    rest = [
        jnp.where((token == base + m + 3 * (slot - 6)) & (slot >= 6), one, zero).astype(BF)
        for m in range(3)
    ]
    return main, rest


def pieces(main, rest, chunk_of):
    tail = None
    for m in range(3):
        chunk = chunk_of(m)
        part = dot(rest[m], chunk)
        tail = part if tail is None else tail + part
        yield m * 1024, dot(main, chunk)
    yield 3072, tail


def qkv_norm(proj, q_gain, k_gain):
    query, key, val = proj[:, :128], proj[:, 128:256], proj[:, 256:]
    rq = lax.rsqrt(row_mean(query * query) + EPS)
    rk = lax.rsqrt(row_mean(key * key) + EPS)
    qn = (query * rq * q_gain).astype(BF)
    kn = (key * rk * k_gain).astype(BF)
    return query, key, rq, rk, qn, kn, val.astype(BF)


def probabilities(qn, kn):
    expo = jnp.exp(dot_nt(qn, kn) * SCALE)
    return expo / jnp.sum(expo, axis=-1, keepdims=True)


def attend(proj, q_gain, k_gain):
    _, _, _, _, qn, kn, val = qkv_norm(proj, q_gain, k_gain)
    return dot(probabilities(qn, kn).astype(BF), val).astype(BF)


def attend_tangent(proj, d_proj, q_gain, k_gain):
    query, key, rq, rk, qn, kn, val = qkv_norm(proj, q_gain, k_gain)
    dq, dk, dv = d_proj[:, :128], d_proj[:, 128:256], d_proj[:, 256:].astype(BF)
    drq = -(rq * rq * rq) * row_mean(query * dq)
    drk = -(rk * rk * rk) * row_mean(key * dk)
    dqn = ((dq * rq + query * drq) * q_gain).astype(BF)
    dkn = ((dk * rk + key * drk) * k_gain).astype(BF)
    probs = probabilities(qn, kn)
    ds = (dot_nt(dqn, kn) + dot_nt(qn, dkn)) * SCALE
    d_probs = probs * (ds - jnp.sum(probs * ds, axis=-1, keepdims=True))
    probs = probs.astype(BF)
    return dot(probs, val).astype(BF), dot(d_probs.astype(BF), val) + dot(probs, dv)


def pack_kernel(state_hbm, probe_hbm, state_ref, probe_ref, state, probe, sem):
    copies = fetch(sem, (state_hbm, state), (probe_hbm, probe))
    for i, (source, write) in enumerate(((state, None), (probe, probe_ref))):
        copies[i].wait()
        main = source[:, :3072]
        sixth = jnp.concatenate([source[q : q + 1, 3072:] for q in range(3)], axis=1)
        seventh = jnp.concatenate([source[q : q + 1, 3072:] for q in range(3, 6)], axis=1)
        whole = jnp.concatenate([main, sixth, seventh], axis=0)
        if write is None:
            for n in range(4):
                state_ref[n] = whole
        else:
            write[:, :3072] = whole
            write[:, 3072:] = whole


def core_order(core):
    def first_token(packed):
        inner = packed & 127
        z = (inner >> 3) & 3
        y = inner >> 5
        c = jnp.where((packed >> 7) == 0, core, 1 - core)
        return (z * 8 + y * 2 + c) * 6

    return first_token


def unpack_state(core, xa, xb, held):
    main, rest = selectors(core_order(core), 256)
    squares = jnp.zeros((TOK, 128), F32)

    def chunk_of(m):
        cols = slice(m * 1024, (m + 1) * 1024)
        return jnp.concatenate([xa[:, cols], xb[:, cols]], axis=0)

    for start, x in pieces(main, rest, chunk_of):
        for b in range(8):
            piece = x[:, b * 128 : (b + 1) * 128]
            squares = squares + piece * piece
            held[start // 128 + b] = piece.astype(BF)
    return lax.rsqrt(row_sum(squares) * (1.0 / 4096) + EPS)


def row_sum(v):
    return jnp.sum(v, axis=-1, keepdims=True)


def first_kernel(
    meta, xa, xb, maps_hbm, gain, q_gain, k_gain, att_ref, col_ref, held, maps, sem
):
    copies = fetch(sem, (maps_hbm, maps))
    recip = unpack_state(meta[0], xa, xb, held)
    copies[0].wait()
    proj = jnp.zeros((TOK, 384), F32)
    for h in range(0, 32, 2):
        left = (held[h].astype(F32) * recip * gain[h]).astype(BF)
        right = (held[h + 1].astype(F32) * recip * gain[h + 1]).astype(BF)
        rows = jnp.concatenate([maps[h], maps[h + 1]], axis=0)
        proj = proj + dot(jnp.concatenate([left, right], axis=1), rows)
    att = attend(proj, q_gain[...], k_gain[...])
    for i in range(4):
        att_ref[i] = att
    col_ref[...] = held[meta[1]]


def blocks(core, own, oth):
    for side, c in ((own, core), (oth, 1 - core)):
        for y in range(4):
            for z in (0, 2):
                yield side, y * 4 + z, z * 8 + y * 2 + c


def plane_products(core, own, oth, rows):
    left = []
    for z in range(4):
        mine, other = own[z], oth[z]
        first = jnp.where(core == 0, mine, other)
        second = jnp.where(core == 0, other, mine)
        left.append(jnp.concatenate([first, second], axis=1))
    for y in range(4):
        mapped = None
        for z in range(4):
            right = jnp.concatenate([rows[y, z * 2], rows[y, z * 2 + 1]], axis=0)
            part = dot(left[z], right)
            mapped = part if mapped is None else mapped + part
        yield y, mapped


def plane_kernel(meta, own, oth, rows_hbm, part_ref, rows, sem):
    fetch(sem, (rows_hbm, rows))[0].wait()
    for y, mapped in plane_products(meta[0], own, oth, rows):
        part_ref[y] = mapped


def middle_kernel(meta, parts, gates, col, vel_ref, mid_ref):
    total = (parts[0] + parts[1]) + (parts[2] + parts[3])
    vel = (gates[meta[1]] * total).astype(BF)
    vel_ref[...] = vel
    mid = (col[...].astype(F32) + STEP * vel.astype(F32)).astype(BF)
    for i in range(4):
        mid_ref[i] = mid


def both_rows(x, probe, recip, d_recip, gain):
    normed = (x * recip * gain).astype(BF)
    d_normed = ((probe * recip + x * d_recip) * gain).astype(BF)
    return jnp.concatenate([normed, d_normed], axis=0)


def tangent_kernel(
    meta, xa_hbm, xb_hbm, packed_hbm, maps_hbm, gain, q_gain, k_gain, after, probe_ref, datt_ref,
    held, xa, xb, packed, maps, sem,
):
    copies = fetch(
        sem, (xa_hbm, xa), (xb_hbm, xb), (packed_hbm.at[:, :3072], packed), (maps_hbm, maps)
    )
    copies[0].wait()
    copies[1].wait()
    recip = unpack_state(meta[0], xa, xb, held)
    main, rest = selectors(lambda row: (row >> 3) * 6, 256)
    copies[2].wait()
    dots = jnp.zeros((TOK, 128), F32)
    for start, x in pieces(main, rest, lambda m: packed[:, m * 1024 : (m + 1) * 1024]):
        for b in range(8):
            piece = x[:, b * 128 : (b + 1) * 128]
            dots = dots + piece * held[start // 128 + b].astype(F32)
            probe_ref[start // 128 + b] = piece.astype(BF)
    d_recip = -(recip * recip * recip) * (row_sum(dots) * (1.0 / 4096))
    copies[3].wait()
    proj = jnp.zeros((2 * TOK, 384), F32)
    for h in range(0, 32, 2):
        pair = [
            both_rows(held[i].astype(F32), probe_ref[i].astype(F32), recip, d_recip, gain[i])
            for i in (h, h + 1)
        ]
        rows = jnp.concatenate([maps[h], maps[h + 1]], axis=0)
        proj = proj + dot(jnp.concatenate(pair, axis=1), rows)
    datt_ref[...] = attend_tangent(proj[:TOK], proj[TOK:], q_gain[...], k_gain[...])[1]


def second_kernel(
    meta, own, oth, probe, maps_hbm, gain, q_gain, k_gain, datt1, both_ref, maps, sem
):
    core = meta[0]
    copies = fetch(sem, (maps_hbm, maps))
    squares = jnp.zeros((TOK, 128), F32)
    dots = jnp.zeros((TOK, 128), F32)
    for side, b, h in blocks(core, own, oth):
        for i in range(2):
            x = side[b + i].astype(F32)
            squares = squares + x * x
            dots = dots + x * probe[h + 8 * i].astype(F32)
    recip = lax.rsqrt(row_sum(squares) * (1.0 / 4096) + EPS)
    d_recip = -(recip * recip * recip) * (row_sum(dots) * (1.0 / 4096))
    copies[0].wait()
    proj = jnp.zeros((2 * TOK, 384), F32)
    for side, b, h in blocks(core, own, oth):
        pair = [
            both_rows(
                side[b + i].astype(F32), probe[h + 8 * i].astype(F32), recip, d_recip, gain[h + 8 * i]
            )
            for i in range(2)
        ]
        rows = jnp.concatenate([maps[h], maps[h + 8]], axis=0)
        proj = proj + dot(jnp.concatenate(pair, axis=1), rows)
    att, d_att = attend_tangent(proj[:TOK], proj[TOK:], q_gain[...], k_gain[...])
    d_both = (d_att + datt1[...]).astype(BF)
    for i in range(4):
        both_ref[i, :TOK] = att
        both_ref[i, TOK:] = d_both


def last_kernel(meta, own, oth, rows_hbm, gates, vel_hbm, probe_hbm, out_ref, rows, vel1, probe, sem):
    core, plane, slab = meta[0], meta[2], meta[3]
    columns = [(probe_hbm.at[slab * 8 + y * 2 + core], probe.at[y]) for y in range(4)]
    copies = fetch(sem, (rows_hbm, rows), (vel_hbm, vel1), *columns)
    row = lax.broadcasted_iota(jnp.int32, (256, TOK), 0)
    token = lax.broadcasted_iota(jnp.int32, (256, TOK), 1)
    hit = (token == (row >> 3) * 6 + (row & 7)) & ((row & 7) < 6)
    lay = jnp.where(hit, jnp.ones((256, TOK), F32), jnp.zeros((256, TOK), F32)).astype(BF)
    for copy in copies:
        copy.wait()
    trace = jnp.zeros((1, 128), F32)
    laid = []
    for y, mapped in plane_products(core, own, oth, rows):
        column = slab * 8 + y * 2 + core
        mapped = mapped * gates[column]
        terms = mapped[TOK:] * probe[y].astype(F32)
        trace = trace + jnp.sum(terms, axis=0, keepdims=True)
        vel = vel1[...].astype(F32)
        part = mapped[:TOK] + jnp.where(plane == y, vel, jnp.zeros_like(vel))
        laid.append(dot(lay, part.astype(BF)))
    trace = row_sum(trace)
    high = trace.astype(BF).astype(F32)
    mid = (trace - high).astype(BF).astype(F32)
    low = trace - high - mid
    lane = lax.broadcasted_iota(jnp.int32, (1, 128), 1)
    coded = jnp.where(lane == 0, high, jnp.where(lane == 1, mid, jnp.where(lane == 2, low, 0.0)))
    slot = lax.broadcasted_iota(jnp.int32, (256, 128), 0) & 7
    for y in range(4):
        block = jnp.where(slot == 6, coded, laid[y]) if y == 0 else laid[y]
        out_ref[:, y * 128 : (y + 1) * 128] = block.astype(BF)


def land_kernel(got, state, next_ref, change_ref):
    total = jnp.zeros((8, 128), F32)
    for z in range(4):
        for c in range(2):
            sums = jnp.zeros((8, 512), F32)
            for y in range(4):
                block = got[z * 8 + y * 2 + c].astype(F32)
                total = total + block[:, :128]
                sums = sums + block
            for y in range(4):
                j = z * 8 + y * 2 + c
                cols = slice(j * 128, (j + 1) * 128)
                both = sums[:6, y * 128 : (y + 1) * 128]
                next_ref[:, cols] = (state[:, cols].astype(F32) + 0.5 * STEP * both).astype(BF)
    change_ref[...] = jnp.broadcast_to(-0.5 * STEP * row_sum(total[6:7, :]) / TOK, (1, 128))


def spread(copies):
    n, rows, lanes = copies.shape
    a = lax.all_to_all(copies.reshape(n * rows, lanes), "z", 0, 0, tiled=True)
    return a, lax.all_to_all(jnp.tile(a, (4, 1)), "y", 0, 0, tiled=True)


def swap(block):
    return lax.ppermute(block, "c", [(0, 1), (1, 0)])


def per_device(state, probe, norm_gain, head_maps, query_gain, key_gain, out_map, out_gate):
    place = lax.axis_index(SEQ)
    meta = [lax.axis_index("c"), place, lax.axis_index("y"), lax.axis_index("z")]
    meta = jnp.stack(meta).astype(jnp.int32)
    gates = out_gate.reshape(32, 1, 128)
    maps = head_maps.reshape(32, 128, 384)
    gain = norm_gain.reshape(32, 1, 128)

    packed_state, packed_probe = call(
        pack_kernel, [shape((4, 8, 3072)), shape((8, 6144))], 0, (state,), (probe,),
        scratch=[pltpu.VMEM((6, 4096), BF), pltpu.VMEM((6, 4096), BF), sems(2)], vmem_mib=FULL,
    )
    probe_all = lax.all_gather(packed_probe, SEQ, axis=0, tiled=True)
    _, own = spread(packed_state)
    by_plane = out_map.reshape(4, 4, 256, 128).transpose(1, 0, 2, 3).reshape(4096, 128)
    by_plane, own = lax.optimization_barrier((by_plane, own))
    plane_outs = lax.all_to_all(by_plane, "y", 0, 0, tiled=True)
    oth = swap(own)
    att1, col = call(
        first_kernel, [shape((4, TOK, 128)), shape((TOK, 128))],
        1, meta, own, oth, (maps,), gain, query_gain, key_gain, scratch=[HELD, MAPS, sems(1)],
    )
    att1, plane_outs = lax.optimization_barrier((att1, plane_outs))
    plane_outs = plane_outs.reshape(4, 8, 128, 128)
    own1 = lax.all_to_all(att1.reshape(4 * TOK, 128), "z", 0, 0, tiled=True)
    oth1 = swap(own1)
    parts = call(
        plane_kernel, shape((4, TOK, 128), F32),
        1, meta, own1.reshape(4, TOK, 128), oth1.reshape(4, TOK, 128), (plane_outs,),
        scratch=[ROWS, sems(1)], vmem_mib=MIDDLE,
    )
    parts = lax.all_to_all(parts.reshape(4 * TOK, 128), "y", 0, 0, tiled=True)
    vel1, mid = call(
        middle_kernel, [shape((TOK, 128)), shape((4, TOK, 128))],
        1, meta, parts.reshape(4, TOK, 128), gates, col, vmem_mib=MIDDLE,
    )
    _, own_m = spread(mid)
    probe_blocks, datt1 = call(
        tangent_kernel, [shape((32, TOK, 128)), shape((TOK, 128), F32)],
        1, meta, (own,), (oth,), (probe_all,), (maps,), gain, query_gain, key_gain, (mid,),
        scratch=[
            HELD, pltpu.VMEM((128, 3072), BF), pltpu.VMEM((128, 3072), BF),
            pltpu.VMEM((256, 3072), BF), MAPS, sems(4),
        ],
        vmem_mib=FULL,
    )
    own_m, datt1 = lax.optimization_barrier((own_m, datt1))
    oth_m = swap(own_m).reshape(16, TOK, 128)
    own_m = own_m.reshape(16, TOK, 128)
    both = call(
        second_kernel, shape((4, 2 * TOK, 128)),
        1, meta, own_m, oth_m, probe_blocks, (maps,), gain, query_gain, key_gain, datt1,
        scratch=[MAPS, sems(1)], vmem_mib=SECOND,
    )
    own2 = lax.all_to_all(both.reshape(8 * TOK, 128), "z", 0, 0, tiled=True)
    oth2 = swap(own2)
    columns = call(
        last_kernel, shape((256, 512)),
        1, meta, own2.reshape(4, 2 * TOK, 128), oth2.reshape(4, 2 * TOK, 128),
        (plane_outs,), gates, (vel1,), (probe_blocks,),
        scratch=[
            ROWS, pltpu.VMEM((TOK, 128), BF),
            pltpu.VMEM((4, TOK, 128), BF), sems(6),
        ],
        vmem_mib=LAST,
    )
    got = lax.all_to_all(columns, SEQ, 0, 0, tiled=True).reshape(32, 8, 512)
    next_state, change = call(
        land_kernel, [shape((6, 4096)), shape((1, 128), F32)], 0, got, state
    )
    return next_state, change[0, :1]


def solution(mesh):
    split = Mesh(mesh.devices.reshape(4, 4, 2, 4, 4), ("z", "y", "c", "w", "x"))
    rows = P(("w", "x", "z", "y", "c"), None)
    return jax.shard_map(
        per_device,
        mesh=split,
        in_specs=(rows, rows, P(), P(SEQ, None, None), P(SEQ, None), P(SEQ, None), P(None, SEQ), P()),
        out_specs=(rows, P(("w", "x"))),
        check_vma=False,
    )
```

```python
import jax
import jax.numpy as jnp
from jax import lax
from jax.experimental import pallas as pl
from jax.experimental.pallas import tpu as pltpu
from jax.sharding import Mesh, PartitionSpec as P

EPS = 1e-06
STEP = 0.5
SEQ = ("z", "y", "c")
BF = jnp.bfloat16
F32 = jnp.float32
NT = (((1,), (1,)), ((), ()))
TOK = 192
SCALE = 128 ** (-0.5)


def dot(a, b):
    return jnp.dot(a, b, preferred_element_type=F32)


def dot_nt(a, b):
    return lax.dot_general(a, b, NT, preferred_element_type=F32)


def row_mean(v):
    return jnp.mean(v, axis=-1, keepdims=True)


HELD = pltpu.VMEM((32, TOK, 128), BF)
MAPS = pltpu.VMEM((32, 128, 384), BF)
ROWS = pltpu.VMEM((4, 8, 128, 128), BF)


FULL = 60
LAST = 51
MIDDLE = 51
SECOND = 51


def sems(n):
    return pltpu.SemaphoreType.DMA((n,))


def fetch(sem, *pairs):
    copies = [pltpu.make_async_copy(a, b, sem.at[i]) for i, (a, b) in enumerate(pairs)]
    for copy in copies:
        copy.start()
    return copies


def call(kernel, out_shape, n_scalar, *args, scratch=(), vmem_mib=20, n_hbm=0):
    in_specs = [pl.BlockSpec(memory_space=pltpu.SMEM)] * n_scalar
    for a in args[n_scalar:]:
        if isinstance(a, tuple):
            in_specs.append(pl.BlockSpec(memory_space=pltpu.HBM))
        else:
            in_specs.append(pl.BlockSpec(memory_space=pltpu.VMEM))
    flat = [a[0] if isinstance(a, tuple) else a for a in args]
    multi = isinstance(out_shape, (tuple, list))
    vmem = pl.BlockSpec(memory_space=pltpu.VMEM)
    hbm = pl.BlockSpec(memory_space=pltpu.HBM)
    return pl.pallas_call(
        kernel,
        out_shape=out_shape,
        in_specs=in_specs,
        out_specs=[vmem] * (len(out_shape) - n_hbm) + [hbm] * n_hbm if multi else vmem,
        scratch_shapes=scratch,
        compiler_params=pltpu.CompilerParams(vmem_limit_bytes=vmem_mib * 1024 * 1024),
    )(*flat)


def shape(dims, kind=BF):
    return jax.ShapeDtypeStruct(dims, kind)


def selectors(first_row_token, rows):
    packed = lax.broadcasted_iota(jnp.int32, (TOK, rows), 1)
    token = lax.broadcasted_iota(jnp.int32, (TOK, rows), 0)
    slot = packed & 7
    base = first_row_token(packed)
    one = jnp.ones((TOK, rows), F32)
    zero = jnp.zeros((TOK, rows), F32)
    main = jnp.where((token == base + slot) & (slot < 6), one, zero).astype(BF)
    rest = [
        jnp.where((token == base + m + 3 * (slot - 6)) & (slot >= 6), one, zero).astype(BF)
        for m in range(3)
    ]
    return main, rest


def pieces(main, rest, chunk_of):
    tail = None
    for m in range(3):
        chunk = chunk_of(m)
        part = dot(rest[m], chunk)
        tail = part if tail is None else tail + part
        yield m * 1024, dot(main, chunk)
    yield 3072, tail


def qkv_norm(proj, q_gain, k_gain):
    query, key, val = proj[:, :128], proj[:, 128:256], proj[:, 256:]
    rq = lax.rsqrt(row_mean(query * query) + EPS)
    rk = lax.rsqrt(row_mean(key * key) + EPS)
    qn = (query * rq * q_gain).astype(BF)
    kn = (key * rk * k_gain).astype(BF)
    return query, key, rq, rk, qn, kn, val.astype(BF)


def probabilities(qn, kn):
    expo = jnp.exp(dot_nt(qn, kn) * SCALE)
    return expo / jnp.sum(expo, axis=-1, keepdims=True)


def attend(proj, q_gain, k_gain):
    _, _, _, _, qn, kn, val = qkv_norm(proj, q_gain, k_gain)
    return dot(probabilities(qn, kn).astype(BF), val).astype(BF)


def attend_tangent(proj, d_proj, q_gain, k_gain):
    query, key, rq, rk, qn, kn, val = qkv_norm(proj, q_gain, k_gain)
    dq, dk, dv = d_proj[:, :128], d_proj[:, 128:256], d_proj[:, 256:].astype(BF)
    drq = -(rq * rq * rq) * row_mean(query * dq)
    drk = -(rk * rk * rk) * row_mean(key * dk)
    dqn = ((dq * rq + query * drq) * q_gain).astype(BF)
    dkn = ((dk * rk + key * drk) * k_gain).astype(BF)
    probs = probabilities(qn, kn)
    ds = (dot_nt(dqn, kn) + dot_nt(qn, dkn)) * SCALE
    d_probs = probs * (ds - jnp.sum(probs * ds, axis=-1, keepdims=True))
    probs = probs.astype(BF)
    return dot(probs, val).astype(BF), dot(d_probs.astype(BF), val) + dot(probs, dv)


def pack_kernel(
    meta, state_hbm, probe_hbm, out_map, state_ref, probe_ref, s0, s1, s2, s3, state, probe, sem
):
    shifted = [(out_map.at[:, (meta[2] + k) & 3], to) for k, to in enumerate((s0, s1, s2, s3))]
    copies = fetch(sem, (state_hbm, state), (probe_hbm, probe), *shifted)
    for i, (source, write) in enumerate(((state, None), (probe, probe_ref))):
        copies[i].wait()
        main = source[:, :3072]
        sixth = jnp.concatenate([source[q : q + 1, 3072:] for q in range(3)], axis=1)
        seventh = jnp.concatenate([source[q : q + 1, 3072:] for q in range(3, 6)], axis=1)
        whole = jnp.concatenate([main, sixth, seventh], axis=0)
        if write is None:
            for n in range(4):
                state_ref[n] = whole
        else:
            write[:, :3072] = whole
            write[:, 3072:] = whole
    for copy in copies[2:]:
        copy.wait()


def core_order(core):
    def first_token(packed):
        inner = packed & 127
        z = (inner >> 3) & 3
        y = inner >> 5
        c = jnp.where((packed >> 7) == 0, core, 1 - core)
        return (z * 8 + y * 2 + c) * 6

    return first_token


def unpack_state(core, xa, xb, held):
    main, rest = selectors(core_order(core), 256)
    squares = jnp.zeros((TOK, 128), F32)

    def chunk_of(m):
        cols = slice(m * 1024, (m + 1) * 1024)
        return jnp.concatenate([xa[:, cols], xb[:, cols]], axis=0)

    for start, x in pieces(main, rest, chunk_of):
        for b in range(8):
            piece = x[:, b * 128 : (b + 1) * 128]
            squares = squares + piece * piece
            held[start // 128 + b] = piece.astype(BF)
    return lax.rsqrt(row_sum(squares) * (1.0 / 4096) + EPS)


def row_sum(v):
    return jnp.sum(v, axis=-1, keepdims=True)


def first_kernel(
    meta, xa, xb, maps_hbm, gain, q_gain, k_gain, att_ref, col_ref, held, maps, sem
):
    copies = fetch(sem, (maps_hbm, maps))
    recip = unpack_state(meta[0], xa, xb, held)
    copies[0].wait()
    proj = jnp.zeros((TOK, 384), F32)
    for h in range(0, 32, 2):
        left = (held[h].astype(F32) * recip * gain[h]).astype(BF)
        right = (held[h + 1].astype(F32) * recip * gain[h + 1]).astype(BF)
        rows = jnp.concatenate([maps[h], maps[h + 1]], axis=0)
        proj = proj + dot(jnp.concatenate([left, right], axis=1), rows)
    att = attend(proj, q_gain[...], k_gain[...])
    for i in range(4):
        att_ref[i] = att
    col_ref[...] = held[meta[1]]


def blocks(core, own, oth):
    for side, c in ((own, core), (oth, 1 - core)):
        for y in range(4):
            for z in (0, 2):
                yield side, y * 4 + z, z * 8 + y * 2 + c


SHIFTS = (0, 1, 3, 2)


def plane_products(core, own, oth, rows):
    left = []
    for z in range(4):
        mine, other = own[z], oth[z]
        first = jnp.where(core == 0, mine, other)
        second = jnp.where(core == 0, other, mine)
        left.append(jnp.concatenate([first, second], axis=1))
    for i in range(4):
        mapped = None
        for z in range(4):
            right = jnp.concatenate([rows[i, z * 2], rows[i, z * 2 + 1]], axis=0)
            part = dot(left[z], right)
            mapped = part if mapped is None else mapped + part
        yield i, mapped


def plane_kernel(meta, own, oth, r0, r1, r2, r3, part_ref, rows, sem):
    copies = fetch(sem, *[(r, rows.at[i]) for i, r in enumerate((r0, r1, r2, r3))])
    for copy in copies:
        copy.wait()
    for i, mapped in plane_products(meta[0], own, oth, rows):
        part_ref[(meta[2] - SHIFTS[i]) & 3] = mapped


def middle_kernel(meta, parts, gates, col, vel_ref, mid_ref):
    total = (parts[0] + parts[1]) + (parts[2] + parts[3])
    vel = (gates[meta[1]] * total).astype(BF)
    vel_ref[...] = vel
    mid = (col[...].astype(F32) + STEP * vel.astype(F32)).astype(BF)
    for i in range(4):
        mid_ref[i] = mid


def both_rows(x, probe, recip, d_recip, gain):
    normed = (x * recip * gain).astype(BF)
    d_normed = ((probe * recip + x * d_recip) * gain).astype(BF)
    return jnp.concatenate([normed, d_normed], axis=0)


def tangent_kernel(
    meta, xa_hbm, xb_hbm, packed_hbm, maps_hbm, gain, q_gain, k_gain, after, probe_ref, datt_ref,
    held, xa, xb, packed, maps, sem,
):
    copies = fetch(
        sem, (xa_hbm, xa), (xb_hbm, xb), (packed_hbm.at[:, :3072], packed), (maps_hbm, maps)
    )
    copies[0].wait()
    copies[1].wait()
    recip = unpack_state(meta[0], xa, xb, held)
    main, rest = selectors(lambda row: (row >> 3) * 6, 256)
    copies[2].wait()
    dots = jnp.zeros((TOK, 128), F32)
    for start, x in pieces(main, rest, lambda m: packed[:, m * 1024 : (m + 1) * 1024]):
        for b in range(8):
            piece = x[:, b * 128 : (b + 1) * 128]
            dots = dots + piece * held[start // 128 + b].astype(F32)
            probe_ref[start // 128 + b] = piece.astype(BF)
    d_recip = -(recip * recip * recip) * (row_sum(dots) * (1.0 / 4096))
    copies[3].wait()
    proj = jnp.zeros((2 * TOK, 384), F32)
    for h in range(0, 32, 2):
        pair = [
            both_rows(held[i].astype(F32), probe_ref[i].astype(F32), recip, d_recip, gain[i])
            for i in (h, h + 1)
        ]
        rows = jnp.concatenate([maps[h], maps[h + 1]], axis=0)
        proj = proj + dot(jnp.concatenate(pair, axis=1), rows)
    datt_ref[...] = attend_tangent(proj[:TOK], proj[TOK:], q_gain[...], k_gain[...])[1]


def second_kernel(
    meta, own, oth, probe, maps_hbm, gain, q_gain, k_gain, datt1, both_ref, maps, sem
):
    core = meta[0]
    copies = fetch(sem, (maps_hbm, maps))
    squares = jnp.zeros((TOK, 128), F32)
    dots = jnp.zeros((TOK, 128), F32)
    for side, b, h in blocks(core, own, oth):
        for i in range(2):
            x = side[b + i].astype(F32)
            squares = squares + x * x
            dots = dots + x * probe[h + 8 * i].astype(F32)
    recip = lax.rsqrt(row_sum(squares) * (1.0 / 4096) + EPS)
    d_recip = -(recip * recip * recip) * (row_sum(dots) * (1.0 / 4096))
    copies[0].wait()
    proj = jnp.zeros((2 * TOK, 384), F32)
    for side, b, h in blocks(core, own, oth):
        pair = [
            both_rows(
                side[b + i].astype(F32), probe[h + 8 * i].astype(F32), recip, d_recip, gain[h + 8 * i]
            )
            for i in range(2)
        ]
        rows = jnp.concatenate([maps[h], maps[h + 8]], axis=0)
        proj = proj + dot(jnp.concatenate(pair, axis=1), rows)
    att, d_att = attend_tangent(proj[:TOK], proj[TOK:], q_gain[...], k_gain[...])
    d_both = (d_att + datt1[...]).astype(BF)
    for i in range(4):
        both_ref[i, :TOK] = att
        both_ref[i, TOK:] = d_both


def last_kernel(
    meta, own, oth, r0, r1, r2, r3, gates, vel_hbm, probe_hbm, out_ref, rows, vel1, probe, sem
):
    core, slab = meta[0], meta[3]
    place_y = [(meta[2] - shift) & 3 for shift in SHIFTS]
    columns = [slab * 8 + y * 2 + core for y in place_y]
    copies = fetch(
        sem,
        *[(r, rows.at[i]) for i, r in enumerate((r0, r1, r2, r3))],
        (vel_hbm, vel1),
        *[(probe_hbm.at[column], probe.at[i]) for i, column in enumerate(columns)],
    )
    row = lax.broadcasted_iota(jnp.int32, (256, TOK), 0)
    token = lax.broadcasted_iota(jnp.int32, (256, TOK), 1)
    hit = (token == (row >> 3) * 6 + (row & 7)) & ((row & 7) < 6)
    lay = jnp.where(hit, jnp.ones((256, TOK), F32), jnp.zeros((256, TOK), F32)).astype(BF)
    for copy in copies:
        copy.wait()
    trace = jnp.zeros((1, 128), F32)
    laid = []
    for i, mapped in plane_products(core, own, oth, rows):
        mapped = mapped * gates[columns[i]]
        terms = mapped[TOK:] * probe[i].astype(F32)
        trace = trace + jnp.sum(terms, axis=0, keepdims=True)
        part = mapped[:TOK]
        if i == 0:
            part = part + vel1[...].astype(F32)
        laid.append(dot(lay, part.astype(BF)))
    trace = row_sum(trace)
    high = trace.astype(BF).astype(F32)
    mid = (trace - high).astype(BF).astype(F32)
    low = trace - high - mid
    lane = lax.broadcasted_iota(jnp.int32, (1, 128), 1)
    coded = jnp.where(lane == 0, high, jnp.where(lane == 1, mid, jnp.where(lane == 2, low, 0.0)))
    slot = lax.broadcasted_iota(jnp.int32, (256, 128), 0) & 7
    for i in range(4):
        block = jnp.where(slot == 6, coded, laid[i]) if i == 0 else laid[i]
        out_ref[:, pl.ds(pl.multiple_of(place_y[i] * 128, 128), 128)] = block.astype(BF)


def land_kernel(got, state, next_ref, change_ref):
    total = jnp.zeros((8, 512), F32)
    for z in range(4):
        for c in range(2):
            sums = jnp.zeros((8, 512), F32)
            for y in range(4):
                block = got[z * 8 + y * 2 + c].astype(F32)
                sums = sums + block
            total = total + sums
            for y in range(4):
                j = z * 8 + y * 2 + c
                cols = slice(j * 128, (j + 1) * 128)
                both = sums[:6, y * 128 : (y + 1) * 128]
                next_ref[:, cols] = (state[:, cols].astype(F32) + 0.5 * STEP * both).astype(BF)
    change_ref[...] = jnp.broadcast_to(-0.5 * STEP * row_sum(total[6:7, :]) / TOK, (1, 128))


def spread(copies):
    n, rows, lanes = copies.shape
    a = lax.all_to_all(copies.reshape(n * rows, lanes), "z", 0, 0, tiled=True)
    return a, lax.all_to_all(jnp.tile(a, (4, 1)), "y", 0, 0, tiled=True)


def swap(block):
    return lax.ppermute(block, "c", [(0, 1), (1, 0)])


def per_device(state, probe, norm_gain, head_maps, query_gain, key_gain, out_map, out_gate):
    place = lax.axis_index(SEQ)
    meta = [lax.axis_index("c"), place, lax.axis_index("y"), lax.axis_index("z")]
    meta = jnp.stack(meta).astype(jnp.int32)
    gates = out_gate.reshape(32, 1, 128)
    maps = head_maps.reshape(32, 128, 384)
    gain = norm_gain.reshape(32, 1, 128)

    packed_state, packed_probe, *sends = call(
        pack_kernel, [shape((4, 8, 3072)), shape((8, 6144))] + [shape((4, 256, 128))] * 4,
        1, meta, (state,), (probe,), (out_map.reshape(4, 4, 256, 128),),
        scratch=[pltpu.VMEM((6, 4096), BF), pltpu.VMEM((6, 4096), BF), sems(6)],
        vmem_mib=FULL, n_hbm=4,
    )
    probe_all = lax.all_gather(packed_probe, SEQ, axis=0, tiled=True)
    _, own = spread(packed_state)
    plane_outs = [sends[0]]
    for k in (1, 3, 2):
        plane_outs.append(lax.ppermute(sends[k], "y", [(y, (y + k) % 4) for y in range(4)]))
    plane_outs = [(piece.reshape(8, 128, 128),) for piece in plane_outs]
    oth = swap(own)
    att1, col = call(
        first_kernel, [shape((4, TOK, 128)), shape((TOK, 128))],
        1, meta, own, oth, (maps,), gain, query_gain, key_gain, scratch=[HELD, MAPS, sems(1)], vmem_mib=51,
    )
    own1 = lax.all_to_all(att1.reshape(4 * TOK, 128), "z", 0, 0, tiled=True)
    oth1 = swap(own1)
    parts = call(
        plane_kernel, shape((4, TOK, 128), F32),
        1, meta, own1.reshape(4, TOK, 128), oth1.reshape(4, TOK, 128), *plane_outs,
        scratch=[ROWS, sems(4)], vmem_mib=MIDDLE,
    )
    parts = lax.all_to_all(parts.reshape(4 * TOK, 128), "y", 0, 0, tiled=True)
    vel1, mid = call(
        middle_kernel, [shape((TOK, 128)), shape((4, TOK, 128))],
        1, meta, parts.reshape(4, TOK, 128), gates, col, vmem_mib=MIDDLE,
    )
    _, own_m = spread(mid)
    probe_blocks, datt1 = call(
        tangent_kernel, [shape((32, TOK, 128)), shape((TOK, 128), F32)],
        1, meta, (own,), (oth,), (probe_all,), (maps,), gain, query_gain, key_gain, (mid,),
        scratch=[
            HELD, pltpu.VMEM((128, 3072), BF), pltpu.VMEM((128, 3072), BF),
            pltpu.VMEM((256, 3072), BF), MAPS, sems(4),
        ],
        vmem_mib=FULL,
    )
    own_m, datt1 = lax.optimization_barrier((own_m, datt1))
    oth_m = swap(own_m).reshape(16, TOK, 128)
    own_m = own_m.reshape(16, TOK, 128)
    both = call(
        second_kernel, shape((4, 2 * TOK, 128)),
        1, meta, own_m, oth_m, probe_blocks, (maps,), gain, query_gain, key_gain, datt1,
        scratch=[MAPS, sems(1)], vmem_mib=SECOND,
    )
    own2 = lax.all_to_all(both.reshape(8 * TOK, 128), "z", 0, 0, tiled=True)
    oth2 = swap(own2)
    columns = call(
        last_kernel, shape((256, 512)),
        1, meta, own2.reshape(4, 2 * TOK, 128), oth2.reshape(4, 2 * TOK, 128),
        *plane_outs, gates, (vel1,), (probe_blocks,),
        scratch=[
            ROWS, pltpu.VMEM((TOK, 128), BF),
            pltpu.VMEM((4, TOK, 128), BF), sems(9),
        ],
        vmem_mib=LAST,
    )
    got = lax.all_to_all(columns, SEQ, 0, 0, tiled=True).reshape(32, 8, 512)
    next_state, change = call(
        land_kernel, [shape((6, 4096)), shape((1, 128), F32)], 0, got, state
    )
    return next_state, change[0, :1]


def solution(mesh):
    split = Mesh(mesh.devices.reshape(4, 4, 2, 4, 4), ("z", "y", "c", "w", "x"))
    rows = P(("w", "x", "z", "y", "c"), None)
    return jax.shard_map(
        per_device,
        mesh=split,
        in_specs=(rows, rows, P(), P(SEQ, None, None), P(SEQ, None), P(SEQ, None), P(None, SEQ), P()),
        out_specs=(rows, P(("w", "x"))),
        check_vma=False,
    )
```

```python
import jax
import jax.numpy as jnp
from jax import lax
from jax.experimental import pallas as pl
from jax.experimental.pallas import tpu as pltpu
from jax.sharding import Mesh, PartitionSpec as P

EPS = 1e-06
STEP = 0.5
SEQ = ("z", "y", "c")
BF = jnp.bfloat16
F32 = jnp.float32
NT = (((1,), (1,)), ((), ()))
TOK = 192
SCALE = 128 ** (-0.5)


def dot(a, b):
    return jnp.dot(a, b, preferred_element_type=F32)


def dot_nt(a, b):
    return lax.dot_general(a, b, NT, preferred_element_type=F32)


def row_mean(v):
    return jnp.mean(v, axis=-1, keepdims=True)


HELD = pltpu.VMEM((32, TOK, 128), BF)
MAPS = pltpu.VMEM((32, 128, 384), BF)
ROWS = pltpu.VMEM((4, 8, 128, 128), BF)


FULL = 60
LAST = 51
MIDDLE = 51
SECOND = 51


def sems(n):
    return pltpu.SemaphoreType.DMA((n,))


def fetch(sem, *pairs):
    copies = [pltpu.make_async_copy(a, b, sem.at[i]) for i, (a, b) in enumerate(pairs)]
    for copy in copies:
        copy.start()
    return copies


def call(kernel, out_shape, n_scalar, *args, scratch=(), vmem_mib=20, n_hbm=0):
    in_specs = [pl.BlockSpec(memory_space=pltpu.SMEM)] * n_scalar
    for a in args[n_scalar:]:
        if isinstance(a, tuple):
            in_specs.append(pl.BlockSpec(memory_space=pltpu.HBM))
        else:
            in_specs.append(pl.BlockSpec(memory_space=pltpu.VMEM))
    flat = [a[0] if isinstance(a, tuple) else a for a in args]
    multi = isinstance(out_shape, (tuple, list))
    vmem = pl.BlockSpec(memory_space=pltpu.VMEM)
    hbm = pl.BlockSpec(memory_space=pltpu.HBM)
    return pl.pallas_call(
        kernel,
        out_shape=out_shape,
        in_specs=in_specs,
        out_specs=[vmem] * (len(out_shape) - n_hbm) + [hbm] * n_hbm if multi else vmem,
        scratch_shapes=scratch,
        compiler_params=pltpu.CompilerParams(vmem_limit_bytes=vmem_mib * 1024 * 1024),
    )(*flat)


def shape(dims, kind=BF):
    return jax.ShapeDtypeStruct(dims, kind)


def selectors(first_row_token, rows):
    packed = lax.broadcasted_iota(jnp.int32, (TOK, rows), 1)
    token = lax.broadcasted_iota(jnp.int32, (TOK, rows), 0)
    slot = packed & 7
    base = first_row_token(packed)
    one = jnp.ones((TOK, rows), F32)
    zero = jnp.zeros((TOK, rows), F32)
    main = jnp.where((token == base + slot) & (slot < 6), one, zero).astype(BF)
    rest = [
        jnp.where((token == base + m + 3 * (slot - 6)) & (slot >= 6), one, zero).astype(BF)
        for m in range(3)
    ]
    return main, rest


def pieces(main, rest, chunk_of):
    tail = None
    for m in range(3):
        chunk = chunk_of(m)
        part = dot(rest[m], chunk)
        tail = part if tail is None else tail + part
        yield m * 1024, dot(main, chunk)
    yield 3072, tail


def qkv_norm(proj, q_gain, k_gain):
    query, key, val = proj[:, :128], proj[:, 128:256], proj[:, 256:]
    rq = lax.rsqrt(row_mean(query * query) + EPS)
    rk = lax.rsqrt(row_mean(key * key) + EPS)
    qn = (query * rq * q_gain).astype(BF)
    kn = (key * rk * k_gain).astype(BF)
    return query, key, rq, rk, qn, kn, val.astype(BF)


def probabilities(qn, kn):
    expo = jnp.exp(dot_nt(qn, kn) * SCALE)
    return expo / jnp.sum(expo, axis=-1, keepdims=True)


def attend(proj, q_gain, k_gain):
    _, _, _, _, qn, kn, val = qkv_norm(proj, q_gain, k_gain)
    return dot(probabilities(qn, kn).astype(BF), val).astype(BF)


def attend_tangent(proj, d_proj, q_gain, k_gain):
    query, key, rq, rk, qn, kn, val = qkv_norm(proj, q_gain, k_gain)
    dq, dk, dv = d_proj[:, :128], d_proj[:, 128:256], d_proj[:, 256:].astype(BF)
    drq = -(rq * rq * rq) * row_mean(query * dq)
    drk = -(rk * rk * rk) * row_mean(key * dk)
    dqn = ((dq * rq + query * drq) * q_gain).astype(BF)
    dkn = ((dk * rk + key * drk) * k_gain).astype(BF)
    probs = probabilities(qn, kn)
    ds = (dot_nt(dqn, kn) + dot_nt(qn, dkn)) * SCALE
    d_probs = probs * (ds - jnp.sum(probs * ds, axis=-1, keepdims=True))
    probs = probs.astype(BF)
    return dot(probs, val).astype(BF), dot(d_probs.astype(BF), val) + dot(probs, dv)


def pack_kernel(
    meta, state_hbm, probe_hbm, out_map, state_ref, probe_ref, s0, s1, s2, s3, state, probe, sem
):
    shifted = [(out_map.at[:, (meta[2] + k) & 3], to) for k, to in enumerate((s0, s1, s2, s3))]
    copies = fetch(sem, (state_hbm, state), (probe_hbm, probe), *shifted)
    for i, (source, write) in enumerate(((state, None), (probe, probe_ref))):
        copies[i].wait()
        main = source[:, :3072]
        sixth = jnp.concatenate([source[q : q + 1, 3072:] for q in range(3)], axis=1)
        seventh = jnp.concatenate([source[q : q + 1, 3072:] for q in range(3, 6)], axis=1)
        whole = jnp.concatenate([main, sixth, seventh], axis=0)
        if write is None:
            for n in range(4):
                state_ref[n] = whole
        else:
            write[:, :3072] = whole
            write[:, 3072:] = whole
    for copy in copies[2:]:
        copy.wait()


def core_order(core):
    def first_token(packed):
        inner = packed & 127
        z = (inner >> 3) & 3
        y = inner >> 5
        c = jnp.where((packed >> 7) == 0, core, 1 - core)
        return (z * 8 + y * 2 + c) * 6

    return first_token


def unpack_state(core, xa, xb, held):
    main, rest = selectors(core_order(core), 256)
    squares = jnp.zeros((TOK, 128), F32)

    def chunk_of(m):
        cols = slice(m * 1024, (m + 1) * 1024)
        return jnp.concatenate([xa[:, cols], xb[:, cols]], axis=0)

    for start, x in pieces(main, rest, chunk_of):
        for b in range(8):
            piece = x[:, b * 128 : (b + 1) * 128]
            squares = squares + piece * piece
            held[start // 128 + b] = piece.astype(BF)
    return lax.rsqrt(row_sum(squares) * (1.0 / 4096) + EPS)


def row_sum(v):
    return jnp.sum(v, axis=-1, keepdims=True)


def first_kernel(
    meta, xa, xb, maps_hbm, gain, q_gain, k_gain, att_ref, col_ref, held, maps, sem
):
    copies = fetch(sem, (maps_hbm, maps))
    recip = unpack_state(meta[0], xa, xb, held)
    copies[0].wait()
    proj = jnp.zeros((TOK, 384), F32)
    for h in range(0, 32, 2):
        left = (held[h].astype(F32) * recip * gain[h]).astype(BF)
        right = (held[h + 1].astype(F32) * recip * gain[h + 1]).astype(BF)
        rows = jnp.concatenate([maps[h], maps[h + 1]], axis=0)
        proj = proj + dot(jnp.concatenate([left, right], axis=1), rows)
    att = attend(proj, q_gain[...], k_gain[...])
    for i in range(4):
        att_ref[i] = att
    col_ref[...] = held[meta[1]]


def blocks(core, own, oth):
    for side, c in ((own, core), (oth, 1 - core)):
        for y in range(4):
            for z in (0, 2):
                yield side, y * 4 + z, z * 8 + y * 2 + c


SHIFTS = (0, 1, 3, 2)


def plane_products(core, own, oth, rows):
    left = []
    for z in range(4):
        mine, other = own[z], oth[z]
        first = jnp.where(core == 0, mine, other)
        second = jnp.where(core == 0, other, mine)
        left.append(jnp.concatenate([first, second], axis=1))
    for i in range(4):
        mapped = None
        for z in range(4):
            right = jnp.concatenate([rows[i, z * 2], rows[i, z * 2 + 1]], axis=0)
            part = dot(left[z], right)
            mapped = part if mapped is None else mapped + part
        yield i, mapped


def plane_kernel(meta, own, oth, r0, r1, r2, r3, part_ref, rows, sem):
    copies = fetch(sem, *[(r, rows.at[i]) for i, r in enumerate((r0, r1, r2, r3))])
    for copy in copies:
        copy.wait()
    for i, mapped in plane_products(meta[0], own, oth, rows):
        part_ref[(meta[2] - SHIFTS[i]) & 3] = mapped


def middle_kernel(meta, parts, gates, col, vel_ref, mid_ref):
    total = (parts[0] + parts[1]) + (parts[2] + parts[3])
    vel = (gates[meta[1]] * total).astype(BF)
    vel_ref[...] = vel
    mid = (col[...].astype(F32) + STEP * vel.astype(F32)).astype(BF)
    for i in range(4):
        mid_ref[i] = mid


def both_rows(x, probe, recip, d_recip, gain):
    normed = (x * recip * gain).astype(BF)
    d_normed = ((probe * recip + x * d_recip) * gain).astype(BF)
    return jnp.concatenate([normed, d_normed], axis=0)


def tangent_kernel(
    meta, xa_hbm, xb_hbm, packed_hbm, maps_hbm, gain, q_gain, k_gain, after, probe_ref, datt_ref,
    held, xa, xb, packed, maps, sem,
):
    copies = fetch(
        sem, (xa_hbm, xa), (xb_hbm, xb), (packed_hbm.at[:, :3072], packed), (maps_hbm, maps)
    )
    copies[0].wait()
    copies[1].wait()
    recip = unpack_state(meta[0], xa, xb, held)
    main, rest = selectors(lambda row: (row >> 3) * 6, 256)
    copies[2].wait()
    dots = jnp.zeros((TOK, 128), F32)
    for start, x in pieces(main, rest, lambda m: packed[:, m * 1024 : (m + 1) * 1024]):
        for b in range(8):
            piece = x[:, b * 128 : (b + 1) * 128]
            dots = dots + piece * held[start // 128 + b].astype(F32)
            probe_ref[start // 128 + b] = piece.astype(BF)
    d_recip = -(recip * recip * recip) * (row_sum(dots) * (1.0 / 4096))
    copies[3].wait()
    proj = jnp.zeros((2 * TOK, 384), F32)
    for h in range(0, 32, 2):
        pair = [
            both_rows(held[i].astype(F32), probe_ref[i].astype(F32), recip, d_recip, gain[i])
            for i in (h, h + 1)
        ]
        rows = jnp.concatenate([maps[h], maps[h + 1]], axis=0)
        proj = proj + dot(jnp.concatenate(pair, axis=1), rows)
    datt_ref[...] = attend_tangent(proj[:TOK], proj[TOK:], q_gain[...], k_gain[...])[1]


def second_kernel(
    meta, own, oth, probe, maps_hbm, gain, q_gain, k_gain, datt1, both_ref, maps, sem
):
    core = meta[0]
    copies = fetch(sem, (maps_hbm, maps))
    squares = jnp.zeros((TOK, 128), F32)
    dots = jnp.zeros((TOK, 128), F32)
    for side, b, h in blocks(core, own, oth):
        for i in range(2):
            x = side[b + i].astype(F32)
            squares = squares + x * x
            dots = dots + x * probe[h + 8 * i].astype(F32)
    recip = lax.rsqrt(row_sum(squares) * (1.0 / 4096) + EPS)
    d_recip = -(recip * recip * recip) * (row_sum(dots) * (1.0 / 4096))
    copies[0].wait()
    proj = jnp.zeros((2 * TOK, 384), F32)
    for side, b, h in blocks(core, own, oth):
        pair = [
            both_rows(
                side[b + i].astype(F32), probe[h + 8 * i].astype(F32), recip, d_recip, gain[h + 8 * i]
            )
            for i in range(2)
        ]
        rows = jnp.concatenate([maps[h], maps[h + 8]], axis=0)
        proj = proj + dot(jnp.concatenate(pair, axis=1), rows)
    att, d_att = attend_tangent(proj[:TOK], proj[TOK:], q_gain[...], k_gain[...])
    d_both = (d_att + datt1[...]).astype(BF)
    for i in range(4):
        both_ref[i, :TOK] = att
        both_ref[i, TOK:] = d_both


def last_kernel(
    meta, own, oth, r0, r1, r2, r3, gates, vel_hbm, probe_hbm, out_ref, rows, vel1, probe, sem
):
    core, slab = meta[0], meta[3]
    place_y = [(meta[2] - shift) & 3 for shift in SHIFTS]
    columns = [slab * 8 + y * 2 + core for y in place_y]
    copies = fetch(
        sem,
        *[(r, rows.at[i]) for i, r in enumerate((r0, r1, r2, r3))],
        (vel_hbm, vel1),
        *[(probe_hbm.at[column], probe.at[i]) for i, column in enumerate(columns)],
    )
    row = lax.broadcasted_iota(jnp.int32, (256, TOK), 0)
    token = lax.broadcasted_iota(jnp.int32, (256, TOK), 1)
    hit = (token == (row >> 3) * 6 + (row & 7)) & ((row & 7) < 6)
    lay = jnp.where(hit, jnp.ones((256, TOK), F32), jnp.zeros((256, TOK), F32)).astype(BF)
    for copy in copies:
        copy.wait()
    trace = jnp.zeros((1, 128), F32)
    laid = []
    for i, mapped in plane_products(core, own, oth, rows):
        mapped = mapped * gates[columns[i]]
        terms = mapped[TOK:] * probe[i].astype(F32)
        trace = trace + jnp.sum(terms, axis=0, keepdims=True)
        part = mapped[:TOK]
        if i == 0:
            part = part + vel1[...].astype(F32)
        laid.append(dot(lay, part.astype(BF)))
    trace = row_sum(trace)
    high = trace.astype(BF).astype(F32)
    mid = (trace - high).astype(BF).astype(F32)
    low = trace - high - mid
    lane = lax.broadcasted_iota(jnp.int32, (1, 128), 1)
    coded = jnp.where(lane == 0, high, jnp.where(lane == 1, mid, jnp.where(lane == 2, low, 0.0)))
    slot = lax.broadcasted_iota(jnp.int32, (256, 128), 0) & 7
    for i in range(4):
        block = jnp.where(slot == 6, coded, laid[i]) if i == 0 else laid[i]
        out_ref[:, pl.ds(pl.multiple_of(place_y[i] * 128, 128), 128)] = block.astype(BF)


def land_kernel(got, state, next_ref, change_ref):
    total = jnp.zeros((8, 512), F32)
    for z in range(4):
        for c in range(2):
            sums = jnp.zeros((8, 512), F32)
            for y in range(4):
                block = got[z * 8 + y * 2 + c].astype(F32)
                sums = sums + block
            total = total + sums
            for y in range(4):
                j = z * 8 + y * 2 + c
                cols = slice(j * 128, (j + 1) * 128)
                both = sums[:6, y * 128 : (y + 1) * 128]
                next_ref[:, cols] = (state[:, cols].astype(F32) + 0.5 * STEP * both).astype(BF)
    change_ref[...] = jnp.broadcast_to(-0.5 * STEP * row_sum(total[6:7, :]) / TOK, (1, 128))


def along_z(copies):
    n, rows, lanes = copies.shape
    return lax.all_to_all(copies.reshape(n * rows, lanes), "z", 0, 0, tiled=True)


def along_y(block):
    return lax.all_to_all(jnp.tile(block, (4, 1)), "y", 0, 0, tiled=True)


def swap(block):
    return lax.ppermute(block, "c", [(0, 1), (1, 0)])


def per_device(state, probe, norm_gain, head_maps, query_gain, key_gain, out_map, out_gate):
    place = lax.axis_index(SEQ)
    meta = [lax.axis_index("c"), place, lax.axis_index("y"), lax.axis_index("z")]
    meta = jnp.stack(meta).astype(jnp.int32)
    gates = out_gate.reshape(32, 1, 128)
    maps = head_maps.reshape(32, 128, 384)
    gain = norm_gain.reshape(32, 1, 128)

    packed_state, packed_probe, *sends = call(
        pack_kernel, [shape((4, 8, 3072)), shape((8, 6144))] + [shape((4, 256, 128))] * 4,
        1, meta, (state,), (probe,), (out_map.reshape(4, 4, 256, 128),),
        scratch=[pltpu.VMEM((6, 4096), BF), pltpu.VMEM((6, 4096), BF), sems(6)],
        vmem_mib=FULL,
    )
    probe_all = lax.all_gather(packed_probe, SEQ, axis=0, tiled=True)
    lines = along_z(packed_state)
    moved = [
        lax.ppermute(sends[k], "y", [(y, (y + k) % 4) for y in range(4)]) for k in (1, 3, 2)
    ]
    lines, moved[0], moved[1] = lax.optimization_barrier((lines, moved[0], moved[1]))
    plane_outs = [(piece.reshape(8, 128, 128),) for piece in (sends[0], *moved)]
    own = along_y(lines)
    oth = swap(own)
    att1, col = call(
        first_kernel, [shape((4, TOK, 128)), shape((TOK, 128))],
        1, meta, own, oth, (maps,), gain, query_gain, key_gain, scratch=[HELD, MAPS, sems(1)], vmem_mib=51,
    )
    own1 = along_z(att1)
    oth1 = swap(own1)
    parts = call(
        plane_kernel, shape((4, TOK, 128), F32),
        1, meta, own1.reshape(4, TOK, 128), oth1.reshape(4, TOK, 128), *plane_outs,
        scratch=[ROWS, sems(4)], vmem_mib=MIDDLE,
    )
    parts = lax.all_to_all(parts.reshape(4 * TOK, 128), "y", 0, 0, tiled=True)
    vel1, mid = call(
        middle_kernel, [shape((TOK, 128)), shape((4, TOK, 128))],
        1, meta, parts.reshape(4, TOK, 128), gates, col, vmem_mib=MIDDLE,
    )
    own_m = along_y(along_z(mid))
    probe_blocks, datt1 = call(
        tangent_kernel, [shape((32, TOK, 128)), shape((TOK, 128), F32)],
        1, meta, (own,), (oth,), (probe_all,), (maps,), gain, query_gain, key_gain, (mid,),
        scratch=[
            HELD, pltpu.VMEM((128, 3072), BF), pltpu.VMEM((128, 3072), BF),
            pltpu.VMEM((256, 3072), BF), MAPS, sems(4),
        ],
        vmem_mib=FULL,
    )
    own_m, datt1 = lax.optimization_barrier((own_m, datt1))
    oth_m = swap(own_m).reshape(16, TOK, 128)
    own_m = own_m.reshape(16, TOK, 128)
    both = call(
        second_kernel, shape((4, 2 * TOK, 128)),
        1, meta, own_m, oth_m, probe_blocks, (maps,), gain, query_gain, key_gain, datt1,
        scratch=[MAPS, sems(1)], vmem_mib=SECOND,
    )
    own2 = lax.all_to_all(both.reshape(8 * TOK, 128), "z", 0, 0, tiled=True)
    oth2 = swap(own2)
    columns = call(
        last_kernel, shape((256, 512)),
        1, meta, own2.reshape(4, 2 * TOK, 128), oth2.reshape(4, 2 * TOK, 128),
        *plane_outs, gates, (vel1,), (probe_blocks,),
        scratch=[
            ROWS, pltpu.VMEM((TOK, 128), BF),
            pltpu.VMEM((4, TOK, 128), BF), sems(9),
        ],
        vmem_mib=LAST,
    )
    got = lax.all_to_all(columns, SEQ, 0, 0, tiled=True).reshape(32, 8, 512)
    next_state, change = call(
        land_kernel, [shape((6, 4096)), shape((1, 128), F32)], 0, got, state
    )
    return next_state, change[0, :1]


def solution(mesh):
    split = Mesh(mesh.devices.reshape(4, 4, 2, 4, 4), ("z", "y", "c", "w", "x"))
    rows = P(("w", "x", "z", "y", "c"), None)
    return jax.shard_map(
        per_device,
        mesh=split,
        in_specs=(rows, rows, P(), P(SEQ, None, None), P(SEQ, None), P(SEQ, None), P(None, SEQ), P()),
        out_specs=(rows, P(("w", "x"))),
        check_vma=False,
    )
```

```python
import jax
import jax.numpy as jnp
from jax import lax
from jax.experimental import pallas as pl
from jax.experimental.pallas import tpu as pltpu
from jax.sharding import Mesh, PartitionSpec as P

EPS = 1e-06
STEP = 0.5
SEQ = ("z", "y", "c")
BF = jnp.bfloat16
F32 = jnp.float32
NT = (((1,), (1,)), ((), ()))
TOK = 192
SCALE = 128 ** (-0.5)


def dot(a, b):
    return jnp.dot(a, b, preferred_element_type=F32)


def dot_nt(a, b):
    return lax.dot_general(a, b, NT, preferred_element_type=F32)


def row_mean(v):
    return jnp.mean(v, axis=-1, keepdims=True)


HELD = pltpu.VMEM((32, TOK, 128), BF)
MAPS = pltpu.VMEM((32, 128, 384), BF)
ROWS = pltpu.VMEM((4, 8, 128, 128), BF)


FULL = 60
LAST = 51
MIDDLE = 51
SECOND = 51


def sems(n):
    return pltpu.SemaphoreType.DMA((n,))


def fetch(sem, *pairs):
    copies = [pltpu.make_async_copy(a, b, sem.at[i]) for i, (a, b) in enumerate(pairs)]
    for copy in copies:
        copy.start()
    return copies


def call(kernel, out_shape, placed, *args, scratch=(), vmem_mib=20, n_hbm=0):
    body = kernel
    if placed:

        def body(*refs):
            c, y, z = lax.axis_index("c"), lax.axis_index("y"), lax.axis_index("z")
            return kernel((c, z * 8 + y * 2 + c, y, z), *refs)

    in_specs = []
    for a in args:
        if isinstance(a, tuple):
            in_specs.append(pl.BlockSpec(memory_space=pltpu.HBM))
        else:
            in_specs.append(pl.BlockSpec(memory_space=pltpu.VMEM))
    flat = [a[0] if isinstance(a, tuple) else a for a in args]
    multi = isinstance(out_shape, (tuple, list))
    vmem = pl.BlockSpec(memory_space=pltpu.VMEM)
    hbm = pl.BlockSpec(memory_space=pltpu.HBM)
    return pl.pallas_call(
        body,
        out_shape=out_shape,
        in_specs=in_specs,
        out_specs=[vmem] * (len(out_shape) - n_hbm) + [hbm] * n_hbm if multi else vmem,
        scratch_shapes=scratch,
        compiler_params=pltpu.CompilerParams(vmem_limit_bytes=vmem_mib * 1024 * 1024),
    )(*flat)


def shape(dims, kind=BF):
    return jax.ShapeDtypeStruct(dims, kind)


def selectors(first_row_token, rows):
    packed = lax.broadcasted_iota(jnp.int32, (TOK, rows), 1)
    token = lax.broadcasted_iota(jnp.int32, (TOK, rows), 0)
    slot = packed & 7
    base = first_row_token(packed)
    one = jnp.ones((TOK, rows), F32)
    zero = jnp.zeros((TOK, rows), F32)
    main = jnp.where((token == base + slot) & (slot < 6), one, zero).astype(BF)
    rest = [
        jnp.where((token == base + m + 3 * (slot - 6)) & (slot >= 6), one, zero).astype(BF)
        for m in range(3)
    ]
    return main, rest


def pieces(main, rest, chunk_of):
    tail = None
    for m in range(3):
        chunk = chunk_of(m)
        part = dot(rest[m], chunk)
        tail = part if tail is None else tail + part
        yield m * 1024, dot(main, chunk)
    yield 3072, tail


def qkv_norm(proj, q_gain, k_gain):
    query, key, val = proj[:, :128], proj[:, 128:256], proj[:, 256:]
    rq = lax.rsqrt(row_mean(query * query) + EPS)
    rk = lax.rsqrt(row_mean(key * key) + EPS)
    qn = (query * rq * q_gain).astype(BF)
    kn = (key * rk * k_gain).astype(BF)
    return query, key, rq, rk, qn, kn, val.astype(BF)


def probabilities(qn, kn):
    expo = jnp.exp(dot_nt(qn, kn) * SCALE)
    return expo / jnp.sum(expo, axis=-1, keepdims=True)


def attend(proj, q_gain, k_gain):
    _, _, _, _, qn, kn, val = qkv_norm(proj, q_gain, k_gain)
    return dot(probabilities(qn, kn).astype(BF), val).astype(BF)


def attend_tangent(proj, d_proj, q_gain, k_gain):
    query, key, rq, rk, qn, kn, val = qkv_norm(proj, q_gain, k_gain)
    dq, dk, dv = d_proj[:, :128], d_proj[:, 128:256], d_proj[:, 256:].astype(BF)
    drq = -(rq * rq * rq) * row_mean(query * dq)
    drk = -(rk * rk * rk) * row_mean(key * dk)
    dqn = ((dq * rq + query * drq) * q_gain).astype(BF)
    dkn = ((dk * rk + key * drk) * k_gain).astype(BF)
    probs = probabilities(qn, kn)
    ds = (dot_nt(dqn, kn) + dot_nt(qn, dkn)) * SCALE
    d_probs = probs * (ds - jnp.sum(probs * ds, axis=-1, keepdims=True))
    probs = probs.astype(BF)
    return dot(probs, val).astype(BF), dot(d_probs.astype(BF), val) + dot(probs, dv)


def pack_kernel(
    meta, state_hbm, probe_hbm, out_map, state_ref, probe_ref, s0, s1, s2, s3, state, probe, sem
):
    shifted = [(out_map.at[:, (meta[2] + k) & 3], to) for k, to in enumerate((s0, s1, s2, s3))]
    copies = fetch(sem, (state_hbm, state), (probe_hbm, probe), *shifted)
    for i, (source, write) in enumerate(((state, None), (probe, probe_ref))):
        copies[i].wait()
        main = source[:, :3072]
        sixth = jnp.concatenate([source[q : q + 1, 3072:] for q in range(3)], axis=1)
        seventh = jnp.concatenate([source[q : q + 1, 3072:] for q in range(3, 6)], axis=1)
        whole = jnp.concatenate([main, sixth, seventh], axis=0)
        if write is None:
            for n in range(4):
                state_ref[n] = whole
        else:
            write[:, :3072] = whole
            write[:, 3072:] = whole[:, :1024]
    for copy in copies[2:]:
        copy.wait()


def core_order(core):
    def first_token(packed):
        inner = packed & 127
        z = (inner >> 3) & 3
        y = inner >> 5
        c = jnp.where((packed >> 7) == 0, core, 1 - core)
        return (z * 8 + y * 2 + c) * 6

    return first_token


def unpack_state(core, xa, xb, held):
    main, rest = selectors(core_order(core), 256)
    squares = jnp.zeros((TOK, 128), F32)

    def chunk_of(m):
        cols = slice(m * 1024, (m + 1) * 1024)
        return jnp.concatenate([xa[:, cols], xb[:, cols]], axis=0)

    for start, x in pieces(main, rest, chunk_of):
        for b in range(8):
            piece = x[:, b * 128 : (b + 1) * 128]
            squares = squares + piece * piece
            held[start // 128 + b] = piece.astype(BF)
    return lax.rsqrt(row_sum(squares) * (1.0 / 4096) + EPS)


def row_sum(v):
    return jnp.sum(v, axis=-1, keepdims=True)


def first_kernel(
    meta, xa, xb, maps_hbm, gain, q_gain, k_gain, att_ref, col_ref, held, maps, sem
):
    copies = fetch(sem, (maps_hbm, maps))
    recip = unpack_state(meta[0], xa, xb, held)
    copies[0].wait()
    proj = jnp.zeros((TOK, 384), F32)
    for h in range(0, 32, 2):
        left = (held[h].astype(F32) * recip * gain[h]).astype(BF)
        right = (held[h + 1].astype(F32) * recip * gain[h + 1]).astype(BF)
        rows = jnp.concatenate([maps[h], maps[h + 1]], axis=0)
        proj = proj + dot(jnp.concatenate([left, right], axis=1), rows)
    att = attend(proj, q_gain[...], k_gain[...])
    for i in range(4):
        att_ref[i] = att
    col_ref[...] = held[meta[1]]


def blocks(core, own, oth):
    for side, c in ((own, core), (oth, 1 - core)):
        for y in range(4):
            for z in (0, 2):
                yield side, y * 4 + z, z * 8 + y * 2 + c


SHIFTS = (0, 1, 3, 2)


def plane_products(core, own, oth, rows):
    left = []
    for z in range(4):
        mine, other = own[z], oth[z]
        first = jnp.where(core == 0, mine, other)
        second = jnp.where(core == 0, other, mine)
        left.append(jnp.concatenate([first, second], axis=1))
    for i in range(4):
        mapped = None
        for z in range(4):
            right = jnp.concatenate([rows[i, z * 2], rows[i, z * 2 + 1]], axis=0)
            part = dot(left[z], right)
            mapped = part if mapped is None else mapped + part
        yield i, mapped


def plane_kernel(meta, own, oth, r0, r1, r2, r3, part_ref, rows, sem):
    copies = fetch(sem, *[(r, rows.at[i]) for i, r in enumerate((r0, r1, r2, r3))])
    for copy in copies:
        copy.wait()
    for i, mapped in plane_products(meta[0], own, oth, rows):
        part_ref[(meta[2] - SHIFTS[i]) & 3] = mapped


def middle_kernel(meta, parts, gates, col, vel_ref, mid_ref):
    total = (parts[0] + parts[1]) + (parts[2] + parts[3])
    vel = (gates[meta[1]] * total).astype(BF)
    vel_ref[...] = vel
    mid = (col[...].astype(F32) + STEP * vel.astype(F32)).astype(BF)
    for i in range(4):
        mid_ref[i] = mid


def both_rows(x, probe, recip, d_recip, gain):
    normed = (x * recip * gain).astype(BF)
    d_normed = ((probe * recip + x * d_recip) * gain).astype(BF)
    return jnp.concatenate([normed, d_normed], axis=0)


def tangent_kernel(
    meta, xa_hbm, xb_hbm, packed_hbm, maps_hbm, gain, q_gain, k_gain, after, probe_ref, datt_ref,
    held, xa, xb, packed, maps, sem,
):
    copies = fetch(
        sem, (xa_hbm, xa), (xb_hbm, xb), (packed_hbm.at[:, :3072], packed), (maps_hbm, maps)
    )
    copies[0].wait()
    copies[1].wait()
    recip = unpack_state(meta[0], xa, xb, held)
    main, rest = selectors(lambda row: (row >> 3) * 6, 256)
    copies[2].wait()
    dots = jnp.zeros((TOK, 128), F32)
    for start, x in pieces(main, rest, lambda m: packed[:, m * 1024 : (m + 1) * 1024]):
        for b in range(8):
            piece = x[:, b * 128 : (b + 1) * 128]
            dots = dots + piece * held[start // 128 + b].astype(F32)
            probe_ref[start // 128 + b] = piece.astype(BF)
    d_recip = -(recip * recip * recip) * (row_sum(dots) * (1.0 / 4096))
    copies[3].wait()
    proj = jnp.zeros((2 * TOK, 384), F32)
    for h in range(0, 32, 2):
        pair = [
            both_rows(held[i].astype(F32), probe_ref[i].astype(F32), recip, d_recip, gain[i])
            for i in (h, h + 1)
        ]
        rows = jnp.concatenate([maps[h], maps[h + 1]], axis=0)
        proj = proj + dot(jnp.concatenate(pair, axis=1), rows)
    datt_ref[...] = attend_tangent(proj[:TOK], proj[TOK:], q_gain[...], k_gain[...])[1]


def second_kernel(
    meta, own, oth, probe, maps_hbm, gain, q_gain, k_gain, datt_hbm, both_ref, maps, datt1, sem
):
    core = meta[0]
    copies = fetch(sem, (maps_hbm, maps), (datt_hbm, datt1))
    squares = jnp.zeros((TOK, 128), F32)
    dots = jnp.zeros((TOK, 128), F32)
    for side, b, h in blocks(core, own, oth):
        for i in range(2):
            x = side[b + i].astype(F32)
            squares = squares + x * x
            dots = dots + x * probe[h + 8 * i].astype(F32)
    recip = lax.rsqrt(row_sum(squares) * (1.0 / 4096) + EPS)
    d_recip = -(recip * recip * recip) * (row_sum(dots) * (1.0 / 4096))
    copies[0].wait()
    proj = jnp.zeros((2 * TOK, 384), F32)
    for side, b, h in blocks(core, own, oth):
        pair = [
            both_rows(
                side[b + i].astype(F32), probe[h + 8 * i].astype(F32), recip, d_recip, gain[h + 8 * i]
            )
            for i in range(2)
        ]
        rows = jnp.concatenate([maps[h], maps[h + 8]], axis=0)
        proj = proj + dot(jnp.concatenate(pair, axis=1), rows)
    att, d_att = attend_tangent(proj[:TOK], proj[TOK:], q_gain[...], k_gain[...])
    copies[1].wait()
    d_both = (d_att + datt1[...]).astype(BF)
    for i in range(4):
        both_ref[i, :TOK] = att
        both_ref[i, TOK:] = d_both


def last_kernel(
    meta, own, oth, r0, r1, r2, r3, gates, vel_hbm, probe_hbm, out_ref, rows, vel1, probe, sem
):
    core, slab = meta[0], meta[3]
    place_y = [(meta[2] - shift) & 3 for shift in SHIFTS]
    columns = [slab * 8 + y * 2 + core for y in place_y]
    copies = fetch(
        sem,
        *[(r, rows.at[i]) for i, r in enumerate((r0, r1, r2, r3))],
        (vel_hbm, vel1),
        *[(probe_hbm.at[column], probe.at[i]) for i, column in enumerate(columns)],
    )
    row = lax.broadcasted_iota(jnp.int32, (256, TOK), 0)
    token = lax.broadcasted_iota(jnp.int32, (256, TOK), 1)
    hit = (token == (row >> 3) * 6 + (row & 7)) & ((row & 7) < 6)
    lay = jnp.where(hit, jnp.ones((256, TOK), F32), jnp.zeros((256, TOK), F32)).astype(BF)
    for copy in copies:
        copy.wait()
    trace = jnp.zeros((1, 128), F32)
    laid = []
    for i, mapped in plane_products(core, own, oth, rows):
        mapped = mapped * gates[columns[i]]
        terms = mapped[TOK:] * probe[i].astype(F32)
        trace = trace + jnp.sum(terms, axis=0, keepdims=True)
        part = mapped[:TOK]
        if i == 0:
            part = part + vel1[...].astype(F32)
        laid.append(dot(lay, part.astype(BF)))
    trace = row_sum(trace)
    high = trace.astype(BF).astype(F32)
    mid = (trace - high).astype(BF).astype(F32)
    low = trace - high - mid
    lane = lax.broadcasted_iota(jnp.int32, (1, 128), 1)
    coded = jnp.where(lane == 0, high, jnp.where(lane == 1, mid, jnp.where(lane == 2, low, 0.0)))
    slot = lax.broadcasted_iota(jnp.int32, (256, 128), 0) & 7
    for i in range(4):
        block = jnp.where(slot == 6, coded, laid[i]) if i == 0 else laid[i]
        out_ref[:, pl.ds(pl.multiple_of(place_y[i] * 128, 128), 128)] = block.astype(BF)


def land_kernel(got, state, next_ref, change_ref):
    total = jnp.zeros((8, 512), F32)
    for z in range(4):
        for c in range(2):
            sums = jnp.zeros((8, 512), F32)
            for y in range(4):
                block = got[z * 8 + y * 2 + c].astype(F32)
                sums = sums + block
            total = total + sums
            for y in range(4):
                j = z * 8 + y * 2 + c
                cols = slice(j * 128, (j + 1) * 128)
                both = sums[:6, y * 128 : (y + 1) * 128]
                next_ref[:, cols] = (state[:, cols].astype(F32) + 0.5 * STEP * both).astype(BF)
    change_ref[...] = jnp.broadcast_to(-0.5 * STEP * row_sum(total[6:7, :]) / TOK, (1, 128))


def along_z(copies):
    n, rows, lanes = copies.shape
    return lax.all_to_all(copies.reshape(n * rows, lanes), "z", 0, 0, tiled=True)


def along_y(block):
    return lax.all_to_all(jnp.tile(block, (4, 1)), "y", 0, 0, tiled=True)


def swap(block):
    return lax.ppermute(block, "c", [(0, 1), (1, 0)])


def per_device(state, probe, norm_gain, head_maps, query_gain, key_gain, out_map, out_gate):
    gates = out_gate.reshape(32, 1, 128)
    maps = head_maps.reshape(32, 128, 384)
    gain = norm_gain.reshape(32, 1, 128)

    packed_state, packed_probe, *sends = call(
        pack_kernel, [shape((4, 8, 3072)), shape((8, 4096))] + [shape((4, 256, 128))] * 4,
        True, (state,), (probe,), (out_map.reshape(4, 4, 256, 128),),
        scratch=[pltpu.VMEM((6, 4096), BF), pltpu.VMEM((6, 4096), BF), sems(6)],
        vmem_mib=FULL,
    )
    probe_all = lax.all_gather(packed_probe, SEQ, axis=0, tiled=True)
    lines = along_z(packed_state)
    moved = [
        lax.ppermute(sends[k], "y", [(y, (y + k) % 4) for y in range(4)]) for k in (1, 3, 2)
    ]
    lines, moved[0] = lax.optimization_barrier((lines, moved[0]))
    own = along_y(lines)
    oth = swap(own)
    att1, col = call(
        first_kernel, [shape((4, TOK, 128)), shape((TOK, 128))],
        True, own, oth, (maps,), gain, query_gain, key_gain, scratch=[HELD, MAPS, sems(1)], vmem_mib=51,
    )
    att1, moved[1] = lax.optimization_barrier((att1, moved[1]))
    plane_outs = [(piece.reshape(8, 128, 128),) for piece in (sends[0], *moved)]
    own1 = along_z(att1)
    oth1 = swap(own1)
    parts = call(
        plane_kernel, shape((4, TOK, 128), F32),
        True, own1.reshape(4, TOK, 128), oth1.reshape(4, TOK, 128), *plane_outs,
        scratch=[ROWS, sems(4)], vmem_mib=MIDDLE,
    )
    parts = lax.all_to_all(parts.reshape(4 * TOK, 128), "y", 0, 0, tiled=True)
    vel1, mid = call(
        middle_kernel, [shape((TOK, 128)), shape((4, TOK, 128))],
        True, parts.reshape(4, TOK, 128), gates, col, vmem_mib=MIDDLE,
    )
    own_m = along_y(along_z(mid))
    probe_blocks, datt1 = call(
        tangent_kernel, [shape((32, TOK, 128)), shape((TOK, 128), F32)],
        True, (own,), (oth,), (probe_all,), (maps,), gain, query_gain, key_gain, (mid,),
        scratch=[
            HELD, pltpu.VMEM((128, 3072), BF), pltpu.VMEM((128, 3072), BF),
            pltpu.VMEM((256, 3072), BF), MAPS, sems(4),
        ],
        vmem_mib=FULL,
    )
    own_m, datt1 = lax.optimization_barrier((own_m, datt1))
    oth_m = swap(own_m).reshape(16, TOK, 128)
    own_m = own_m.reshape(16, TOK, 128)
    both = call(
        second_kernel, shape((4, 2 * TOK, 128)),
        True, own_m, oth_m, probe_blocks, (maps,), gain, query_gain, key_gain, (datt1,),
        scratch=[MAPS, pltpu.VMEM((TOK, 128), F32), sems(2)], vmem_mib=SECOND,
    )
    own2 = lax.all_to_all(both.reshape(8 * TOK, 128), "z", 0, 0, tiled=True)
    oth2 = swap(own2)
    columns = call(
        last_kernel, shape((256, 512)),
        True, own2.reshape(4, 2 * TOK, 128), oth2.reshape(4, 2 * TOK, 128),
        *plane_outs, gates, (vel1,), (probe_blocks,),
        scratch=[
            ROWS, pltpu.VMEM((TOK, 128), BF),
            pltpu.VMEM((4, TOK, 128), BF), sems(9),
        ],
        vmem_mib=LAST,
    )
    got = lax.all_to_all(columns, SEQ, 0, 0, tiled=True).reshape(32, 8, 512)
    next_state, change = call(
        land_kernel, [shape((6, 4096)), shape((1, 128), F32)], False, got, state
    )
    return next_state, change[0, :1]


def solution(mesh):
    split = Mesh(mesh.devices.reshape(4, 4, 2, 4, 4), ("z", "y", "c", "w", "x"))
    rows = P(("w", "x", "z", "y", "c"), None)
    return jax.shard_map(
        per_device,
        mesh=split,
        in_specs=(rows, rows, P(), P(SEQ, None, None), P(SEQ, None), P(SEQ, None), P(None, SEQ), P()),
        out_specs=(rows, P(("w", "x"))),
        check_vma=False,
    )
```

```python
import jax
import jax.numpy as jnp
from jax import lax
from jax.experimental import pallas as pl
from jax.experimental.pallas import tpu as pltpu
from jax.sharding import Mesh, PartitionSpec as P

EPS = 1e-06
STEP = 0.5
SEQ = ("z", "y", "c")
BF = jnp.bfloat16
F32 = jnp.float32
NT = (((1,), (1,)), ((), ()))
TOK = 192
SCALE = 128 ** (-0.5)


def dot(a, b):
    return jnp.dot(a, b, preferred_element_type=F32)


def dot_nt(a, b):
    return lax.dot_general(a, b, NT, preferred_element_type=F32)


def row_mean(v):
    return jnp.mean(v, axis=-1, keepdims=True)


HELD = pltpu.VMEM((32, TOK, 128), BF)
MAPS = pltpu.VMEM((32, 128, 384), BF)
ROWS = pltpu.VMEM((4, 8, 128, 128), BF)


FULL = 60
LAST = 51
MIDDLE = 51
SECOND = 51


def sems(n):
    return pltpu.SemaphoreType.DMA((n,))


def fetch(sem, *pairs):
    copies = [pltpu.make_async_copy(a, b, sem.at[i]) for i, (a, b) in enumerate(pairs)]
    for copy in copies:
        copy.start()
    return copies


def call(kernel, out_shape, placed, *args, scratch=(), vmem_mib=20, n_hbm=0):
    body = kernel
    if placed:

        def body(*refs):
            c, y, z = lax.axis_index("c"), lax.axis_index("y"), lax.axis_index("z")
            return kernel((c, z * 8 + y * 2 + c, y, z), *refs)

    in_specs = []
    for a in args:
        if isinstance(a, tuple):
            in_specs.append(pl.BlockSpec(memory_space=pltpu.HBM))
        else:
            in_specs.append(pl.BlockSpec(memory_space=pltpu.VMEM))
    flat = [a[0] if isinstance(a, tuple) else a for a in args]
    multi = isinstance(out_shape, (tuple, list))
    vmem = pl.BlockSpec(memory_space=pltpu.VMEM)
    hbm = pl.BlockSpec(memory_space=pltpu.HBM)
    return pl.pallas_call(
        body,
        out_shape=out_shape,
        in_specs=in_specs,
        out_specs=[vmem] * (len(out_shape) - n_hbm) + [hbm] * n_hbm if multi else vmem,
        scratch_shapes=scratch,
        compiler_params=pltpu.CompilerParams(vmem_limit_bytes=vmem_mib * 1024 * 1024),
    )(*flat)


def shape(dims, kind=BF):
    return jax.ShapeDtypeStruct(dims, kind)


def selectors(first_row_token, rows):
    packed = lax.broadcasted_iota(jnp.int32, (TOK, rows), 1)
    token = lax.broadcasted_iota(jnp.int32, (TOK, rows), 0)
    slot = packed & 7
    base = first_row_token(packed)
    one = jnp.ones((TOK, rows), F32)
    zero = jnp.zeros((TOK, rows), F32)
    main = jnp.where((token == base + slot) & (slot < 6), one, zero).astype(BF)
    rest = [
        jnp.where((token == base + m + 3 * (slot - 6)) & (slot >= 6), one, zero).astype(BF)
        for m in range(3)
    ]
    return main, rest


def pieces(main, rest, chunk_of):
    tail = None
    for m in range(3):
        chunk = chunk_of(m)
        part = dot(rest[m], chunk)
        tail = part if tail is None else tail + part
        yield m * 1024, dot(main, chunk)
    yield 3072, tail


def qkv_norm(proj, q_gain, k_gain):
    query, key, val = proj[:, :128], proj[:, 128:256], proj[:, 256:]
    rq = lax.rsqrt(row_mean(query * query) + EPS)
    rk = lax.rsqrt(row_mean(key * key) + EPS)
    qn = (query * rq * q_gain).astype(BF)
    kn = (key * rk * k_gain).astype(BF)
    return query, key, rq, rk, qn, kn, val.astype(BF)


def probabilities(qn, kn):
    expo = jnp.exp(dot_nt(qn, kn) * SCALE)
    return expo / jnp.sum(expo, axis=-1, keepdims=True)


def attend(proj, q_gain, k_gain):
    _, _, _, _, qn, kn, val = qkv_norm(proj, q_gain, k_gain)
    return dot(probabilities(qn, kn).astype(BF), val).astype(BF)


def attend_tangent(proj, d_proj, q_gain, k_gain):
    query, key, rq, rk, qn, kn, val = qkv_norm(proj, q_gain, k_gain)
    dq, dk, dv = d_proj[:, :128], d_proj[:, 128:256], d_proj[:, 256:].astype(BF)
    drq = -(rq * rq * rq) * row_mean(query * dq)
    drk = -(rk * rk * rk) * row_mean(key * dk)
    dqn = ((dq * rq + query * drq) * q_gain).astype(BF)
    dkn = ((dk * rk + key * drk) * k_gain).astype(BF)
    probs = probabilities(qn, kn)
    ds = (dot_nt(dqn, kn) + dot_nt(qn, dkn)) * SCALE
    d_probs = probs * (ds - jnp.sum(probs * ds, axis=-1, keepdims=True))
    probs = probs.astype(BF)
    return dot(probs, val).astype(BF), dot(d_probs.astype(BF), val) + dot(probs, dv)


def pack_kernel(
    meta, state_hbm, probe_hbm, out_map, state_ref, probe_ref, s0, s1, s2, s3, state, probe, sem
):
    shifted = [(out_map.at[:, (meta[2] + k) & 3], to) for k, to in enumerate((s0, s1, s2, s3))]
    copies = fetch(sem, (state_hbm, state), (probe_hbm, probe), *shifted)
    for i, (source, write) in enumerate(((state, None), (probe, probe_ref))):
        copies[i].wait()
        main = source[:, :3072]
        sixth = jnp.concatenate([source[q : q + 1, 3072:] for q in range(3)], axis=1)
        seventh = jnp.concatenate([source[q : q + 1, 3072:] for q in range(3, 6)], axis=1)
        whole = jnp.concatenate([main, sixth, seventh], axis=0)
        if write is None:
            for n in range(4):
                state_ref[n] = whole
        else:
            write[:, :3072] = whole
            write[:, 3072:] = whole[:, :1024]
    for copy in copies[2:]:
        copy.wait()


def core_order(core):
    def first_token(packed):
        inner = packed & 127
        z = (inner >> 3) & 3
        y = inner >> 5
        c = jnp.where((packed >> 7) == 0, core, 1 - core)
        return (z * 8 + y * 2 + c) * 6

    return first_token


def unpack_state(core, xa, xb, held):
    main, rest = selectors(core_order(core), 256)
    squares = jnp.zeros((TOK, 128), F32)

    def chunk_of(m):
        cols = slice(m * 1024, (m + 1) * 1024)
        return jnp.concatenate([xa[:, cols], xb[:, cols]], axis=0)

    for start, x in pieces(main, rest, chunk_of):
        for b in range(8):
            piece = x[:, b * 128 : (b + 1) * 128]
            squares = squares + piece * piece
            held[start // 128 + b] = piece.astype(BF)
    return lax.rsqrt(row_sum(squares) * (1.0 / 4096) + EPS)


def row_sum(v):
    return jnp.sum(v, axis=-1, keepdims=True)


def first_kernel(
    meta, xa, xb, maps_hbm, gain, q_gain, k_gain, att_ref, col_ref, held, maps, sem
):
    copies = fetch(sem, (maps_hbm, maps))
    recip = unpack_state(meta[0], xa, xb, held)
    copies[0].wait()
    proj = jnp.zeros((TOK, 384), F32)
    for h in range(0, 32, 2):
        left = (held[h].astype(F32) * recip * gain[h]).astype(BF)
        right = (held[h + 1].astype(F32) * recip * gain[h + 1]).astype(BF)
        rows = jnp.concatenate([maps[h], maps[h + 1]], axis=0)
        proj = proj + dot(jnp.concatenate([left, right], axis=1), rows)
    att = attend(proj, q_gain[...], k_gain[...])
    for i in range(4):
        att_ref[i] = att
    col_ref[...] = held[meta[1]]


def blocks(core, own, oth):
    for side, c in ((own, core), (oth, 1 - core)):
        for y in range(4):
            for z in (0, 2):
                yield side, y * 4 + z, z * 8 + y * 2 + c


SHIFTS = (0, 1, 3, 2)


def plane_products(core, own, oth, rows):
    left = []
    for z in range(4):
        mine, other = own[z], oth[z]
        first = jnp.where(core == 0, mine, other)
        second = jnp.where(core == 0, other, mine)
        left.append(jnp.concatenate([first, second], axis=1))
    for i in range(4):
        mapped = None
        for z in range(4):
            right = jnp.concatenate([rows[i, z * 2], rows[i, z * 2 + 1]], axis=0)
            part = dot(left[z], right)
            mapped = part if mapped is None else mapped + part
        yield i, mapped


def plane_kernel(meta, own, oth, r0, r1, r2, r3, part_ref, rows, sem):
    copies = fetch(sem, *[(r, rows.at[i]) for i, r in enumerate((r0, r1, r2, r3))])
    for copy in copies:
        copy.wait()
    for i, mapped in plane_products(meta[0], own, oth, rows):
        part_ref[(meta[2] - SHIFTS[i]) & 3] = mapped


def middle_kernel(meta, parts, gates, col, vel_ref, mid_ref):
    total = (parts[0] + parts[1]) + (parts[2] + parts[3])
    vel = (gates[meta[1]] * total).astype(BF)
    vel_ref[...] = vel
    mid = (col[...].astype(F32) + STEP * vel.astype(F32)).astype(BF)
    for i in range(4):
        mid_ref[i] = mid


def both_rows(x, probe, recip, d_recip, gain):
    normed = (x * recip * gain).astype(BF)
    d_normed = ((probe * recip + x * d_recip) * gain).astype(BF)
    return jnp.concatenate([normed, d_normed], axis=0)


def tangent_kernel(
    meta, xa_hbm, xb_hbm, packed_hbm, maps_hbm, gain, q_gain, k_gain, after, probe_ref,
    held, xa, xb, packed, maps, sem,
):
    copies = fetch(
        sem, (xa_hbm, xa), (xb_hbm, xb), (packed_hbm.at[:, :3072], packed), (maps_hbm, maps)
    )
    copies[0].wait()
    copies[1].wait()
    recip = unpack_state(meta[0], xa, xb, held)
    main, rest = selectors(lambda row: (row >> 3) * 6, 256)
    copies[2].wait()
    dots = jnp.zeros((TOK, 128), F32)
    for start, x in pieces(main, rest, lambda m: packed[:, m * 1024 : (m + 1) * 1024]):
        for b in range(8):
            piece = x[:, b * 128 : (b + 1) * 128]
            dots = dots + piece * held[start // 128 + b].astype(F32)
            probe_ref[start // 128 + b] = piece.astype(BF)
    d_recip = -(recip * recip * recip) * (row_sum(dots) * (1.0 / 4096))
    copies[3].wait()
    proj = jnp.zeros((2 * TOK, 384), F32)
    for h in range(0, 32, 2):
        pair = [
            both_rows(held[i].astype(F32), probe_ref[i].astype(F32), recip, d_recip, gain[i])
            for i in (h, h + 1)
        ]
        rows = jnp.concatenate([maps[h], maps[h + 1]], axis=0)
        proj = proj + dot(jnp.concatenate(pair, axis=1), rows)
    d_att = attend_tangent(proj[:TOK], proj[TOK:], q_gain[...], k_gain[...])[1]
    high = d_att.astype(BF)
    probe_ref[32] = high
    probe_ref[33] = (d_att - high.astype(F32)).astype(BF)


def second_kernel(
    meta, own, oth, probe_hbm, maps_hbm, gain, q_gain, k_gain, both_ref, probe, maps, sem
):
    core = meta[0]
    copies = fetch(sem, (probe_hbm, probe), (maps_hbm, maps))
    squares = jnp.zeros((TOK, 128), F32)
    dots = jnp.zeros((TOK, 128), F32)
    for side, b, h in blocks(core, own, oth):
        for i in range(2):
            x = side[b + i].astype(F32)
            squares = squares + x * x
    copies[0].wait()
    for side, b, h in blocks(core, own, oth):
        for i in range(2):
            dots = dots + side[b + i].astype(F32) * probe[h + 8 * i].astype(F32)
    recip = lax.rsqrt(row_sum(squares) * (1.0 / 4096) + EPS)
    d_recip = -(recip * recip * recip) * (row_sum(dots) * (1.0 / 4096))
    copies[1].wait()
    proj = jnp.zeros((2 * TOK, 384), F32)
    for side, b, h in blocks(core, own, oth):
        pair = [
            both_rows(
                side[b + i].astype(F32), probe[h + 8 * i].astype(F32), recip, d_recip, gain[h + 8 * i]
            )
            for i in range(2)
        ]
        rows = jnp.concatenate([maps[h], maps[h + 8]], axis=0)
        proj = proj + dot(jnp.concatenate(pair, axis=1), rows)
    att, d_att = attend_tangent(proj[:TOK], proj[TOK:], q_gain[...], k_gain[...])
    d_first = probe[32].astype(F32) + probe[33].astype(F32)
    d_both = (d_att + d_first).astype(BF)
    for i in range(4):
        both_ref[i, :TOK] = att
        both_ref[i, TOK:] = d_both


def last_kernel(
    meta, own, oth, r0, r1, r2, r3, gates, vel_hbm, probe_hbm, out_ref, rows, vel1, probe, sem
):
    core, slab = meta[0], meta[3]
    place_y = [(meta[2] - shift) & 3 for shift in SHIFTS]
    columns = [slab * 8 + y * 2 + core for y in place_y]
    copies = fetch(
        sem,
        *[(r, rows.at[i]) for i, r in enumerate((r0, r1, r2, r3))],
        (vel_hbm, vel1),
        *[(probe_hbm.at[column], probe.at[i]) for i, column in enumerate(columns)],
    )
    row = lax.broadcasted_iota(jnp.int32, (256, TOK), 0)
    token = lax.broadcasted_iota(jnp.int32, (256, TOK), 1)
    hit = (token == (row >> 3) * 6 + (row & 7)) & ((row & 7) < 6)
    lay = jnp.where(hit, jnp.ones((256, TOK), F32), jnp.zeros((256, TOK), F32)).astype(BF)
    for copy in copies:
        copy.wait()
    trace = jnp.zeros((1, 128), F32)
    laid = []
    for i, mapped in plane_products(core, own, oth, rows):
        mapped = mapped * gates[columns[i]]
        terms = mapped[TOK:] * probe[i].astype(F32)
        trace = trace + jnp.sum(terms, axis=0, keepdims=True)
        part = mapped[:TOK]
        if i == 0:
            part = part + vel1[...].astype(F32)
        laid.append(dot(lay, part.astype(BF)))
    trace = row_sum(trace)
    high = trace.astype(BF).astype(F32)
    mid = (trace - high).astype(BF).astype(F32)
    low = trace - high - mid
    lane = lax.broadcasted_iota(jnp.int32, (1, 128), 1)
    coded = jnp.where(lane == 0, high, jnp.where(lane == 1, mid, jnp.where(lane == 2, low, 0.0)))
    slot = lax.broadcasted_iota(jnp.int32, (256, 128), 0) & 7
    for i in range(4):
        block = jnp.where(slot == 6, coded, laid[i]) if i == 0 else laid[i]
        out_ref[:, pl.ds(pl.multiple_of(place_y[i] * 128, 128), 128)] = block.astype(BF)


def land_kernel(got, state, next_ref, change_ref):
    total = jnp.zeros((8, 512), F32)
    for z in range(4):
        for c in range(2):
            sums = jnp.zeros((8, 512), F32)
            for y in range(4):
                block = got[z * 8 + y * 2 + c].astype(F32)
                sums = sums + block
            total = total + sums
            for y in range(4):
                j = z * 8 + y * 2 + c
                cols = slice(j * 128, (j + 1) * 128)
                both = sums[:6, y * 128 : (y + 1) * 128]
                next_ref[:, cols] = (state[:, cols].astype(F32) + 0.5 * STEP * both).astype(BF)
    change_ref[...] = jnp.broadcast_to(-0.5 * STEP * row_sum(total[6:7, :]) / TOK, (1, 128))


def along_z(copies):
    n, rows, lanes = copies.shape
    return lax.all_to_all(copies.reshape(n * rows, lanes), "z", 0, 0, tiled=True)


def along_y(block):
    return lax.all_to_all(jnp.tile(block, (4, 1)), "y", 0, 0, tiled=True)


def swap(block):
    return lax.ppermute(block, "c", [(0, 1), (1, 0)])


def per_device(state, probe, norm_gain, head_maps, query_gain, key_gain, out_map, out_gate):
    gates = out_gate.reshape(32, 1, 128)
    maps = head_maps.reshape(32, 128, 384)
    gain = norm_gain.reshape(32, 1, 128)

    packed_state, packed_probe, *sends = call(
        pack_kernel, [shape((4, 8, 3072)), shape((8, 4096))] + [shape((4, 256, 128))] * 4,
        True, (state,), (probe,), (out_map.reshape(4, 4, 256, 128),),
        scratch=[pltpu.VMEM((6, 4096), BF), pltpu.VMEM((6, 4096), BF), sems(6)],
        vmem_mib=FULL,
    )
    probe_all = lax.all_gather(packed_probe, SEQ, axis=0, tiled=True)
    lines = along_z(packed_state)
    moved = [
        lax.ppermute(sends[k], "y", [(y, (y + k) % 4) for y in range(4)]) for k in (1, 3, 2)
    ]
    lines, moved[0], moved[1] = lax.optimization_barrier((lines, moved[0], moved[1]))
    own = along_y(lines)
    oth = swap(own)
    att1, col = call(
        first_kernel, [shape((4, TOK, 128)), shape((TOK, 128))],
        True, own, oth, (maps,), gain, query_gain, key_gain, scratch=[HELD, MAPS, sems(1)], vmem_mib=51,
    )
    plane_outs = [(piece.reshape(8, 128, 128),) for piece in (sends[0], *moved)]
    own1 = along_z(att1)
    oth1 = swap(own1)
    parts = call(
        plane_kernel, shape((4, TOK, 128), F32),
        True, own1.reshape(4, TOK, 128), oth1.reshape(4, TOK, 128), *plane_outs,
        scratch=[ROWS, sems(4)], vmem_mib=MIDDLE,
    )
    parts = lax.all_to_all(parts.reshape(4 * TOK, 128), "y", 0, 0, tiled=True)
    vel1, mid = call(
        middle_kernel, [shape((TOK, 128)), shape((4, TOK, 128))],
        True, parts.reshape(4, TOK, 128), gates, col, vmem_mib=MIDDLE,
    )
    own_m = along_y(along_z(mid))
    probe_blocks = call(
        tangent_kernel, shape((34, TOK, 128)),
        True, (own,), (oth,), (probe_all,), (maps,), gain, query_gain, key_gain, (mid,),
        scratch=[
            HELD, pltpu.VMEM((128, 3072), BF), pltpu.VMEM((128, 3072), BF),
            pltpu.VMEM((256, 3072), BF), MAPS, sems(4),
        ],
        vmem_mib=FULL,
    )
    own_m, probe_blocks = lax.optimization_barrier((own_m, probe_blocks))
    oth_m = swap(own_m).reshape(16, TOK, 128)
    own_m = own_m.reshape(16, TOK, 128)
    both = call(
        second_kernel, shape((4, 2 * TOK, 128)),
        True, own_m, oth_m, (probe_blocks,), (maps,), gain, query_gain, key_gain,
        scratch=[pltpu.VMEM((34, TOK, 128), BF), MAPS, sems(2)], vmem_mib=SECOND,
    )
    own2 = lax.all_to_all(both.reshape(8 * TOK, 128), "z", 0, 0, tiled=True)
    oth2 = swap(own2)
    columns = call(
        last_kernel, shape((256, 512)),
        True, own2.reshape(4, 2 * TOK, 128), oth2.reshape(4, 2 * TOK, 128),
        *plane_outs, gates, (vel1,), (probe_blocks,),
        scratch=[
            ROWS, pltpu.VMEM((TOK, 128), BF),
            pltpu.VMEM((4, TOK, 128), BF), sems(9),
        ],
        vmem_mib=LAST,
    )
    got = lax.all_to_all(columns, SEQ, 0, 0, tiled=True).reshape(32, 8, 512)
    next_state, change = call(
        land_kernel, [shape((6, 4096)), shape((1, 128), F32)], False, got, state
    )
    return next_state, change[0, :1]


def solution(mesh):
    split = Mesh(mesh.devices.reshape(4, 4, 2, 4, 4), ("z", "y", "c", "w", "x"))
    rows = P(("w", "x", "z", "y", "c"), None)
    return jax.shard_map(
        per_device,
        mesh=split,
        in_specs=(rows, rows, P(), P(SEQ, None, None), P(SEQ, None), P(SEQ, None), P(None, SEQ), P()),
        out_specs=(rows, P(("w", "x"))),
        check_vma=False,
    )
```

```python
import jax
import jax.numpy as jnp
from jax import lax
from jax.experimental import pallas as pl
from jax.experimental.pallas import tpu as pltpu
from jax.sharding import Mesh, PartitionSpec as P

EPS = 1e-06
STEP = 0.5
SEQ = ("z", "y", "c")
BF = jnp.bfloat16
F32 = jnp.float32
NT = (((1,), (1,)), ((), ()))
TOK = 192
SCALE = 128 ** (-0.5)


def dot(a, b):
    return jnp.dot(a, b, preferred_element_type=F32)


def dot_nt(a, b):
    return lax.dot_general(a, b, NT, preferred_element_type=F32)


def row_mean(v):
    return jnp.mean(v, axis=-1, keepdims=True)


HELD = pltpu.VMEM((32, TOK, 128), BF)
MAPS = pltpu.VMEM((32, 128, 384), BF)
ROWS = pltpu.VMEM((4, 8, 128, 128), BF)


FULL = 60
LAST = 51
MIDDLE = 51
SECOND = 51


def sems(n):
    return pltpu.SemaphoreType.DMA((n,))


def fetch(sem, *pairs):
    copies = [pltpu.make_async_copy(a, b, sem.at[i]) for i, (a, b) in enumerate(pairs)]
    for copy in copies:
        copy.start()
    return copies


def call(kernel, out_shape, placed, *args, scratch=(), vmem_mib=20, n_hbm=0):
    body = kernel
    if placed:

        def body(*refs):
            c, y, z = lax.axis_index("c"), lax.axis_index("y"), lax.axis_index("z")
            return kernel((c, z * 8 + y * 2 + c, y, z), *refs)

    in_specs = []
    for a in args:
        if isinstance(a, tuple):
            in_specs.append(pl.BlockSpec(memory_space=pltpu.HBM))
        else:
            in_specs.append(pl.BlockSpec(memory_space=pltpu.VMEM))
    flat = [a[0] if isinstance(a, tuple) else a for a in args]
    multi = isinstance(out_shape, (tuple, list))
    vmem = pl.BlockSpec(memory_space=pltpu.VMEM)
    hbm = pl.BlockSpec(memory_space=pltpu.HBM)
    return pl.pallas_call(
        body,
        out_shape=out_shape,
        in_specs=in_specs,
        out_specs=[vmem] * (len(out_shape) - n_hbm) + [hbm] * n_hbm if multi else vmem,
        scratch_shapes=scratch,
        compiler_params=pltpu.CompilerParams(vmem_limit_bytes=vmem_mib * 1024 * 1024),
    )(*flat)


def shape(dims, kind=BF):
    return jax.ShapeDtypeStruct(dims, kind)


def selectors(first_row_token, rows):
    packed = lax.broadcasted_iota(jnp.int32, (TOK, rows), 1)
    token = lax.broadcasted_iota(jnp.int32, (TOK, rows), 0)
    slot = packed & 7
    base = first_row_token(packed)
    one = jnp.ones((TOK, rows), F32)
    zero = jnp.zeros((TOK, rows), F32)
    main = jnp.where((token == base + slot) & (slot < 6), one, zero).astype(BF)
    rest = [
        jnp.where((token == base + m + 3 * (slot - 6)) & (slot >= 6), one, zero).astype(BF)
        for m in range(3)
    ]
    return main, rest


def pieces(main, rest, chunk_of):
    tail = None
    for m in range(3):
        chunk = chunk_of(m)
        part = dot(rest[m], chunk)
        tail = part if tail is None else tail + part
        yield m * 1024, dot(main, chunk)
    yield 3072, tail


def qkv_norm(proj, q_gain, k_gain):
    query, key, val = proj[:, :128], proj[:, 128:256], proj[:, 256:]
    rq = lax.rsqrt(row_mean(query * query) + EPS)
    rk = lax.rsqrt(row_mean(key * key) + EPS)
    qn = (query * rq * q_gain).astype(BF)
    kn = (key * rk * k_gain).astype(BF)
    return query, key, rq, rk, qn, kn, val.astype(BF)


def probabilities(qn, kn):
    expo = jnp.exp(dot_nt(qn, kn) * SCALE)
    return expo / jnp.sum(expo, axis=-1, keepdims=True)


def attend(proj, q_gain, k_gain):
    _, _, _, _, qn, kn, val = qkv_norm(proj, q_gain, k_gain)
    return dot(probabilities(qn, kn).astype(BF), val).astype(BF)


def attend_tangent(proj, d_proj, q_gain, k_gain):
    query, key, rq, rk, qn, kn, val = qkv_norm(proj, q_gain, k_gain)
    dq, dk, dv = d_proj[:, :128], d_proj[:, 128:256], d_proj[:, 256:].astype(BF)
    drq = -(rq * rq * rq) * row_mean(query * dq)
    drk = -(rk * rk * rk) * row_mean(key * dk)
    dqn = ((dq * rq + query * drq) * q_gain).astype(BF)
    dkn = ((dk * rk + key * drk) * k_gain).astype(BF)
    probs = probabilities(qn, kn)
    ds = (dot_nt(dqn, kn) + dot_nt(qn, dkn)) * SCALE
    d_probs = probs * (ds - jnp.sum(probs * ds, axis=-1, keepdims=True))
    probs = probs.astype(BF)
    return dot(probs, val).astype(BF), dot(d_probs.astype(BF), val) + dot(probs, dv)


def pack_kernel(
    meta, state_hbm, probe_hbm, out_map, state_ref, probe_ref, s0, s1, s2, s3, state, probe, sem
):
    shifted = [(out_map.at[:, (meta[2] + k) & 3], to) for k, to in enumerate((s0, s1, s2, s3))]
    copies = fetch(sem, (state_hbm, state), (probe_hbm, probe), *shifted)
    for i, (source, write) in enumerate(((state, None), (probe, probe_ref))):
        copies[i].wait()
        main = source[:, :3072]
        sixth = jnp.concatenate([source[q : q + 1, 3072:] for q in range(3)], axis=1)
        seventh = jnp.concatenate([source[q : q + 1, 3072:] for q in range(3, 6)], axis=1)
        whole = jnp.concatenate([main, sixth, seventh], axis=0)
        if write is None:
            for n in range(4):
                state_ref[n] = whole
        else:
            write[:, :3072] = whole
            write[:, 3072:] = whole[:, :1024]
    for copy in copies[2:]:
        copy.wait()


def core_order(core):
    def first_token(packed):
        inner = packed & 127
        z = (inner >> 3) & 3
        y = inner >> 5
        c = jnp.where((packed >> 7) == 0, core, 1 - core)
        return (z * 8 + y * 2 + c) * 6

    return first_token


def unpack_state(core, xa, xb, held):
    main, rest = selectors(core_order(core), 256)
    squares = jnp.zeros((TOK, 128), F32)

    def chunk_of(m):
        cols = slice(m * 1024, (m + 1) * 1024)
        return jnp.concatenate([xa[:, cols], xb[:, cols]], axis=0)

    for start, x in pieces(main, rest, chunk_of):
        for b in range(8):
            piece = x[:, b * 128 : (b + 1) * 128]
            squares = squares + piece * piece
            held[start // 128 + b] = piece.astype(BF)
    return lax.rsqrt(row_sum(squares) * (1.0 / 4096) + EPS)


def row_sum(v):
    return jnp.sum(v, axis=-1, keepdims=True)


def first_kernel(
    meta, xa, xb, maps_hbm, gain, q_gain, k_gain, att_ref, col_ref, held, maps, sem
):
    copies = fetch(sem, (maps_hbm, maps))
    recip = unpack_state(meta[0], xa, xb, held)
    copies[0].wait()
    proj = jnp.zeros((TOK, 384), F32)
    for h in range(0, 32, 2):
        left = (held[h].astype(F32) * recip * gain[h]).astype(BF)
        right = (held[h + 1].astype(F32) * recip * gain[h + 1]).astype(BF)
        rows = jnp.concatenate([maps[h], maps[h + 1]], axis=0)
        proj = proj + dot(jnp.concatenate([left, right], axis=1), rows)
    att = attend(proj, q_gain[...], k_gain[...])
    for i in range(4):
        att_ref[i] = att
    col_ref[...] = held[meta[1]]


def blocks(core, own, oth):
    for side, c in ((own, core), (oth, 1 - core)):
        for y in range(4):
            for z in (0, 2):
                yield side, y * 4 + z, z * 8 + y * 2 + c


SHIFTS = (0, 1, 3, 2)


def plane_products(core, own, oth, rows, copies):
    left = []
    for z in range(4):
        mine, other = own[z], oth[z]
        first = jnp.where(core == 0, mine, other)
        second = jnp.where(core == 0, other, mine)
        left.append(jnp.concatenate([first, second], axis=1))
    for i in range(4):
        copies[i].wait()
        mapped = None
        for z in range(4):
            right = jnp.concatenate([rows[i, z * 2], rows[i, z * 2 + 1]], axis=0)
            part = dot(left[z], right)
            mapped = part if mapped is None else mapped + part
        yield i, mapped


def plane_kernel(meta, own, oth, r0, r1, r2, r3, part_ref, rows, sem):
    copies = fetch(sem, *[(r, rows.at[i]) for i, r in enumerate((r0, r1, r2, r3))])
    for i, mapped in plane_products(meta[0], own, oth, rows, copies):
        part_ref[(meta[2] - SHIFTS[i]) & 3] = mapped


def middle_kernel(meta, parts, gates, col, vel_ref, mid_ref):
    total = (parts[0] + parts[1]) + (parts[2] + parts[3])
    vel = (gates[meta[1]] * total).astype(BF)
    vel_ref[...] = vel
    mid = (col[...].astype(F32) + STEP * vel.astype(F32)).astype(BF)
    for i in range(4):
        mid_ref[i] = mid


def both_rows(x, probe, recip, d_recip, gain):
    normed = (x * recip * gain).astype(BF)
    d_normed = ((probe * recip + x * d_recip) * gain).astype(BF)
    return jnp.concatenate([normed, d_normed], axis=0)


def tangent_kernel(
    meta, xa_hbm, xb_hbm, packed_hbm, maps_hbm, gain, q_gain, k_gain, after, probe_ref,
    held, xa, xb, packed, maps, sem,
):
    copies = fetch(
        sem, (xa_hbm, xa), (xb_hbm, xb), (packed_hbm.at[:, :3072], packed), (maps_hbm, maps)
    )
    copies[0].wait()
    copies[1].wait()
    recip = unpack_state(meta[0], xa, xb, held)
    main, rest = selectors(lambda row: (row >> 3) * 6, 256)
    copies[2].wait()
    dots = jnp.zeros((TOK, 128), F32)
    for start, x in pieces(main, rest, lambda m: packed[:, m * 1024 : (m + 1) * 1024]):
        for b in range(8):
            piece = x[:, b * 128 : (b + 1) * 128]
            dots = dots + piece * held[start // 128 + b].astype(F32)
            probe_ref[start // 128 + b] = piece.astype(BF)
    d_recip = -(recip * recip * recip) * (row_sum(dots) * (1.0 / 4096))
    copies[3].wait()
    proj = jnp.zeros((2 * TOK, 384), F32)
    for h in range(0, 32, 2):
        pair = [
            both_rows(held[i].astype(F32), probe_ref[i].astype(F32), recip, d_recip, gain[i])
            for i in (h, h + 1)
        ]
        rows = jnp.concatenate([maps[h], maps[h + 1]], axis=0)
        proj = proj + dot(jnp.concatenate(pair, axis=1), rows)
    d_att = attend_tangent(proj[:TOK], proj[TOK:], q_gain[...], k_gain[...])[1]
    high = d_att.astype(BF)
    probe_ref[32] = high
    probe_ref[33] = (d_att - high.astype(F32)).astype(BF)


def second_kernel(
    meta, own, oth, probe_hbm, maps_hbm, gain, q_gain, k_gain, both_ref, probe, maps, sem
):
    core = meta[0]
    copies = fetch(sem, (probe_hbm, probe), (maps_hbm, maps))
    squares = jnp.zeros((TOK, 128), F32)
    dots = jnp.zeros((TOK, 128), F32)
    for side, b, h in blocks(core, own, oth):
        for i in range(2):
            x = side[b + i].astype(F32)
            squares = squares + x * x
    copies[0].wait()
    for side, b, h in blocks(core, own, oth):
        for i in range(2):
            dots = dots + side[b + i].astype(F32) * probe[h + 8 * i].astype(F32)
    recip = lax.rsqrt(row_sum(squares) * (1.0 / 4096) + EPS)
    d_recip = -(recip * recip * recip) * (row_sum(dots) * (1.0 / 4096))
    copies[1].wait()
    proj = jnp.zeros((2 * TOK, 384), F32)
    for side, b, h in blocks(core, own, oth):
        pair = [
            both_rows(
                side[b + i].astype(F32), probe[h + 8 * i].astype(F32), recip, d_recip, gain[h + 8 * i]
            )
            for i in range(2)
        ]
        rows = jnp.concatenate([maps[h], maps[h + 8]], axis=0)
        proj = proj + dot(jnp.concatenate(pair, axis=1), rows)
    att, d_att = attend_tangent(proj[:TOK], proj[TOK:], q_gain[...], k_gain[...])
    d_first = probe[32].astype(F32) + probe[33].astype(F32)
    d_both = (d_att + d_first).astype(BF)
    for i in range(4):
        both_ref[i, :TOK] = att
        both_ref[i, TOK:] = d_both


def last_kernel(
    meta, own, oth, r0, r1, r2, r3, gates, vel_hbm, probe_hbm, out_ref, rows, vel1, probe, sem
):
    core, slab = meta[0], meta[3]
    place_y = [(meta[2] - shift) & 3 for shift in SHIFTS]
    columns = [slab * 8 + y * 2 + core for y in place_y]
    copies = fetch(
        sem,
        *[(r, rows.at[i]) for i, r in enumerate((r0, r1, r2, r3))],
        (vel_hbm, vel1),
        *[(probe_hbm.at[column], probe.at[i]) for i, column in enumerate(columns)],
    )
    row = lax.broadcasted_iota(jnp.int32, (256, TOK), 0)
    token = lax.broadcasted_iota(jnp.int32, (256, TOK), 1)
    hit = (token == (row >> 3) * 6 + (row & 7)) & ((row & 7) < 6)
    lay = jnp.where(hit, jnp.ones((256, TOK), F32), jnp.zeros((256, TOK), F32)).astype(BF)
    trace = jnp.zeros((1, 128), F32)
    laid = []
    for i, mapped in plane_products(core, own, oth, rows, copies):
        mapped = mapped * gates[columns[i]]
        copies[5 + i].wait()
        terms = mapped[TOK:] * probe[i].astype(F32)
        trace = trace + jnp.sum(terms, axis=0, keepdims=True)
        part = mapped[:TOK]
        if i == 0:
            copies[4].wait()
            part = part + vel1[...].astype(F32)
        laid.append(dot(lay, part.astype(BF)))
    trace = row_sum(trace)
    high = trace.astype(BF).astype(F32)
    mid = (trace - high).astype(BF).astype(F32)
    low = trace - high - mid
    lane = lax.broadcasted_iota(jnp.int32, (1, 128), 1)
    coded = jnp.where(lane == 0, high, jnp.where(lane == 1, mid, jnp.where(lane == 2, low, 0.0)))
    slot = lax.broadcasted_iota(jnp.int32, (256, 128), 0) & 7
    for i in range(4):
        block = jnp.where(slot == 6, coded, laid[i]) if i == 0 else laid[i]
        out_ref[:, pl.ds(pl.multiple_of(place_y[i] * 128, 128), 128)] = block.astype(BF)


def land_kernel(got, state, next_ref, change_ref):
    total = jnp.zeros((8, 512), F32)
    for z in range(4):
        for c in range(2):
            sums = jnp.zeros((8, 512), F32)
            for y in range(4):
                block = got[z * 8 + y * 2 + c].astype(F32)
                sums = sums + block
            total = total + sums
            for y in range(4):
                j = z * 8 + y * 2 + c
                cols = slice(j * 128, (j + 1) * 128)
                both = sums[:6, y * 128 : (y + 1) * 128]
                next_ref[:, cols] = (state[:, cols].astype(F32) + 0.5 * STEP * both).astype(BF)
    change_ref[...] = jnp.broadcast_to(-0.5 * STEP * row_sum(total[6:7, :]) / TOK, (1, 128))


def along_z(copies):
    n, rows, lanes = copies.shape
    return lax.all_to_all(copies.reshape(n * rows, lanes), "z", 0, 0, tiled=True)


def along_y(block):
    return lax.all_to_all(jnp.tile(block, (4, 1)), "y", 0, 0, tiled=True)


def swap(block):
    return lax.ppermute(block, "c", [(0, 1), (1, 0)])


def per_device(state, probe, norm_gain, head_maps, query_gain, key_gain, out_map, out_gate):
    gates = out_gate.reshape(32, 1, 128)
    maps = head_maps.reshape(32, 128, 384)
    gain = norm_gain.reshape(32, 1, 128)

    packed_state, packed_probe, *sends = call(
        pack_kernel, [shape((4, 8, 3072)), shape((8, 4096))] + [shape((4, 256, 128))] * 4,
        True, (state,), (probe,), (out_map.reshape(4, 4, 256, 128),),
        scratch=[pltpu.VMEM((6, 4096), BF), pltpu.VMEM((6, 4096), BF), sems(6)],
        vmem_mib=FULL,
    )
    probe_all = lax.all_gather(packed_probe, SEQ, axis=0, tiled=True)
    lines = along_z(packed_state)
    moved = [
        lax.ppermute(sends[k], "y", [(y, (y + k) % 4) for y in range(4)]) for k in (1, 3, 2)
    ]
    lines, moved[0], moved[1] = lax.optimization_barrier((lines, moved[0], moved[1]))
    own = along_y(lines)
    oth = swap(own)
    att1, col = call(
        first_kernel, [shape((4, TOK, 128)), shape((TOK, 128))],
        True, own, oth, (maps,), gain, query_gain, key_gain, scratch=[HELD, MAPS, sems(1)], vmem_mib=51,
    )
    plane_outs = [(piece.reshape(8, 128, 128),) for piece in (sends[0], *moved)]
    own1 = along_z(att1)
    oth1 = swap(own1)
    parts = call(
        plane_kernel, shape((4, TOK, 128), F32),
        True, own1.reshape(4, TOK, 128), oth1.reshape(4, TOK, 128), *plane_outs,
        scratch=[ROWS, sems(4)], vmem_mib=MIDDLE,
    )
    parts = lax.all_to_all(parts.reshape(4 * TOK, 128), "y", 0, 0, tiled=True)
    vel1, mid = call(
        middle_kernel, [shape((TOK, 128)), shape((4, TOK, 128))],
        True, parts.reshape(4, TOK, 128), gates, col, vmem_mib=MIDDLE,
    )
    own_m = along_y(along_z(mid))
    probe_blocks = call(
        tangent_kernel, shape((34, TOK, 128)),
        True, (own,), (oth,), (probe_all,), (maps,), gain, query_gain, key_gain, (mid,),
        scratch=[
            HELD, pltpu.VMEM((128, 3072), BF), pltpu.VMEM((128, 3072), BF),
            pltpu.VMEM((256, 3072), BF), MAPS, sems(4),
        ],
        vmem_mib=FULL,
    )
    own_m, probe_blocks = lax.optimization_barrier((own_m, probe_blocks))
    oth_m = swap(own_m).reshape(16, TOK, 128)
    own_m = own_m.reshape(16, TOK, 128)
    both = call(
        second_kernel, shape((4, 2 * TOK, 128)),
        True, own_m, oth_m, (probe_blocks,), (maps,), gain, query_gain, key_gain,
        scratch=[pltpu.VMEM((34, TOK, 128), BF), MAPS, sems(2)], vmem_mib=SECOND,
    )
    own2 = lax.all_to_all(both.reshape(8 * TOK, 128), "z", 0, 0, tiled=True)
    oth2 = swap(own2)
    columns = call(
        last_kernel, shape((256, 512)),
        True, own2.reshape(4, 2 * TOK, 128), oth2.reshape(4, 2 * TOK, 128),
        *plane_outs, gates, (vel1,), (probe_blocks,),
        scratch=[
            ROWS, pltpu.VMEM((TOK, 128), BF),
            pltpu.VMEM((4, TOK, 128), BF), sems(9),
        ],
        vmem_mib=LAST,
    )
    got = lax.all_to_all(columns, SEQ, 0, 0, tiled=True).reshape(32, 8, 512)
    next_state, change = call(
        land_kernel, [shape((6, 4096)), shape((1, 128), F32)], False, got, state
    )
    return next_state, change[0, :1]


def solution(mesh):
    split = Mesh(mesh.devices.reshape(4, 4, 2, 4, 4), ("z", "y", "c", "w", "x"))
    rows = P(("w", "x", "z", "y", "c"), None)
    return jax.shard_map(
        per_device,
        mesh=split,
        in_specs=(rows, rows, P(), P(SEQ, None, None), P(SEQ, None), P(SEQ, None), P(None, SEQ), P()),
        out_specs=(rows, P(("w", "x"))),
        check_vma=False,
    )
```

```python
import jax
import jax.numpy as jnp
from jax import lax
from jax.experimental import pallas as pl
from jax.experimental.pallas import tpu as pltpu
from jax.sharding import Mesh, PartitionSpec as P

EPS = 1e-06
STEP = 0.5
SEQ = ("z", "y", "c")
BF = jnp.bfloat16
F32 = jnp.float32
NT = (((1,), (1,)), ((), ()))
TOK = 192
SCALE = 128 ** (-0.5)


def dot(a, b):
    return jnp.dot(a, b, preferred_element_type=F32)


def dot_nt(a, b):
    return lax.dot_general(a, b, NT, preferred_element_type=F32)


def row_mean(v):
    return jnp.mean(v, axis=-1, keepdims=True)


HELD = pltpu.VMEM((32, TOK, 128), BF)
MAPS = pltpu.VMEM((32, 128, 384), BF)
ROWS = pltpu.VMEM((4, 8, 128, 128), BF)


FULL = 60
LAST = 51
MIDDLE = 51
SECOND = 51


def sems(n):
    return pltpu.SemaphoreType.DMA((n,))


def fetch(sem, *pairs):
    copies = [pltpu.make_async_copy(a, b, sem.at[i]) for i, (a, b) in enumerate(pairs)]
    for copy in copies:
        copy.start()
    return copies


def call(kernel, out_shape, placed, *args, scratch=(), vmem_mib=20, n_hbm=0):
    body = kernel
    if placed:

        def body(*refs):
            c, y, z = lax.axis_index("c"), lax.axis_index("y"), lax.axis_index("z")
            return kernel((c, z * 8 + y * 2 + c, y, z), *refs)

    in_specs = []
    for a in args:
        if isinstance(a, tuple):
            in_specs.append(pl.BlockSpec(memory_space=pltpu.HBM))
        else:
            in_specs.append(pl.BlockSpec(memory_space=pltpu.VMEM))
    flat = [a[0] if isinstance(a, tuple) else a for a in args]
    multi = isinstance(out_shape, (tuple, list))
    vmem = pl.BlockSpec(memory_space=pltpu.VMEM)
    hbm = pl.BlockSpec(memory_space=pltpu.HBM)
    return pl.pallas_call(
        body,
        out_shape=out_shape,
        in_specs=in_specs,
        out_specs=[vmem] * (len(out_shape) - n_hbm) + [hbm] * n_hbm if multi else vmem,
        scratch_shapes=scratch,
        compiler_params=pltpu.CompilerParams(vmem_limit_bytes=vmem_mib * 1024 * 1024),
    )(*flat)


def shape(dims, kind=BF):
    return jax.ShapeDtypeStruct(dims, kind)


def selectors(first_row_token, rows):
    packed = lax.broadcasted_iota(jnp.int32, (TOK, rows), 1)
    token = lax.broadcasted_iota(jnp.int32, (TOK, rows), 0)
    slot = packed & 7
    base = first_row_token(packed)
    one = jnp.ones((TOK, rows), F32)
    zero = jnp.zeros((TOK, rows), F32)
    main = jnp.where((token == base + slot) & (slot < 6), one, zero).astype(BF)
    rest = [
        jnp.where((token == base + m + 3 * (slot - 6)) & (slot >= 6), one, zero).astype(BF)
        for m in range(3)
    ]
    return main, rest


def pieces(main, rest, chunk_of):
    tail = None
    for m in range(3):
        chunk = chunk_of(m)
        part = dot(rest[m], chunk)
        tail = part if tail is None else tail + part
        yield m * 1024, dot(main, chunk)
    yield 3072, tail


def qkv_norm(proj, q_gain, k_gain):
    query, key, val = proj[:, :128], proj[:, 128:256], proj[:, 256:]
    rq = lax.rsqrt(row_mean(query * query) + EPS)
    rk = lax.rsqrt(row_mean(key * key) + EPS)
    qn = (query * rq * q_gain).astype(BF)
    kn = (key * rk * k_gain).astype(BF)
    return query, key, rq, rk, qn, kn, val.astype(BF)


def probabilities(qn, kn):
    expo = jnp.exp(dot_nt(qn, kn) * SCALE)
    return expo / jnp.sum(expo, axis=-1, keepdims=True)


def attend(proj, q_gain, k_gain):
    _, _, _, _, qn, kn, val = qkv_norm(proj, q_gain, k_gain)
    return dot(probabilities(qn, kn).astype(BF), val).astype(BF)


def attend_tangent(proj, d_proj, q_gain, k_gain):
    query, key, rq, rk, qn, kn, val = qkv_norm(proj, q_gain, k_gain)
    dq, dk, dv = d_proj[:, :128], d_proj[:, 128:256], d_proj[:, 256:].astype(BF)
    drq = -(rq * rq * rq) * row_mean(query * dq)
    drk = -(rk * rk * rk) * row_mean(key * dk)
    dqn = ((dq * rq + query * drq) * q_gain).astype(BF)
    dkn = ((dk * rk + key * drk) * k_gain).astype(BF)
    probs = probabilities(qn, kn)
    ds = (dot_nt(dqn, kn) + dot_nt(qn, dkn)) * SCALE
    d_probs = probs * (ds - jnp.sum(probs * ds, axis=-1, keepdims=True))
    probs = probs.astype(BF)
    return dot(probs, val).astype(BF), dot(d_probs.astype(BF), val) + dot(probs, dv)


def pack_kernel(meta, state, probe, out_map, state_ref, probe_ref, s0, s1, s2, s3, sem):
    shifted = [(out_map.at[:, (meta[2] + k) & 3], to) for k, to in enumerate((s0, s1, s2, s3))]
    copies = fetch(sem, *shifted)
    for source, write in ((state, None), (probe, probe_ref)):
        main = source[:, :3072]
        sixth = jnp.concatenate([source[q : q + 1, 3072:] for q in range(3)], axis=1)
        seventh = jnp.concatenate([source[q : q + 1, 3072:] for q in range(3, 6)], axis=1)
        whole = jnp.concatenate([main, sixth, seventh], axis=0)
        if write is None:
            for n in range(4):
                state_ref[n] = whole
        else:
            write[:, :3072] = whole
            write[:, 3072:] = whole[:, :1024]
    for copy in copies:
        copy.wait()


def core_order(core):
    def first_token(packed):
        inner = packed & 127
        z = (inner >> 3) & 3
        y = inner >> 5
        c = jnp.where((packed >> 7) == 0, core, 1 - core)
        return (z * 8 + y * 2 + c) * 6

    return first_token


def unpack_state(core, xa, xb, held):
    main, rest = selectors(core_order(core), 256)
    squares = jnp.zeros((TOK, 128), F32)

    def chunk_of(m):
        cols = slice(m * 1024, (m + 1) * 1024)
        return jnp.concatenate([xa[:, cols], xb[:, cols]], axis=0)

    for start, x in pieces(main, rest, chunk_of):
        for b in range(8):
            piece = x[:, b * 128 : (b + 1) * 128]
            squares = squares + piece * piece
            held[start // 128 + b] = piece.astype(BF)
    return lax.rsqrt(row_sum(squares) * (1.0 / 4096) + EPS)


def row_sum(v):
    return jnp.sum(v, axis=-1, keepdims=True)


def first_kernel(
    meta, xa, xb, maps_hbm, gain, q_gain, k_gain, att_ref, col_ref, held, maps, sem
):
    copies = fetch(sem, (maps_hbm, maps))
    recip = unpack_state(meta[0], xa, xb, held)
    copies[0].wait()
    proj = jnp.zeros((TOK, 384), F32)
    for h in range(0, 32, 2):
        left = (held[h].astype(F32) * recip * gain[h]).astype(BF)
        right = (held[h + 1].astype(F32) * recip * gain[h + 1]).astype(BF)
        rows = jnp.concatenate([maps[h], maps[h + 1]], axis=0)
        proj = proj + dot(jnp.concatenate([left, right], axis=1), rows)
    att = attend(proj, q_gain[...], k_gain[...])
    for i in range(4):
        att_ref[i] = att
    col_ref[...] = held[meta[1]]


def blocks(core, own, oth):
    for side, c in ((own, core), (oth, 1 - core)):
        for y in range(4):
            for z in (0, 2):
                yield side, y * 4 + z, z * 8 + y * 2 + c


SHIFTS = (0, 1, 3, 2)


def plane_products(core, own, oth, rows):
    left = []
    for z in range(4):
        mine, other = own[z], oth[z]
        first = jnp.where(core == 0, mine, other)
        second = jnp.where(core == 0, other, mine)
        left.append(jnp.concatenate([first, second], axis=1))
    for i in range(4):
        mapped = None
        for z in range(4):
            right = jnp.concatenate([rows[i, z * 2], rows[i, z * 2 + 1]], axis=0)
            part = dot(left[z], right)
            mapped = part if mapped is None else mapped + part
        yield i, mapped


def plane_kernel(meta, own, oth, r0, r1, r2, r3, part_ref, rows, sem):
    copies = fetch(sem, *[(r, rows.at[i]) for i, r in enumerate((r0, r1, r2, r3))])
    for copy in copies:
        copy.wait()
    for i, mapped in plane_products(meta[0], own, oth, rows):
        part_ref[(meta[2] - SHIFTS[i]) & 3] = mapped


def middle_kernel(meta, parts, gates, col, vel_ref, mid_ref):
    total = (parts[0] + parts[1]) + (parts[2] + parts[3])
    vel = (gates[meta[1]] * total).astype(BF)
    vel_ref[...] = vel
    mid = (col[...].astype(F32) + STEP * vel.astype(F32)).astype(BF)
    for i in range(4):
        mid_ref[i] = mid


def both_rows(x, probe, recip, d_recip, gain):
    normed = (x * recip * gain).astype(BF)
    d_normed = ((probe * recip + x * d_recip) * gain).astype(BF)
    return jnp.concatenate([normed, d_normed], axis=0)


def tangent_kernel(
    meta, xa_hbm, xb_hbm, packed_hbm, maps_hbm, gain, q_gain, k_gain, after, probe_ref,
    held, xa, xb, packed, maps, sem,
):
    copies = fetch(
        sem, (xa_hbm, xa), (xb_hbm, xb), (packed_hbm.at[:, :3072], packed), (maps_hbm, maps)
    )
    copies[0].wait()
    copies[1].wait()
    recip = unpack_state(meta[0], xa, xb, held)
    main, rest = selectors(lambda row: (row >> 3) * 6, 256)
    copies[2].wait()
    dots = jnp.zeros((TOK, 128), F32)
    for start, x in pieces(main, rest, lambda m: packed[:, m * 1024 : (m + 1) * 1024]):
        for b in range(8):
            piece = x[:, b * 128 : (b + 1) * 128]
            dots = dots + piece * held[start // 128 + b].astype(F32)
            probe_ref[start // 128 + b] = piece.astype(BF)
    d_recip = -(recip * recip * recip) * (row_sum(dots) * (1.0 / 4096))
    copies[3].wait()
    proj = jnp.zeros((2 * TOK, 384), F32)
    for h in range(0, 32, 2):
        pair = [
            both_rows(held[i].astype(F32), probe_ref[i].astype(F32), recip, d_recip, gain[i])
            for i in (h, h + 1)
        ]
        rows = jnp.concatenate([maps[h], maps[h + 1]], axis=0)
        proj = proj + dot(jnp.concatenate(pair, axis=1), rows)
    d_att = attend_tangent(proj[:TOK], proj[TOK:], q_gain[...], k_gain[...])[1]
    high = d_att.astype(BF)
    probe_ref[32] = high
    probe_ref[33] = (d_att - high.astype(F32)).astype(BF)


def second_kernel(
    meta, own, oth, probe_hbm, maps_hbm, gain, q_gain, k_gain, both_ref, probe, maps, sem
):
    core = meta[0]
    copies = fetch(sem, (probe_hbm, probe), (maps_hbm, maps))
    squares = jnp.zeros((TOK, 128), F32)
    dots = jnp.zeros((TOK, 128), F32)
    for side, b, h in blocks(core, own, oth):
        for i in range(2):
            x = side[b + i].astype(F32)
            squares = squares + x * x
    copies[0].wait()
    for side, b, h in blocks(core, own, oth):
        for i in range(2):
            dots = dots + side[b + i].astype(F32) * probe[h + 8 * i].astype(F32)
    recip = lax.rsqrt(row_sum(squares) * (1.0 / 4096) + EPS)
    d_recip = -(recip * recip * recip) * (row_sum(dots) * (1.0 / 4096))
    copies[1].wait()
    proj = jnp.zeros((2 * TOK, 384), F32)
    for side, b, h in blocks(core, own, oth):
        pair = [
            both_rows(
                side[b + i].astype(F32), probe[h + 8 * i].astype(F32), recip, d_recip, gain[h + 8 * i]
            )
            for i in range(2)
        ]
        rows = jnp.concatenate([maps[h], maps[h + 8]], axis=0)
        proj = proj + dot(jnp.concatenate(pair, axis=1), rows)
    att, d_att = attend_tangent(proj[:TOK], proj[TOK:], q_gain[...], k_gain[...])
    d_first = probe[32].astype(F32) + probe[33].astype(F32)
    d_both = (d_att + d_first).astype(BF)
    for i in range(4):
        both_ref[i, :TOK] = att
        both_ref[i, TOK:] = d_both


def last_kernel(
    meta, own, oth, r0, r1, r2, r3, gates, vel_hbm, probe_hbm, out_ref, rows, vel1, probe, sem
):
    core, slab = meta[0], meta[3]
    place_y = [(meta[2] - shift) & 3 for shift in SHIFTS]
    columns = [slab * 8 + y * 2 + core for y in place_y]
    copies = fetch(
        sem,
        *[(r, rows.at[i]) for i, r in enumerate((r0, r1, r2, r3))],
        (vel_hbm, vel1),
        *[(probe_hbm.at[column], probe.at[i]) for i, column in enumerate(columns)],
    )
    row = lax.broadcasted_iota(jnp.int32, (256, TOK), 0)
    token = lax.broadcasted_iota(jnp.int32, (256, TOK), 1)
    hit = (token == (row >> 3) * 6 + (row & 7)) & ((row & 7) < 6)
    lay = jnp.where(hit, jnp.ones((256, TOK), F32), jnp.zeros((256, TOK), F32)).astype(BF)
    for copy in copies:
        copy.wait()
    trace = jnp.zeros((1, 128), F32)
    laid = []
    for i, mapped in plane_products(core, own, oth, rows):
        mapped = mapped * gates[columns[i]]
        terms = mapped[TOK:] * probe[i].astype(F32)
        trace = trace + jnp.sum(terms, axis=0, keepdims=True)
        part = mapped[:TOK]
        if i == 0:
            part = part + vel1[...].astype(F32)
        laid.append(dot(lay, part.astype(BF)))
    trace = row_sum(trace)
    high = trace.astype(BF).astype(F32)
    mid = (trace - high).astype(BF).astype(F32)
    low = trace - high - mid
    lane = lax.broadcasted_iota(jnp.int32, (1, 128), 1)
    coded = jnp.where(lane == 0, high, jnp.where(lane == 1, mid, jnp.where(lane == 2, low, 0.0)))
    slot = lax.broadcasted_iota(jnp.int32, (256, 128), 0) & 7
    for i in range(4):
        block = jnp.where(slot == 6, coded, laid[i]) if i == 0 else laid[i]
        out_ref[:, pl.ds(pl.multiple_of(place_y[i] * 128, 128), 128)] = block.astype(BF)


def land_kernel(got, state, next_ref, change_ref):
    total = jnp.zeros((8, 512), F32)
    for z in range(4):
        for c in range(2):
            sums = jnp.zeros((8, 512), F32)
            for y in range(4):
                block = got[z * 8 + y * 2 + c].astype(F32)
                sums = sums + block
            total = total + sums
            for y in range(4):
                j = z * 8 + y * 2 + c
                cols = slice(j * 128, (j + 1) * 128)
                both = sums[:6, y * 128 : (y + 1) * 128]
                next_ref[:, cols] = (state[:, cols].astype(F32) + 0.5 * STEP * both).astype(BF)
    change_ref[...] = jnp.broadcast_to(-0.5 * STEP * row_sum(total[6:7, :]) / TOK, (1, 128))


def along_z(copies):
    n, rows, lanes = copies.shape
    return lax.all_to_all(copies.reshape(n * rows, lanes), "z", 0, 0, tiled=True)


def along_y(block):
    return lax.all_to_all(jnp.tile(block, (4, 1)), "y", 0, 0, tiled=True)


def swap(block):
    return lax.ppermute(block, "c", [(0, 1), (1, 0)])


def per_device(state, probe, norm_gain, head_maps, query_gain, key_gain, out_map, out_gate):
    gates = out_gate.reshape(32, 1, 128)
    maps = head_maps.reshape(32, 128, 384)
    gain = norm_gain.reshape(32, 1, 128)

    packed_state, packed_probe, *sends = call(
        pack_kernel, [shape((4, 8, 3072)), shape((8, 4096))] + [shape((4, 256, 128))] * 4,
        True, state, probe, (out_map.reshape(4, 4, 256, 128),),
        scratch=[sems(4)],
        vmem_mib=FULL,
    )
    probe_all = lax.all_gather(packed_probe, SEQ, axis=0, tiled=True)
    lines = along_z(packed_state)
    moved = [
        lax.ppermute(sends[k], "y", [(y, (y + k) % 4) for y in range(4)]) for k in (1, 3, 2)
    ]
    lines, moved[0], moved[1] = lax.optimization_barrier((lines, moved[0], moved[1]))
    own = along_y(lines)
    oth = swap(own)
    att1, col = call(
        first_kernel, [shape((4, TOK, 128)), shape((TOK, 128))],
        True, own, oth, (maps,), gain, query_gain, key_gain, scratch=[HELD, MAPS, sems(1)], vmem_mib=51,
    )
    plane_outs = [(piece.reshape(8, 128, 128),) for piece in (sends[0], *moved)]
    own1 = along_z(att1)
    oth1 = swap(own1)
    parts = call(
        plane_kernel, shape((4, TOK, 128), F32),
        True, own1.reshape(4, TOK, 128), oth1.reshape(4, TOK, 128), *plane_outs,
        scratch=[ROWS, sems(4)], vmem_mib=MIDDLE,
    )
    parts = lax.all_to_all(parts.reshape(4 * TOK, 128), "y", 0, 0, tiled=True)
    vel1, mid = call(
        middle_kernel, [shape((TOK, 128)), shape((4, TOK, 128))],
        True, parts.reshape(4, TOK, 128), gates, col, vmem_mib=MIDDLE,
    )
    own_m = along_y(along_z(mid))
    probe_blocks = call(
        tangent_kernel, shape((34, TOK, 128)),
        True, (own,), (oth,), (probe_all,), (maps,), gain, query_gain, key_gain, (mid,),
        scratch=[
            HELD, pltpu.VMEM((128, 3072), BF), pltpu.VMEM((128, 3072), BF),
            pltpu.VMEM((256, 3072), BF), MAPS, sems(4),
        ],
        vmem_mib=FULL,
    )
    own_m, probe_blocks = lax.optimization_barrier((own_m, probe_blocks))
    oth_m = swap(own_m).reshape(16, TOK, 128)
    own_m = own_m.reshape(16, TOK, 128)
    both = call(
        second_kernel, shape((4, 2 * TOK, 128)),
        True, own_m, oth_m, (probe_blocks,), (maps,), gain, query_gain, key_gain,
        scratch=[pltpu.VMEM((34, TOK, 128), BF), MAPS, sems(2)], vmem_mib=SECOND,
    )
    own2 = lax.all_to_all(both.reshape(8 * TOK, 128), "z", 0, 0, tiled=True)
    oth2 = swap(own2)
    columns = call(
        last_kernel, shape((256, 512)),
        True, own2.reshape(4, 2 * TOK, 128), oth2.reshape(4, 2 * TOK, 128),
        *plane_outs, gates, (vel1,), (probe_blocks,),
        scratch=[
            ROWS, pltpu.VMEM((TOK, 128), BF),
            pltpu.VMEM((4, TOK, 128), BF), sems(9),
        ],
        vmem_mib=LAST,
    )
    got = lax.all_to_all(columns, SEQ, 0, 0, tiled=True).reshape(32, 8, 512)
    next_state, change = call(
        land_kernel, [shape((6, 4096)), shape((1, 128), F32)], False, got, state
    )
    return next_state, change[0, :1]


def solution(mesh):
    split = Mesh(mesh.devices.reshape(4, 4, 2, 4, 4), ("z", "y", "c", "w", "x"))
    rows = P(("w", "x", "z", "y", "c"), None)
    return jax.shard_map(
        per_device,
        mesh=split,
        in_specs=(rows, rows, P(), P(SEQ, None, None), P(SEQ, None), P(SEQ, None), P(None, SEQ), P()),
        out_specs=(rows, P(("w", "x"))),
        check_vma=False,
    )
```

```python
import jax
import jax.numpy as jnp
from jax import lax
from jax.experimental import pallas as pl
from jax.experimental.pallas import tpu as pltpu
from jax.sharding import Mesh, PartitionSpec as P

EPS = 1e-06
STEP = 0.5
SEQ = ("z", "y", "c")
BF = jnp.bfloat16
F32 = jnp.float32
NT = (((1,), (1,)), ((), ()))
TOK = 192
SCALE = 128 ** (-0.5)


def dot(a, b):
    return jnp.dot(a, b, preferred_element_type=F32)


def dot_nt(a, b):
    return lax.dot_general(a, b, NT, preferred_element_type=F32)


def row_mean(v):
    return jnp.mean(v, axis=-1, keepdims=True)


HELD = pltpu.VMEM((32, TOK, 128), BF)
MAPS = pltpu.VMEM((32, 128, 384), BF)
ROWS = pltpu.VMEM((4, 8, 128, 128), BF)


FULL = 60
LAST = 51
MIDDLE = 51
SECOND = 51


def sems(n):
    return pltpu.SemaphoreType.DMA((n,))


def fetch(sem, *pairs):
    copies = [pltpu.make_async_copy(a, b, sem.at[i]) for i, (a, b) in enumerate(pairs)]
    for copy in copies:
        copy.start()
    return copies


def call(kernel, out_shape, placed, *args, scratch=(), vmem_mib=20, n_hbm=0):
    body = kernel
    if placed:

        def body(*refs):
            c, y, z = lax.axis_index("c"), lax.axis_index("y"), lax.axis_index("z")
            return kernel((c, z * 8 + y * 2 + c, y, z), *refs)

    in_specs = []
    for a in args:
        if isinstance(a, tuple):
            in_specs.append(pl.BlockSpec(memory_space=pltpu.HBM))
        else:
            in_specs.append(pl.BlockSpec(memory_space=pltpu.VMEM))
    flat = [a[0] if isinstance(a, tuple) else a for a in args]
    multi = isinstance(out_shape, (tuple, list))
    vmem = pl.BlockSpec(memory_space=pltpu.VMEM)
    hbm = pl.BlockSpec(memory_space=pltpu.HBM)
    return pl.pallas_call(
        body,
        out_shape=out_shape,
        in_specs=in_specs,
        out_specs=[vmem] * (len(out_shape) - n_hbm) + [hbm] * n_hbm if multi else vmem,
        scratch_shapes=scratch,
        compiler_params=pltpu.CompilerParams(vmem_limit_bytes=vmem_mib * 1024 * 1024),
    )(*flat)


def shape(dims, kind=BF):
    return jax.ShapeDtypeStruct(dims, kind)


def selectors(first_row_token, rows):
    packed = lax.broadcasted_iota(jnp.int32, (TOK, rows), 1)
    token = lax.broadcasted_iota(jnp.int32, (TOK, rows), 0)
    slot = packed & 7
    base = first_row_token(packed)
    one = jnp.ones((TOK, rows), F32)
    zero = jnp.zeros((TOK, rows), F32)
    main = jnp.where((token == base + slot) & (slot < 6), one, zero).astype(BF)
    rest = [
        jnp.where((token == base + m + 3 * (slot - 6)) & (slot >= 6), one, zero).astype(BF)
        for m in range(3)
    ]
    return main, rest


def pieces(main, rest, chunk_of):
    tail = None
    for m in range(3):
        chunk = chunk_of(m)
        part = dot(rest[m], chunk)
        tail = part if tail is None else tail + part
        yield m * 1024, dot(main, chunk)
    yield 3072, tail


def qkv_norm(proj, q_gain, k_gain):
    query, key, val = proj[:, :128], proj[:, 128:256], proj[:, 256:]
    rq = lax.rsqrt(row_mean(query * query) + EPS)
    rk = lax.rsqrt(row_mean(key * key) + EPS)
    qn = (query * rq * q_gain).astype(BF)
    kn = (key * rk * k_gain).astype(BF)
    return query, key, rq, rk, qn, kn, val.astype(BF)


def probabilities(qn, kn):
    expo = jnp.exp(dot_nt(qn, kn) * SCALE)
    return expo / jnp.sum(expo, axis=-1, keepdims=True)


def attend(proj, q_gain, k_gain):
    _, _, _, _, qn, kn, val = qkv_norm(proj, q_gain, k_gain)
    return dot(probabilities(qn, kn).astype(BF), val).astype(BF)


def attend_tangent(proj, d_proj, q_gain, k_gain):
    query, key, rq, rk, qn, kn, val = qkv_norm(proj, q_gain, k_gain)
    dq, dk, dv = d_proj[:, :128], d_proj[:, 128:256], d_proj[:, 256:].astype(BF)
    drq = -(rq * rq * rq) * row_mean(query * dq)
    drk = -(rk * rk * rk) * row_mean(key * dk)
    dqn = ((dq * rq + query * drq) * q_gain).astype(BF)
    dkn = ((dk * rk + key * drk) * k_gain).astype(BF)
    probs = probabilities(qn, kn)
    ds = (dot_nt(dqn, kn) + dot_nt(qn, dkn)) * SCALE
    d_probs = probs * (ds - jnp.sum(probs * ds, axis=-1, keepdims=True))
    probs = probs.astype(BF)
    return dot(probs, val).astype(BF), dot(d_probs.astype(BF), val) + dot(probs, dv)


def pack_kernel(meta, state, probe, out_map, state_ref, probe_ref, s0, s1, s2, s3, sem):
    shifted = [(out_map.at[:, (meta[2] + k) & 3], to) for k, to in enumerate((s0, s1, s2, s3))]
    copies = fetch(sem, *shifted)
    for source, write in ((state, None), (probe, probe_ref)):
        main = source[:, :3072]
        sixth = jnp.concatenate([source[q : q + 1, 3072:] for q in range(3)], axis=1)
        seventh = jnp.concatenate([source[q : q + 1, 3072:] for q in range(3, 6)], axis=1)
        whole = jnp.concatenate([main, sixth, seventh], axis=0)
        if write is None:
            for n in range(4):
                state_ref[n] = whole
        else:
            write[:, :3072] = whole
            write[:, 3072:] = whole[:, :1024]
    for copy in copies:
        copy.wait()


def core_order(core):
    def first_token(packed):
        inner = packed & 127
        z = (inner >> 3) & 3
        y = inner >> 5
        c = jnp.where((packed >> 7) == 0, core, 1 - core)
        return (z * 8 + y * 2 + c) * 6

    return first_token


def unpack_state(core, xa, xb, held):
    main, rest = selectors(core_order(core), 256)
    squares = jnp.zeros((TOK, 128), F32)

    def chunk_of(m):
        cols = slice(m * 1024, (m + 1) * 1024)
        return jnp.concatenate([xa[:, cols], xb[:, cols]], axis=0)

    for start, x in pieces(main, rest, chunk_of):
        for b in range(8):
            piece = x[:, b * 128 : (b + 1) * 128]
            squares = squares + piece * piece
            held[start // 128 + b] = piece.astype(BF)
    return lax.rsqrt(row_sum(squares) * (1.0 / 4096) + EPS)


def row_sum(v):
    return jnp.sum(v, axis=-1, keepdims=True)


def first_kernel(
    meta, xa, xb, maps_hbm, gain, q_gain, k_gain, att_ref, col_ref, held, maps, sem
):
    copies = fetch(sem, (maps_hbm, maps))
    recip = unpack_state(meta[0], xa, xb, held)
    copies[0].wait()
    proj = jnp.zeros((TOK, 384), F32)
    for h in range(0, 32, 2):
        left = (held[h].astype(F32) * recip * gain[h]).astype(BF)
        right = (held[h + 1].astype(F32) * recip * gain[h + 1]).astype(BF)
        rows = jnp.concatenate([maps[h], maps[h + 1]], axis=0)
        proj = proj + dot(jnp.concatenate([left, right], axis=1), rows)
    att = attend(proj, q_gain[...], k_gain[...])
    for i in range(4):
        att_ref[i] = att
    col_ref[...] = held[meta[1]]


def blocks(core, own, oth):
    for side, c in ((own, core), (oth, 1 - core)):
        for y in range(4):
            for z in (0, 2):
                yield side, y * 4 + z, z * 8 + y * 2 + c


SHIFTS = (0, 1, 3, 2)


def plane_products(core, own, oth, rows):
    left = []
    for z in range(4):
        mine, other = own[z], oth[z]
        first = jnp.where(core == 0, mine, other)
        second = jnp.where(core == 0, other, mine)
        left.append(jnp.concatenate([first, second], axis=1))
    for i in range(4):
        mapped = None
        for z in range(4):
            right = jnp.concatenate([rows[i, z * 2], rows[i, z * 2 + 1]], axis=0)
            part = dot(left[z], right)
            mapped = part if mapped is None else mapped + part
        yield i, mapped


def plane_kernel(meta, own, oth, r0, r1, r2, r3, part_ref, rows, sem):
    copies = fetch(sem, *[(r, rows.at[i]) for i, r in enumerate((r0, r1, r2, r3))])
    for copy in copies:
        copy.wait()
    for i, mapped in plane_products(meta[0], own, oth, rows):
        part_ref[(meta[2] - SHIFTS[i]) & 3] = mapped


def middle_kernel(meta, parts, gates, col, vel_ref, mid_ref):
    total = (parts[0] + parts[1]) + (parts[2] + parts[3])
    vel = (gates[meta[1]] * total).astype(BF)
    vel_ref[...] = vel
    mid = (col[...].astype(F32) + STEP * vel.astype(F32)).astype(BF)
    for i in range(4):
        mid_ref[i] = mid


def both_rows(x, probe, recip, d_recip, gain):
    normed = (x * recip * gain).astype(BF)
    d_normed = ((probe * recip + x * d_recip) * gain).astype(BF)
    return jnp.concatenate([normed, d_normed], axis=0)


def tangent_kernel(
    meta, xa_hbm, xb_hbm, packed_hbm, maps_hbm, gain, q_gain, k_gain, after, probe_ref,
    held, xa, xb, packed, maps, sem,
):
    copies = fetch(
        sem, (xa_hbm, xa), (xb_hbm, xb), (packed_hbm.at[:, :3072], packed), (maps_hbm, maps)
    )
    copies[0].wait()
    copies[1].wait()
    recip = unpack_state(meta[0], xa, xb, held)
    main, rest = selectors(lambda row: (row >> 3) * 6, 256)
    copies[2].wait()
    dots = jnp.zeros((TOK, 128), F32)
    for start, x in pieces(main, rest, lambda m: packed[:, m * 1024 : (m + 1) * 1024]):
        for b in range(8):
            piece = x[:, b * 128 : (b + 1) * 128]
            dots = dots + piece * held[start // 128 + b].astype(F32)
            probe_ref[start // 128 + b] = piece.astype(BF)
    d_recip = -(recip * recip * recip) * (row_sum(dots) * (1.0 / 4096))
    copies[3].wait()
    proj = jnp.zeros((2 * TOK, 384), F32)
    for h in range(0, 32, 2):
        pair = [
            both_rows(held[i].astype(F32), probe_ref[i].astype(F32), recip, d_recip, gain[i])
            for i in (h, h + 1)
        ]
        rows = jnp.concatenate([maps[h], maps[h + 1]], axis=0)
        proj = proj + dot(jnp.concatenate(pair, axis=1), rows)
    d_att = attend_tangent(proj[:TOK], proj[TOK:], q_gain[...], k_gain[...])[1]
    high = d_att.astype(BF)
    probe_ref[32] = high
    probe_ref[33] = (d_att - high.astype(F32)).astype(BF)


def second_kernel(
    meta, own, oth, probe_hbm, maps_hbm, gain, q_gain, k_gain, both_ref, probe, maps, sem
):
    core = meta[0]
    copies = fetch(sem, (probe_hbm, probe), (maps_hbm, maps))
    squares = jnp.zeros((TOK, 128), F32)
    dots = jnp.zeros((TOK, 128), F32)
    for side, b, h in blocks(core, own, oth):
        for i in range(2):
            x = side[b + i].astype(F32)
            squares = squares + x * x
    copies[0].wait()
    for side, b, h in blocks(core, own, oth):
        for i in range(2):
            dots = dots + side[b + i].astype(F32) * probe[h + 8 * i].astype(F32)
    recip = lax.rsqrt(row_sum(squares) * (1.0 / 4096) + EPS)
    d_recip = -(recip * recip * recip) * (row_sum(dots) * (1.0 / 4096))
    copies[1].wait()
    proj = jnp.zeros((2 * TOK, 384), F32)
    for side, b, h in blocks(core, own, oth):
        pair = [
            both_rows(
                side[b + i].astype(F32), probe[h + 8 * i].astype(F32), recip, d_recip, gain[h + 8 * i]
            )
            for i in range(2)
        ]
        rows = jnp.concatenate([maps[h], maps[h + 8]], axis=0)
        proj = proj + dot(jnp.concatenate(pair, axis=1), rows)
    att, d_att = attend_tangent(proj[:TOK], proj[TOK:], q_gain[...], k_gain[...])
    d_first = probe[32].astype(F32) + probe[33].astype(F32)
    d_both = (d_att + d_first).astype(BF)
    for i in range(4):
        both_ref[i, :TOK] = att
        both_ref[i, TOK:] = d_both


def last_kernel(
    meta, own, oth, r0, r1, r2, r3, gates, vel_hbm, probe_hbm, out_ref, rows, vel1, probe, sem
):
    core, slab = meta[0], meta[3]
    place_y = [(meta[2] - shift) & 3 for shift in SHIFTS]
    columns = [slab * 8 + y * 2 + core for y in place_y]
    copies = fetch(
        sem,
        *[(r, rows.at[i]) for i, r in enumerate((r0, r1, r2, r3))],
        (vel_hbm, vel1),
        *[(probe_hbm.at[column], probe.at[i]) for i, column in enumerate(columns)],
    )
    row = lax.broadcasted_iota(jnp.int32, (256, TOK), 0)
    token = lax.broadcasted_iota(jnp.int32, (256, TOK), 1)
    hit = (token == (row >> 3) * 6 + (row & 7)) & ((row & 7) < 6)
    lay = jnp.where(hit, jnp.ones((256, TOK), F32), jnp.zeros((256, TOK), F32)).astype(BF)
    for copy in copies:
        copy.wait()
    trace = jnp.zeros((1, 128), F32)
    laid = []
    for i, mapped in plane_products(core, own, oth, rows):
        mapped = mapped * gates[columns[i]]
        terms = mapped[TOK:] * probe[i].astype(F32)
        trace = trace + jnp.sum(terms, axis=0, keepdims=True)
        part = mapped[:TOK]
        if i == 0:
            part = part + vel1[...].astype(F32)
        laid.append(dot(lay, part.astype(BF)))
    trace = row_sum(trace)
    high = trace.astype(BF).astype(F32)
    mid = (trace - high).astype(BF).astype(F32)
    low = trace - high - mid
    lane = lax.broadcasted_iota(jnp.int32, (1, 128), 1)
    coded = jnp.where(lane == 0, high, jnp.where(lane == 1, mid, jnp.where(lane == 2, low, 0.0)))
    slot = lax.broadcasted_iota(jnp.int32, (256, 128), 0) & 7
    for i in range(4):
        block = jnp.where(slot == 6, coded, laid[i]) if i == 0 else laid[i]
        out_ref[:, pl.ds(pl.multiple_of(place_y[i] * 128, 128), 128)] = block.astype(BF)


def land_kernel(got, state, next_ref, change_ref):
    total = jnp.zeros((8, 512), F32)
    for z in range(4):
        for c in range(2):
            sums = jnp.zeros((8, 512), F32)
            for y in range(4):
                block = got[z * 8 + y * 2 + c].astype(F32)
                sums = sums + block
            total = total + sums
            for y in range(4):
                j = z * 8 + y * 2 + c
                cols = slice(j * 128, (j + 1) * 128)
                both = sums[:6, y * 128 : (y + 1) * 128]
                next_ref[:, cols] = (state[:, cols].astype(F32) + 0.5 * STEP * both).astype(BF)
    change_ref[...] = jnp.broadcast_to(-0.5 * STEP * row_sum(total[6:7, :]) / TOK, (1, 128))


def along_z(copies):
    n, rows, lanes = copies.shape
    return lax.all_to_all(copies.reshape(n * rows, lanes), "z", 0, 0, tiled=True)


def along_y(block):
    return lax.all_to_all(jnp.tile(block, (4, 1)), "y", 0, 0, tiled=True)


def swap(block):
    return lax.ppermute(block, "c", [(0, 1), (1, 0)])


def per_device(state, probe, norm_gain, head_maps, query_gain, key_gain, out_map, out_gate):
    gates = out_gate.reshape(32, 1, 128)
    maps = head_maps.reshape(32, 128, 384)
    gain = norm_gain.reshape(32, 1, 128)

    packed_state, packed_probe, *sends = call(
        pack_kernel, [shape((4, 8, 3072)), shape((8, 4096))] + [shape((4, 256, 128))] * 4,
        True, state, probe, (out_map.reshape(4, 4, 256, 128),),
        scratch=[sems(4)],
        vmem_mib=FULL,
    )
    probe_all = lax.all_gather(packed_probe, SEQ, axis=0, tiled=True)
    lines = along_z(packed_state)
    moved = [
        lax.ppermute(sends[k], "y", [(y, (y + k) % 4) for y in range(4)]) for k in (1, 3, 2)
    ]
    lines, moved[0], moved[2] = lax.optimization_barrier((lines, moved[0], moved[2]))
    own = along_y(lines)
    oth = swap(own)
    att1, col = call(
        first_kernel, [shape((4, TOK, 128)), shape((TOK, 128))],
        True, own, oth, (maps,), gain, query_gain, key_gain, scratch=[HELD, MAPS, sems(1)], vmem_mib=51,
    )
    plane_outs = [(piece.reshape(8, 128, 128),) for piece in (sends[0], *moved)]
    own1 = along_z(att1)
    oth1 = swap(own1)
    parts = call(
        plane_kernel, shape((4, TOK, 128), F32),
        True, own1.reshape(4, TOK, 128), oth1.reshape(4, TOK, 128), *plane_outs,
        scratch=[ROWS, sems(4)], vmem_mib=MIDDLE,
    )
    parts = lax.all_to_all(parts.reshape(4 * TOK, 128), "y", 0, 0, tiled=True)
    vel1, mid = call(
        middle_kernel, [shape((TOK, 128)), shape((4, TOK, 128))],
        True, parts.reshape(4, TOK, 128), gates, col, vmem_mib=MIDDLE,
    )
    own_m = along_y(along_z(mid))
    probe_blocks = call(
        tangent_kernel, shape((34, TOK, 128)),
        True, (own,), (oth,), (probe_all,), (maps,), gain, query_gain, key_gain, (mid,),
        scratch=[
            HELD, pltpu.VMEM((128, 3072), BF), pltpu.VMEM((128, 3072), BF),
            pltpu.VMEM((256, 3072), BF), MAPS, sems(4),
        ],
        vmem_mib=FULL,
    )
    own_m, probe_blocks = lax.optimization_barrier((own_m, probe_blocks))
    oth_m = swap(own_m).reshape(16, TOK, 128)
    own_m = own_m.reshape(16, TOK, 128)
    both = call(
        second_kernel, shape((4, 2 * TOK, 128)),
        True, own_m, oth_m, (probe_blocks,), (maps,), gain, query_gain, key_gain,
        scratch=[pltpu.VMEM((34, TOK, 128), BF), MAPS, sems(2)], vmem_mib=SECOND,
    )
    own2 = lax.all_to_all(both.reshape(8 * TOK, 128), "z", 0, 0, tiled=True)
    oth2 = swap(own2)
    columns = call(
        last_kernel, shape((256, 512)),
        True, own2.reshape(4, 2 * TOK, 128), oth2.reshape(4, 2 * TOK, 128),
        *plane_outs, gates, (vel1,), (probe_blocks,),
        scratch=[
            ROWS, pltpu.VMEM((TOK, 128), BF),
            pltpu.VMEM((4, TOK, 128), BF), sems(9),
        ],
        vmem_mib=LAST,
    )
    got = lax.all_to_all(columns, SEQ, 0, 0, tiled=True).reshape(32, 8, 512)
    next_state, change = call(
        land_kernel, [shape((6, 4096)), shape((1, 128), F32)], False, got, state
    )
    return next_state, change[0, :1]


def solution(mesh):
    split = Mesh(mesh.devices.reshape(4, 4, 2, 4, 4), ("z", "y", "c", "w", "x"))
    rows = P(("w", "x", "z", "y", "c"), None)
    return jax.shard_map(
        per_device,
        mesh=split,
        in_specs=(rows, rows, P(), P(SEQ, None, None), P(SEQ, None), P(SEQ, None), P(None, SEQ), P()),
        out_specs=(rows, P(("w", "x"))),
        check_vma=False,
    )
```
